32 devices in a mesh: grp: 2 (over x), blk: 16 (over z, y, core).
Axes of the slice: x: 2, y: 2, z: 4, core: 2. Of those that a mesh axis runs over, the one named last changes fastest.
Arguments:
- tokens: bfloat16 [512, 6144], P(('grp', 'blk')), parts along dimension 0, may hold values from -6 to 6
- cotangent: bfloat16 [128, 6144], P(('grp', 'blk')), parts along dimension 0, may hold values from -2.390625 to 2.390625
- gate_weight: bfloat16 [6144, 8192], P(None, 'blk'), may hold values from -0.078125 to 0.078125
- up_weight: bfloat16 [6144, 8192], P(None, 'blk'), may hold values from -0.078125 to 0.078125
- down_weight: bfloat16 [8192, 6144], P('blk'), may hold values from -0.0625 to 0.0625
- logits: float32 [512, 8], P(('grp', 'blk')), parts along dimension 0, may hold values from -24 to 300, as said below
- ref_logits: float32 [512, 8], P(('grp', 'blk')), parts along dimension 0, may hold values from -24 to 300, as said below
- routes: int32 [512, 2], P(('grp', 'blk')), parts along dimension 0, may hold values from 0 to 7, as said below
Outputs:
- grad_gate: bfloat16 [12288, 8192], P('grp', 'blk'), parts along dimension 0
- grad_up: bfloat16 [12288, 8192], P('grp', 'blk'), parts along dimension 0
- grad_down: bfloat16 [16384, 6144], P(('grp', 'blk')), parts along dimension 0
- grad_tokens: bfloat16 [512, 6144], P(('grp', 'blk')), parts along dimension 0
- grad_logits: float32 [512, 8], P(('grp', 'blk')), parts along dimension 0
- entropy: float32 [512], P(('grp', 'blk')), parts along dimension 0
- divergence: float32 [512], P(('grp', 'blk')), parts along dimension 0
The draws below stay inside these ranges and needn't reach their ends.
There are 2 independent parts, one for each index of `grp`. The reference program is written for one: setup_inputs(seed, part) draws one part's arguments, and reference() takes and returns one part's arrays. A program takes and returns all parts, laid end to end along the dimension named above; an argument that names none is the same for every part. Nothing has to cross between parts.
Inputs may be any that keep to these rules, and one draw needn't show every extreme that they name: `routes`: each row names two different experts. In each aligned block of 16 rows (the tokens of one index of blk) between half of 4 and 4 rows name expert 0, and in every draw some block has exactly 4. `logits`: finite values. `ref_logits`: finite values.
All inputs are finite; a program needn't handle non-finite values.
Results may differ from the reference program's by a relative error of at most 0.0056.
Values may be sent and summed in bfloat16 or wider, within the bound.
No kernel may reach another device: no remote copies, remote signals or barrier semaphores. Data moves between devices by JAX's collectives and lax.ppermute only.
A program may use at most 128 MiB of HBM per device.

```python
import jax
import jax.numpy as jnp

D = 6144
FF = 8192
EXPERTS = 8
TOK_DEV = 16
CAP = 4
TOKENS = 256
SLOTS = 64


def logit_base(key):
    return jax.random.normal(key, (TOKENS, EXPERTS), jnp.float32) * 2.0


def draw_logits(key, part):
    base = logit_base(key)
    key = jax.random.fold_in(key, 21)
    k_noise = jax.random.fold_in(key, 0)
    values = base + 0.7 * jax.random.normal(k_noise, (TOKENS, EXPERTS), jnp.float32)
    return values


def draw_ref_logits(key, part):
    base = logit_base(key)
    key = jax.random.fold_in(key, 22)
    k_noise = jax.random.fold_in(key, 0)
    values = base + 0.7 * jax.random.normal(k_noise, (TOKENS, EXPERTS), jnp.float32)
    return values


def draw_routes(key, part):
    key = jax.random.fold_in(key, 23)
    blocks = TOKENS // TOK_DEV
    k_count, k_full, k_rank, k_first, k_shift, k_flip = jax.random.split(key, 6)
    counts = jax.random.randint(k_count, (blocks,), CAP // 2, CAP + 1)
    full = jax.random.randint(k_full, (), 0, blocks)
    counts = jnp.where(jnp.arange(blocks) == full, CAP, counts)
    rank_keys = jax.random.split(k_rank, blocks)
    ranks = jax.vmap(lambda k: jax.random.permutation(k, TOK_DEV))(rank_keys)
    chosen = ranks < counts[:, None]
    other_one = jax.random.randint(k_first, (blocks, TOK_DEV), 1, EXPERTS)
    shift = jax.random.randint(k_shift, (blocks, TOK_DEV), 1, EXPERTS - 1)
    other_two = 1 + (other_one - 1 + shift) % (EXPERTS - 1)
    first = jnp.where(chosen, 0, other_one)
    second = jnp.where(chosen, other_one, other_two)
    flip = jax.random.randint(k_flip, (blocks, TOK_DEV), 0, 2)
    left = jnp.where(flip == 1, second, first)
    right = jnp.where(flip == 1, first, second)
    return jnp.stack([left, right], axis=-1).reshape(TOKENS, 2).astype(jnp.int32)


def steps_of(own_key, shape, cuts, least, top_value):
    def one(dim, blocks):
        draws = jax.random.uniform(jax.random.fold_in(jax.random.fold_in(own_key, 6), dim), (blocks,), jnp.float32, least / len(cuts), top_value / len(cuts))
        return jnp.repeat(jnp.exp(draws), shape[dim] // blocks).reshape((-1,) + (1,) * (len(shape) - dim - 1))

    factor_of = one(*cuts[0])
    for cut in cuts[1:]:
        factor_of = factor_of * one(*cut)
    return factor_of


def noise(own_key, shape, spread, limit, pieces=(), kind=jnp.bfloat16):
    gain = steps_of(own_key, shape, pieces, -0.22, 0.18) if pieces else 1.0
    entries = jax.random.normal(own_key, shape, jnp.float32) * spread * gain
    return jnp.minimum(jnp.maximum(entries, -limit), limit).astype(kind)


def setup_inputs(seed: int = 0, part: int = 0) -> dict:
    key_of = jax.random.split(jax.random.key(seed), 9)
    part_splits = jax.random.split(jax.random.fold_in(key_of[8], part), 9)
    tokens = noise(part_splits[0], (TOKENS, D), 1.0, 6.0, ((0, 16),))
    cotangent = noise(part_splits[1], (SLOTS, D), 0.3, 2.390625, ((0, 16),))
    gate_weight = noise(key_of[2], (D, FF), D ** -0.5, 0.078125, ((1, 16),))
    up_weight = noise(key_of[3], (D, FF), D ** -0.5, 0.078125, ((1, 16),))
    down_weight = noise(key_of[4], (FF, D), FF ** -0.5, 0.0625, ((0, 16),))
    logits = draw_logits(jax.random.fold_in(jax.random.fold_in(key_of[8], part), 71), part)
    ref_logits = draw_ref_logits(jax.random.fold_in(jax.random.fold_in(key_of[8], part), 71), part)
    routes = draw_routes(jax.random.fold_in(jax.random.fold_in(key_of[8], part), 71), part)
    return dict(tokens=tokens, cotangent=cotangent, gate_weight=gate_weight, up_weight=up_weight, down_weight=down_weight, logits=logits, ref_logits=ref_logits, routes=routes)


def block_slots(row_mask):
    return jnp.nonzero(row_mask, size=CAP, fill_value=0)[0].astype(jnp.int32)


def reference(tokens, cotangent, gate_weight, up_weight, down_weight, logits, ref_logits, routes):
    policy_log = jax.nn.log_softmax(logits, axis=1)
    frozen_log = jax.nn.log_softmax(ref_logits, axis=1)
    probs = jnp.exp(policy_log)
    entropy = -jnp.sum(probs * policy_log, axis=1)
    divergence = jnp.sum(probs * (policy_log - frozen_log), axis=1)
    is_window = routes == 0
    routed = jnp.any(is_window, axis=1)
    partner = routes[:, 0] + routes[:, 1]
    columns = jnp.arange(EXPERTS, dtype=jnp.int32)
    partner_hot = (columns[None, :] == partner[:, None]).astype(jnp.float32)
    partner_logit = jnp.sum(logits * partner_hot, axis=1)
    gate = jnp.where(routed, jax.nn.sigmoid(logits[:, 0] - partner_logit), jnp.float32(0.0))
    gate_low = gate.astype(jnp.bfloat16)
    blocks = TOKENS // TOK_DEV
    routed_blocks = routed.reshape(blocks, TOK_DEV)
    local_index = jax.vmap(block_slots)(routed_blocks)
    block_counts = jnp.sum(routed_blocks.astype(jnp.int32), axis=1)
    offsets = (jnp.arange(blocks, dtype=jnp.int32) * TOK_DEV)[:, None]
    index = (local_index + offsets).reshape(SLOTS).astype(jnp.int32)
    valid = (jnp.arange(CAP, dtype=jnp.int32)[None, :] < block_counts[:, None]).reshape(SLOTS)
    x_rows = jnp.where(valid[:, None], tokens[index], jnp.zeros((), jnp.bfloat16))
    y_rows = cotangent
    g_rows = jnp.where(valid, gate_low[index].astype(jnp.float32), jnp.float32(0.0))[:, None]
    pre_gate = jnp.dot(x_rows, gate_weight, preferred_element_type=jnp.float32)
    pre_up = jnp.dot(x_rows, up_weight, preferred_element_type=jnp.float32)
    sig = jax.nn.sigmoid(pre_gate)
    act = pre_gate * sig
    hidden = act * pre_up
    weighted = (g_rows * hidden).astype(jnp.bfloat16)
    back = jnp.dot(y_rows, down_weight.T, preferred_element_type=jnp.float32)
    products = jnp.sum(hidden * back, axis=1)
    scaled = g_rows * back
    d_pre_gate = (scaled * pre_up * sig * (1.0 + pre_gate * (1.0 - sig))).astype(jnp.bfloat16)
    d_pre_up = (scaled * act).astype(jnp.bfloat16)
    grad_down = jnp.dot(weighted.T, y_rows, preferred_element_type=jnp.float32).astype(jnp.bfloat16)
    grad_gate = jnp.dot(x_rows.T, d_pre_gate, preferred_element_type=jnp.float32).astype(jnp.bfloat16)
    grad_up = jnp.dot(x_rows.T, d_pre_up, preferred_element_type=jnp.float32).astype(jnp.bfloat16)
    row_grad = jnp.dot(d_pre_gate, gate_weight.T, preferred_element_type=jnp.float32)
    row_grad = row_grad + jnp.dot(d_pre_up, up_weight.T, preferred_element_type=jnp.float32)
    row_grad = jnp.where(valid[:, None], row_grad, jnp.float32(0.0))
    grad_tokens = jnp.zeros((TOKENS, D), jnp.float32).at[index].add(row_grad).astype(jnp.bfloat16)
    token_products = jnp.zeros((TOKENS,), jnp.float32).at[index].add(jnp.where(valid, products, jnp.float32(0.0)))
    slope = gate * (1.0 - gate)
    window_hot = (columns == 0).astype(jnp.float32)
    kl_grad = probs * (policy_log - frozen_log - divergence[:, None])
    grad_logits = kl_grad + (window_hot[None, :] - partner_hot) * (token_products * slope)[:, None]
    return grad_gate, grad_up, grad_down, grad_tokens, grad_logits, entropy, divergence
```

```python
import jax
import jax.numpy as jnp
from jax import lax
from jax.sharding import PartitionSpec as P


def contract_rows(left, right):
    return lax.dot_general(
        left, right, (((0,), (0,)), ((), ())), preferred_element_type=jnp.float32
    )


def contract_cols(left, right):
    return lax.dot_general(
        left, right, (((1,), (1,)), ((), ())), preferred_element_type=jnp.float32
    )


def make_shards(n):
    nz = n // 4

    def z_shift(d):
        return [(z * 4 + r, ((z + d) % nz) * 4 + r) for z in range(nz) for r in range(4)]

    def flip(bit):
        return [(i, i ^ bit) for i in range(n)]

    def gather(block):
        column = [block] + [lax.ppermute(block, "blk", z_shift(d)) for d in range(1, nz)]
        column = jnp.stack(column)
        plane = jnp.concatenate([column, lax.ppermute(column, "blk", flip(2))])
        whole = jnp.concatenate([plane, lax.ppermute(plane, "blk", flip(1))])
        return whole.reshape(n * block.shape[0], block.shape[1])

    def scatter(part):
        rows = part.shape[0] // n
        part = part.reshape(2, n // 2, rows, part.shape[1])
        got = lax.ppermute(part[1].astype(jnp.bfloat16), "blk", flip(1))
        part = part[0] + got.astype(jnp.float32)
        part = part.reshape(2, nz, rows, part.shape[2])
        got = lax.ppermute(part[1].astype(jnp.bfloat16), "blk", flip(2))
        part = part[0] + got.astype(jnp.float32)
        total = part[0]
        low = part.astype(jnp.bfloat16)
        for d in range(1, nz):
            got = lax.ppermute(low[d], "blk", z_shift(nz - d))
            total = total + got.astype(jnp.float32)
        return total

    def shards(
        tokens, cotangent, gate_weight, up_weight, down_weight, logits, ref_logits, routes
    ):
        policy_log = jax.nn.log_softmax(logits, axis=1)
        frozen_log = jax.nn.log_softmax(ref_logits, axis=1)
        probs = jnp.exp(policy_log)
        entropy = -jnp.sum(probs * policy_log, axis=1)
        divergence = jnp.sum(probs * (policy_log - frozen_log), axis=1)
        is_window = routes == 0
        routed = jnp.any(is_window, axis=1)
        partner = routes[:, 0] + routes[:, 1]
        columns = jnp.arange(logits.shape[1], dtype=jnp.int32)
        partner_hot = (columns[None, :] == partner[:, None]).astype(jnp.float32)
        partner_logit = jnp.sum(logits * partner_hot, axis=1)
        gate = jnp.where(
            routed, jax.nn.sigmoid(logits[:, 0] - partner_logit), jnp.float32(0.0)
        )
        gate_low = gate.astype(jnp.bfloat16)
        slot_count, width = cotangent.shape
        position = jnp.cumsum(routed.astype(jnp.int32)) - 1
        slot_ids = jnp.arange(slot_count, dtype=jnp.int32)
        select = (position[None, :] == slot_ids[:, None]) & routed[None, :]
        select_low = select.astype(jnp.bfloat16)
        select_full = select.astype(jnp.float32)
        x_slots = jnp.dot(select_low, tokens, preferred_element_type=jnp.float32).astype(
            jnp.bfloat16
        )
        g_slots = jnp.sum(select_full * gate_low.astype(jnp.float32)[None, :], axis=1).astype(
            jnp.bfloat16
        )
        y_all = gather(cotangent)
        send = jnp.concatenate(
            [x_slots, jnp.broadcast_to(g_slots[:, None], (slot_count, 128))], axis=1
        )
        xg_all = gather(send)
        x_all = xg_all[:, :width]
        g_col = xg_all[:, width : width + 1].astype(jnp.float32)
        pre_gate = jnp.dot(x_all, gate_weight, preferred_element_type=jnp.float32)
        pre_up = jnp.dot(x_all, up_weight, preferred_element_type=jnp.float32)
        sig = jax.nn.sigmoid(pre_gate)
        act = pre_gate * sig
        hidden = act * pre_up
        weighted = (g_col * hidden).astype(jnp.bfloat16)
        back = contract_cols(y_all, down_weight)
        products = jnp.sum(hidden * back, axis=1)
        scaled = g_col * back
        store_gate = (scaled * pre_up * sig * (1.0 + pre_gate * (1.0 - sig))).astype(
            jnp.bfloat16
        )
        store_up = (scaled * act).astype(jnp.bfloat16)
        row_grad = contract_cols(store_gate, gate_weight) + contract_cols(store_up, up_weight)
        high = lax.reduce_precision(products, 8, 7)
        low = products - high
        lane = jnp.arange(128, dtype=jnp.int32)[None, :]
        extra = jnp.where(lane == 0, high[:, None], jnp.where(lane == 1, low[:, None], 0.0))
        home = scatter(jnp.concatenate([row_grad, extra], axis=1))
        acc_gate = contract_rows(x_all, store_gate)
        acc_up = contract_rows(x_all, store_up)
        acc_down = contract_rows(weighted, y_all)
        slot_grads = home[:, :width].astype(jnp.bfloat16)
        slot_products = home[:, width] + home[:, width + 1]
        grad_tokens = contract_rows(select_low, slot_grads).astype(jnp.bfloat16)
        token_products = jnp.sum(select_full * slot_products[:, None], axis=0)
        slope = gate * (1.0 - gate)
        window_hot = (columns == 0).astype(jnp.float32)
        kl_grad = probs * (policy_log - frozen_log - divergence[:, None])
        grad_logits = (
            kl_grad + (window_hot[None, :] - partner_hot) * (token_products * slope)[:, None]
        )
        return (
            acc_gate.astype(jnp.bfloat16),
            acc_up.astype(jnp.bfloat16),
            acc_down.astype(jnp.bfloat16),
            grad_tokens,
            grad_logits,
            entropy,
            divergence,
        )

    return shards


def solution(mesh):
    in_specs = (
        P(("grp", "blk"), None),
        P(("grp", "blk"), None),
        P(None, "blk"),
        P(None, "blk"),
        P("blk", None),
        P(("grp", "blk"), None),
        P(("grp", "blk"), None),
        P(("grp", "blk"), None),
    )
    out_specs = (
        P("grp", "blk"),
        P("grp", "blk"),
        P(("grp", "blk"), None),
        P(("grp", "blk"), None),
        P(("grp", "blk"), None),
        P(("grp", "blk")),
        P(("grp", "blk")),
    )
    return jax.shard_map(
        make_shards(mesh.shape["blk"]),
        mesh=mesh,
        in_specs=in_specs,
        out_specs=out_specs,
        check_vma=False,
    )
```

```python
import jax
import jax.numpy as jnp
from jax import lax
from jax.experimental import pallas as pl
from jax.experimental.pallas import tpu as pltpu
from jax.sharding import PartitionSpec as P

F32 = jnp.float32
BF16 = jnp.bfloat16
LANES = 128
MIB = 1 << 20


def dot(left, right, dims):
    return lax.dot_general(left, right, (dims, ((), ())), preferred_element_type=F32)


def whole(count):
    return [pl.BlockSpec(memory_space=pltpu.VMEM)] * count


def call(kernel, outs, args, flops, moved, limit=8):
    return pl.pallas_call(
        kernel,
        out_shape=[jax.ShapeDtypeStruct(s, t) for s, t in outs],
        in_specs=whole(len(args)),
        out_specs=whole(len(outs)),
        compiler_params=pltpu.CompilerParams(vmem_limit_bytes=limit * MIB),
        cost_estimate=pl.CostEstimate(flops=flops, bytes_accessed=moved, transcendentals=0),
    )(*args)


def lane_pair(rows, first, second):
    lane = lax.broadcasted_iota(jnp.int32, (rows, LANES), 1)
    return jnp.where(lane == 0, first, jnp.where(lane == 1, second, 0.0))


def split_pair(value):
    high = value.astype(BF16).astype(F32)
    return lane_pair(value.shape[0], high, value - high)


def router_kernel(
    tokens, logits, ref_logits, routes, send, entropy, divergence, base, coef, select_out
):
    slots, width = send.shape[0], tokens.shape[1]
    experts, count = logits.shape
    x, r = logits[...], ref_logits[...]
    shifted = x - jnp.max(x, axis=0, keepdims=True)
    policy_log = shifted - jnp.log(jnp.sum(jnp.exp(shifted), axis=0, keepdims=True))
    shifted = r - jnp.max(r, axis=0, keepdims=True)
    frozen_log = shifted - jnp.log(jnp.sum(jnp.exp(shifted), axis=0, keepdims=True))
    probs = jnp.exp(policy_log)
    ratio = policy_log - frozen_log
    div = jnp.sum(probs * ratio, axis=0, keepdims=True)
    entropy[...] = -jnp.sum(probs * policy_log, axis=0, keepdims=True)
    divergence[...] = div
    base[...] = probs * (ratio - div)
    first, second = routes[0:1, :], routes[1:2, :]
    routed = jnp.where((first == 0) | (second == 0), 1.0, 0.0)
    expert = lax.broadcasted_iota(jnp.int32, (experts, count), 0)
    partner_hot = jnp.where(expert == first + second, 1.0, 0.0)
    partner_logit = jnp.sum(x * partner_hot, axis=0, keepdims=True)
    gate = jnp.where(routed > 0.0, jax.nn.sigmoid(x[0:1, :] - partner_logit), 0.0)
    coef[...] = (jnp.where(expert == 0, 1.0, 0.0) - partner_hot) * (gate * (1.0 - gate))
    token = lax.broadcasted_iota(jnp.int32, (1, count), 1)
    position = jnp.full((1, count), -1.0, F32)
    for t in range(count):
        position += jnp.where(token >= t, routed[:, t : t + 1], 0.0)
    slot = lax.broadcasted_iota(jnp.int32, (count, count), 0)
    hit = (slot == position.astype(jnp.int32)) & (routed > 0.0) & (slot < slots)
    select = jnp.where(hit, 1.0, 0.0)
    select_out[...] = select
    x_slots = dot(select.astype(BF16), tokens[...], ((1,), (0,)))
    send[:, :width] = x_slots[:slots].astype(BF16)
    gate_low = gate.astype(BF16).astype(F32)
    g_slots = jnp.sum(select * gate_low, axis=1, keepdims=True)
    send[:, width:] = jnp.broadcast_to(g_slots[:slots], (slots, LANES)).astype(BF16)


def back_kernel(y, down, back):
    back[...] = dot(y[...], down[...], ((1,), (1,)))


def expert_kernel(x, back, gate_w, up_w, send, keep, weighted, d_gate, d_up, acc_gate, acc_up):
    rows, width = x.shape[0], gate_w.shape[0]
    half = rows // 2
    step = 1536

    def fore(i, carry):
        at = pl.ds(pl.multiple_of(i * step, step), step)
        xs = x[:, at]
        acc_gate[...] += dot(xs, gate_w[at, :], ((1,), (0,)))
        acc_up[...] += dot(xs, up_w[at, :], ((1,), (0,)))
        return carry

    acc_gate[...] = jnp.zeros_like(acc_gate)
    acc_up[...] = jnp.zeros_like(acc_up)
    lax.fori_loop(0, width // step, fore, 0)
    pre_gate, pre_up = acc_gate[...], acc_up[...]
    g = x[:, width:][:, 0:1].astype(F32)
    sig = jax.nn.sigmoid(pre_gate)
    act = pre_gate * sig
    hidden = act * pre_up
    weighted[...] = (g * hidden).astype(BF16)
    products = jnp.sum(hidden * back[...], axis=1, keepdims=True)
    scaled = g * back[...]
    d_gate[...] = (scaled * pre_up * sig * (1.0 + pre_gate * (1.0 - sig))).astype(BF16)
    d_up[...] = (scaled * act).astype(BF16)
    keep[:, width:] = lane_pair(half, products[:half], 0.0)
    send[:, width:] = split_pair(products[half:]).astype(BF16)
    wide = 512

    def rear(i, carry):
        at = pl.ds(pl.multiple_of(i * wide, wide), wide)
        part = dot(d_gate[...], gate_w[at, :], ((1,), (1,)))
        part += dot(d_up[...], up_w[at, :], ((1,), (1,)))
        keep[:, at] = part[:half]
        send[:, at] = part[half:].astype(BF16)
        return carry

    lax.fori_loop(0, width // wide, rear, 0)


def fold_kernel(have, got, keep, send):
    half = keep.shape[0]
    width = keep.shape[1] - LANES
    total = have[:, :width] + got[:, :width].astype(F32)
    keep[:, :width] = total[:half]
    send[:, :width] = total[half:].astype(BF16)
    tail = have[:, width:] + got[:, width:].astype(F32)
    value = tail[:, 0:1] + tail[:, 1:2]
    keep[:, width:] = lane_pair(half, value[:half], 0.0)
    send[:, width:] = split_pair(value[half:]).astype(BF16)


def home_kernel(have, got, select, base, coef, grad_tokens, grad_logits):
    slots = have.shape[0]
    width = have.shape[1] - LANES
    count = select.shape[0]
    total = (have[:, :width] + got[:, :width].astype(F32)).astype(BF16)
    padded = jnp.concatenate([total, jnp.zeros((count - slots, width), BF16)], axis=0)
    grad_tokens[...] = dot(select[...].astype(BF16), padded, ((0,), (0,))).astype(BF16)
    tail = have[:, width:] + got[:, width:].astype(F32)
    value = tail[:, 0:1] + tail[:, 1:2]
    token_products = jnp.sum(select[0:slots, :] * value, axis=0, keepdims=True)
    grad_logits[...] = base[...] + coef[...] * token_products


def rows_kernel(left, right, out):
    out[...] = dot(left[...], right[...], ((0,), (0,))).astype(BF16)


def grad_rows(left, right):
    slots, cols = right.shape
    rows = left.shape[1] // 1024 * 1024
    return pl.pallas_call(
        rows_kernel,
        grid=(rows // 1024,),
        out_shape=jax.ShapeDtypeStruct((rows, cols), BF16),
        in_specs=[
            pl.BlockSpec((slots, 1024), lambda i: (0, i)),
            pl.BlockSpec((slots, cols), lambda i: (0, 0)),
        ],
        out_specs=pl.BlockSpec((1024, cols), lambda i: (i, 0)),
        compiler_params=pltpu.CompilerParams(vmem_limit_bytes=16 * MIB),
        cost_estimate=pl.CostEstimate(
            flops=8 * slots * rows * cols, bytes_accessed=2 * rows * cols, transcendentals=0
        ),
    )(left, right)


def grad_cols(left, right):
    slots, rows = left.shape
    cols = right.shape[1]
    return pl.pallas_call(
        rows_kernel,
        grid=(cols // 1024,),
        out_shape=jax.ShapeDtypeStruct((rows, cols), BF16),
        in_specs=[
            pl.BlockSpec((slots, rows), lambda i: (0, 0)),
            pl.BlockSpec((slots, 1024), lambda i: (0, i)),
        ],
        out_specs=pl.BlockSpec((rows, 1024), lambda i: (0, i)),
        compiler_params=pltpu.CompilerParams(vmem_limit_bytes=16 * MIB),
        cost_estimate=pl.CostEstimate(
            flops=8 * slots * rows * cols, bytes_accessed=2 * rows * cols, transcendentals=0
        ),
    )(left, right)


def make_shards(n):
    z_bits = []
    bit = n // 2
    while bit >= 4:
        z_bits.append(bit)
        bit //= 2
    nz = n // 4

    def swap(block, bit):
        return lax.ppermute(block, "blk", [(i, i ^ bit) for i in range(n)])

    def grow(block, bits):
        block = block[None]
        for bit in bits:
            block = jnp.concatenate([block, swap(block, bit)])
        return block

    def shards(
        tokens, cotangent, gate_weight, up_weight, down_weight, logits, ref_logits, routes
    ):
        count, width = tokens.shape
        slots = cotangent.shape[0]
        experts = logits.shape[1]
        hidden = down_weight.shape[0]
        rows = n * slots
        wide = width + LANES
        gate_w = pltpu.with_memory_space_constraint(gate_weight, pltpu.VMEM)
        up_w = pltpu.with_memory_space_constraint(up_weight, pltpu.VMEM)
        down_w = pltpu.with_memory_space_constraint(down_weight, pltpu.VMEM)

        send, entropy, divergence, base, coef, select = call(
            router_kernel,
            [
                ((slots, wide), BF16),
                ((1, count), F32),
                ((1, count), F32),
                ((experts, count), F32),
                ((experts, count), F32),
                ((count, count), F32),
            ],
            [tokens, logits.T, ref_logits.T, routes.T],
            1 << 20,
            1 << 18,
        )

        y_part = grow(cotangent, [2] + z_bits)
        y_part = y_part.reshape(nz, 2, slots, width).transpose(1, 0, 2, 3)
        y_part = y_part.reshape(rows // 2, width)
        y_all = jnp.concatenate([y_part, swap(y_part, 1)])
        x_part = grow(send, z_bits + [2]).reshape(rows // 2, wide)
        x_all = jnp.concatenate([x_part, swap(x_part, 1)])

        work = 2 * rows * width * hidden
        (back,) = call(
            back_kernel, [((rows, hidden), F32)], [y_all, down_w], 4 * work, 2 * width * hidden, 16
        )
        half = rows // 2
        low, keep, weighted, d_gate, d_up = pl.pallas_call(
            expert_kernel,
            out_shape=[
                jax.ShapeDtypeStruct((half, wide), BF16),
                jax.ShapeDtypeStruct((half, wide), F32),
                jax.ShapeDtypeStruct((rows, hidden), BF16),
                jax.ShapeDtypeStruct((rows, hidden), BF16),
                jax.ShapeDtypeStruct((rows, hidden), BF16),
            ],
            in_specs=whole(4),
            out_specs=whole(5),
            scratch_shapes=[pltpu.VMEM((rows, hidden), F32)] * 2,
            compiler_params=pltpu.CompilerParams(vmem_limit_bytes=32 * MIB),
            cost_estimate=pl.CostEstimate(
                flops=16 * work, bytes_accessed=4 * width * hidden, transcendentals=0
            ),
        )(x_all, back, gate_w, up_w)

        for bit in [1, 2] + z_bits[::-1]:
            got = swap(low, bit)
            if bit == z_bits[0]:
                break
            half //= 2
            keep, low = call(
                fold_kernel,
                [((half, wide), F32), ((half, wide), BF16)],
                [keep, got],
                4 * half * wide,
                16 * half * wide,
            )

        grad_down = grad_cols(weighted, y_all)
        grad_gate = grad_rows(x_all, d_gate)
        grad_up = grad_rows(x_all, d_up)

        grad_tokens, grad_logits = call(
            home_kernel,
            [((count, width), BF16), ((experts, count), F32)],
            [keep, got, select, base, coef],
            1 << 20,
            1 << 18,
        )
        return (
            grad_gate,
            grad_up,
            grad_down,
            grad_tokens,
            grad_logits.T,
            entropy.reshape(count),
            divergence.reshape(count),
        )

    return shards


def solution(mesh):
    in_specs = (
        P(("grp", "blk"), None),
        P(("grp", "blk"), None),
        P(None, "blk"),
        P(None, "blk"),
        P("blk", None),
        P(("grp", "blk"), None),
        P(("grp", "blk"), None),
        P(("grp", "blk"), None),
    )
    out_specs = (
        P("grp", "blk"),
        P("grp", "blk"),
        P(("grp", "blk"), None),
        P(("grp", "blk"), None),
        P(("grp", "blk"), None),
        P(("grp", "blk")),
        P(("grp", "blk")),
    )
    return jax.shard_map(
        make_shards(mesh.shape["blk"]),
        mesh=mesh,
        in_specs=in_specs,
        out_specs=out_specs,
        check_vma=False,
    )
```

```python
import functools

import jax
import jax.numpy as jnp
from jax import lax
from jax.experimental import pallas as pl
from jax.experimental.pallas import tpu as pltpu
from jax.sharding import PartitionSpec as P

F32 = jnp.float32
BF16 = jnp.bfloat16
LANES = 128
MIB = 1 << 20


def dot(left, right, dims):
    return lax.dot_general(left, right, (dims, ((), ())), preferred_element_type=F32)


def whole(count):
    return [pl.BlockSpec(memory_space=pltpu.VMEM)] * count


def call(kernel, outs, args, flops, moved, limit=8):
    return pl.pallas_call(
        kernel,
        out_shape=[jax.ShapeDtypeStruct(s, t) for s, t in outs],
        in_specs=whole(len(args)),
        out_specs=whole(len(outs)),
        compiler_params=pltpu.CompilerParams(vmem_limit_bytes=limit * MIB),
        cost_estimate=pl.CostEstimate(flops=flops, bytes_accessed=moved, transcendentals=0),
    )(*args)


def lane_pair(rows, first, second):
    lane = lax.broadcasted_iota(jnp.int32, (rows, LANES), 1)
    return jnp.where(lane == 0, first, jnp.where(lane == 1, second, 0.0))


def split_pair(value):
    high = value.astype(BF16).astype(F32)
    return lane_pair(value.shape[0], high, value - high)


def router_kernel(
    tokens_in,
    logits_in,
    ref_in,
    routes_in,
    send,
    entropy,
    divergence,
    base,
    coef,
    select_out,
    tokens,
    logits,
    ref_logits,
    routes,
    sems,
):
    sources = (logits_in, ref_in, routes_in, tokens_in)
    targets = (logits, ref_logits, routes, tokens)
    copies = [
        pltpu.make_async_copy(s, t, sems.at[i]) for i, (s, t) in enumerate(zip(sources, targets))
    ]
    for copy in copies:
        copy.start()
    for copy in copies[:3]:
        copy.wait()
    slots, width = send.shape[0], tokens.shape[1]
    experts, count = logits.shape
    x, r = logits[...], ref_logits[...]
    shifted = x - jnp.max(x, axis=0, keepdims=True)
    policy_log = shifted - jnp.log(jnp.sum(jnp.exp(shifted), axis=0, keepdims=True))
    shifted = r - jnp.max(r, axis=0, keepdims=True)
    frozen_log = shifted - jnp.log(jnp.sum(jnp.exp(shifted), axis=0, keepdims=True))
    probs = jnp.exp(policy_log)
    ratio = policy_log - frozen_log
    div = jnp.sum(probs * ratio, axis=0, keepdims=True)
    entropy[...] = -jnp.sum(probs * policy_log, axis=0, keepdims=True)
    divergence[...] = div
    base[...] = probs * (ratio - div)
    first, second = routes[0:1, :], routes[1:2, :]
    routed = jnp.where((first == 0) | (second == 0), 1.0, 0.0)
    expert = lax.broadcasted_iota(jnp.int32, (experts, count), 0)
    partner_hot = jnp.where(expert == first + second, 1.0, 0.0)
    partner_logit = jnp.sum(x * partner_hot, axis=0, keepdims=True)
    gate = jnp.where(routed > 0.0, jax.nn.sigmoid(x[0:1, :] - partner_logit), 0.0)
    coef[...] = (jnp.where(expert == 0, 1.0, 0.0) - partner_hot) * (gate * (1.0 - gate))
    token = lax.broadcasted_iota(jnp.int32, (1, count), 1)
    position = jnp.full((1, count), -1.0, F32)
    for t in range(count):
        position += jnp.where(token >= t, routed[:, t : t + 1], 0.0)
    slot = lax.broadcasted_iota(jnp.int32, (count, count), 0)
    hit = (slot == position.astype(jnp.int32)) & (routed > 0.0) & (slot < slots)
    select = jnp.where(hit, 1.0, 0.0)
    select_out[...] = select
    gate_low = gate.astype(BF16).astype(F32)
    g_slots = jnp.sum(select * gate_low, axis=1, keepdims=True)
    send[:, width:] = jnp.broadcast_to(g_slots[:slots], (slots, LANES)).astype(BF16)
    copies[3].wait()
    x_slots = dot(select.astype(BF16), tokens[...], ((1,), (0,)))
    send[:, :width] = x_slots[:slots].astype(BF16)


def back_kernel(y, down_in, back, down, sems):
    step = down.shape[2]

    def copy(i):
        at = pl.ds(pl.multiple_of(i * step, step), step)
        return pltpu.make_async_copy(down_in.at[:, at], down.at[i], sems.at[i])

    for i in range(down.shape[0]):
        copy(i).start()
    back[...] = jnp.zeros_like(back)

    def body(i, carry):
        copy(i).wait()
        at = pl.ds(pl.multiple_of(i * step, step), step)
        back[...] += dot(y[:, at], down[i], ((1,), (1,)))
        return carry

    lax.fori_loop(0, down.shape[0], body, 0)


def expert_kernel(
    x, back, gate_in, up_in, send, keep, weighted, d_both, gate_w, up_w, acc_gate, acc_up, sems
):
    rows, width, hidden_dim = x.shape[0], gate_w.shape[0], gate_w.shape[1]
    half = rows // 2
    chunks = sems.shape[1]
    step = width // chunks

    def copy(k, i):
        at = pl.ds(pl.multiple_of(i * step, step), step)
        source, target = ((gate_in, gate_w), (up_in, up_w))[k]
        return pltpu.make_async_copy(source.at[at], target.at[at], sems.at[k, i])

    for i in range(chunks):
        copy(0, i).start()
        copy(1, i).start()

    def fore(i, carry):
        at = pl.ds(pl.multiple_of(i * step, step), step)
        xs = x[:, at]
        copy(0, i).wait()
        acc_gate[...] += dot(xs, gate_w[at, :], ((1,), (0,)))
        copy(1, i).wait()
        acc_up[...] += dot(xs, up_w[at, :], ((1,), (0,)))
        return carry

    acc_gate[...] = jnp.zeros_like(acc_gate)
    acc_up[...] = jnp.zeros_like(acc_up)
    lax.fori_loop(0, chunks, fore, 0)
    pre_gate, pre_up = acc_gate[...], acc_up[...]
    g = x[:, width:][:, 0:1].astype(F32)
    sig = jax.nn.sigmoid(pre_gate)
    act = pre_gate * sig
    hidden = act * pre_up
    weighted[...] = (g * hidden).astype(BF16)
    products = jnp.sum(hidden * back[...], axis=1, keepdims=True)
    scaled = g * back[...]
    d_gate = (scaled * pre_up * sig * (1.0 + pre_gate * (1.0 - sig))).astype(BF16)
    d_up = (scaled * act).astype(BF16)
    d_both[:, :hidden_dim] = d_gate
    d_both[:, hidden_dim:] = d_up
    keep[:, width:] = lane_pair(half, products[:half], 0.0)
    send[:, width:] = split_pair(products[half:]).astype(BF16)
    wide = 512

    def rear(i, carry):
        at = pl.ds(pl.multiple_of(i * wide, wide), wide)
        part = dot(d_both[:, :hidden_dim], gate_w[at, :], ((1,), (1,)))
        part += dot(d_both[:, hidden_dim:], up_w[at, :], ((1,), (1,)))
        keep[:, at] = part[:half]
        send[:, at] = part[half:].astype(BF16)
        return carry

    lax.fori_loop(0, width // wide, rear, 0)


def fold_kernel(have, got, keep, send):
    half = keep.shape[0]
    width = keep.shape[1] - LANES
    total = have[:, :width] + got[:, :width].astype(F32)
    keep[:, :width] = total[:half]
    send[:, :width] = total[half:].astype(BF16)
    tail = have[:, width:] + got[:, width:].astype(F32)
    value = tail[:, 0:1] + tail[:, 1:2]
    keep[:, width:] = lane_pair(half, value[:half], 0.0)
    send[:, width:] = split_pair(value[half:]).astype(BF16)


def home_kernel(have, got, select, base, coef, grad_tokens, grad_logits):
    slots = have.shape[0]
    width = have.shape[1] - LANES
    count = select.shape[0]
    total = (have[:, :width] + got[:, :width].astype(F32)).astype(BF16)
    padded = jnp.concatenate([total, jnp.zeros((count - slots, width), BF16)], axis=0)
    grad_tokens[...] = dot(select[...].astype(BF16), padded, ((0,), (0,))).astype(BF16)
    tail = have[:, width:] + got[:, width:].astype(F32)
    value = tail[:, 0:1] + tail[:, 1:2]
    token_products = jnp.sum(select[0:slots, :] * value, axis=0, keepdims=True)
    grad_logits[...] = base[...] + coef[...] * token_products


def down_kernel(weighted, y, out, buf, sems):
    chunks, _, step = buf.shape

    def copy(i):
        at = pl.ds(pl.multiple_of(i * step, step), step)
        return pltpu.make_async_copy(buf.at[i], out.at[:, at], sems.at[i])

    def body(i, carry):
        at = pl.ds(pl.multiple_of(i * step, step), step)
        buf[i] = dot(weighted[...], y[:, at], ((0,), (0,))).astype(BF16)
        copy(i).start()
        return carry

    def finish(i, carry):
        copy(i).wait()
        return carry

    lax.fori_loop(0, chunks, body, 0)
    lax.fori_loop(0, chunks, finish, 0)


def pair_kernel(first_row, x, d_both, *refs):
    gate_out, up_out, gate_buf, up_buf, sems = refs[-5:]
    chunks, step, cols = gate_buf.shape

    def copy(k, i):
        at = pl.ds(pl.multiple_of(first_row + i * step, step), step)
        source, target = ((gate_buf, gate_out), (up_buf, up_out))[k]
        return pltpu.make_async_copy(source.at[i], target.at[at], sems.at[k, i])

    def body(i, carry):
        at = pl.ds(pl.multiple_of(first_row + i * step, step), step)
        both = dot(x[:, at], d_both[...], ((0,), (0,))).astype(BF16)
        gate_buf[i] = both[:, :cols]
        up_buf[i] = both[:, cols:]
        copy(0, i).start()
        copy(1, i).start()
        return carry

    def finish(i, carry):
        copy(0, i).wait()
        copy(1, i).wait()
        return carry

    lax.fori_loop(0, chunks, body, 0)
    lax.fori_loop(0, chunks, finish, 0)


def grad_down_of(weighted, y):
    hidden, width = weighted.shape[1], y.shape[1]
    step = 512
    return pl.pallas_call(
        down_kernel,
        out_shape=jax.ShapeDtypeStruct((hidden, width), BF16),
        in_specs=whole(2),
        out_specs=pl.BlockSpec(memory_space=pl.ANY),
        scratch_shapes=[
            pltpu.VMEM((width // step, hidden, step), BF16),
            pltpu.SemaphoreType.DMA((width // step,)),
        ],
        compiler_params=pltpu.CompilerParams(vmem_limit_bytes=16 * MIB),
        cost_estimate=pl.CostEstimate(
            flops=8 * weighted.size * width, bytes_accessed=2 * hidden * width, transcendentals=0
        ),
    )(weighted, y)


def grad_pair_of(x, d_both, width, part, parts, before):
    cols = d_both.shape[1] // 2
    step = 256
    rows = width // parts
    outs = [jax.ShapeDtypeStruct((width, cols), BF16)] * 2
    anywhere = pl.BlockSpec(memory_space=pl.ANY)
    return pl.pallas_call(
        functools.partial(pair_kernel, part * rows),
        out_shape=outs,
        in_specs=whole(2) + [anywhere] * len(before),
        out_specs=[anywhere] * 2,
        scratch_shapes=[
            pltpu.VMEM((rows // step, step, cols), BF16),
            pltpu.VMEM((rows // step, step, cols), BF16),
            pltpu.SemaphoreType.DMA((2, rows // step)),
        ],
        input_output_aliases={2 + i: i for i in range(len(before))},
        compiler_params=pltpu.CompilerParams(vmem_limit_bytes=16 * MIB),
        cost_estimate=pl.CostEstimate(
            flops=8 * x.shape[0] * rows * 2 * cols,
            bytes_accessed=4 * rows * cols,
            transcendentals=0,
        ),
    )(x, d_both, *before)


def make_shards(n):
    z_bits = []
    bit = n // 2
    while bit >= 4:
        z_bits.append(bit)
        bit //= 2
    nz = n // 4

    def swap(block, bit):
        return lax.ppermute(block, "blk", [(i, i ^ bit) for i in range(n)])

    def grow(block, bits):
        block = block[None]
        for bit in bits:
            block = lax.optimization_barrier(jnp.concatenate([block, swap(block, bit)]))
        return block

    def shards(
        tokens, cotangent, gate_weight, up_weight, down_weight, logits, ref_logits, routes
    ):
        count, width = tokens.shape
        slots = cotangent.shape[0]
        experts = logits.shape[1]
        hidden = down_weight.shape[0]
        rows = n * slots
        wide = width + LANES
        anywhere = pl.BlockSpec(memory_space=pl.ANY)

        send, entropy, divergence, base, coef, select = pl.pallas_call(
            router_kernel,
            out_shape=[
                jax.ShapeDtypeStruct((slots, wide), BF16),
                jax.ShapeDtypeStruct((1, count), F32),
                jax.ShapeDtypeStruct((1, count), F32),
                jax.ShapeDtypeStruct((experts, count), F32),
                jax.ShapeDtypeStruct((experts, count), F32),
                jax.ShapeDtypeStruct((count, count), F32),
            ],
            in_specs=[anywhere] * 4,
            out_specs=whole(6),
            scratch_shapes=[
                pltpu.VMEM((count, width), BF16),
                pltpu.VMEM((experts, count), F32),
                pltpu.VMEM((experts, count), F32),
                pltpu.VMEM((2, count), jnp.int32),
                pltpu.SemaphoreType.DMA((4,)),
            ],
            compiler_params=pltpu.CompilerParams(vmem_limit_bytes=8 * MIB),
            cost_estimate=pl.CostEstimate(
                flops=1 << 20, bytes_accessed=1 << 18, transcendentals=0
            ),
        )(tokens, logits.T, ref_logits.T, routes.T)

        y_part = grow(cotangent, z_bits[:-1] + [2, z_bits[-1]])
        y_part = y_part.reshape(2, 2, nz // 2, slots, width).transpose(1, 0, 2, 3, 4)
        y_part = y_part.reshape(rows // 2, width)
        y_all = jnp.concatenate([y_part, swap(y_part, 1)])
        x_part = grow(send, z_bits + [2]).reshape(rows // 2, wide)
        x_all = jnp.concatenate([x_part, swap(x_part, 1)])

        work = 2 * rows * width * hidden
        back = pl.pallas_call(
            back_kernel,
            out_shape=jax.ShapeDtypeStruct((rows, hidden), F32),
            in_specs=whole(1) + [anywhere],
            out_specs=whole(1)[0],
            scratch_shapes=[
                pltpu.VMEM((8, hidden, width // 8), BF16),
                pltpu.SemaphoreType.DMA((8,)),
            ],
            compiler_params=pltpu.CompilerParams(vmem_limit_bytes=24 * MIB),
            cost_estimate=pl.CostEstimate(
                flops=4 * work, bytes_accessed=2 * width * hidden, transcendentals=0
            ),
        )(y_all, down_weight)
        half = rows // 2
        low, keep, weighted, d_both = pl.pallas_call(
            expert_kernel,
            out_shape=[
                jax.ShapeDtypeStruct((half, wide), BF16),
                jax.ShapeDtypeStruct((half, wide), F32),
                jax.ShapeDtypeStruct((rows, hidden), BF16),
                jax.ShapeDtypeStruct((rows, 2 * hidden), BF16),
            ],
            in_specs=whole(2) + [anywhere] * 2,
            out_specs=whole(4),
            scratch_shapes=[
                pltpu.VMEM((width, hidden), BF16),
                pltpu.VMEM((width, hidden), BF16),
                pltpu.VMEM((rows, hidden), F32),
                pltpu.VMEM((rows, hidden), F32),
                pltpu.SemaphoreType.DMA((2, 8)),
            ],
            compiler_params=pltpu.CompilerParams(vmem_limit_bytes=32 * MIB),
            cost_estimate=pl.CostEstimate(
                flops=16 * work, bytes_accessed=4 * width * hidden, transcendentals=0
            ),
        )(x_all, back, gate_weight, up_weight)

        for bit in [1, 2] + z_bits[::-1]:
            got = swap(low, bit)
            if bit == z_bits[0]:
                break
            half //= 2
            keep, low = call(
                fold_kernel,
                [((half, wide), F32), ((half, wide), BF16)],
                [keep, got],
                4 * half * wide,
                16 * half * wide,
            )

        grad_down = grad_down_of(weighted, y_all)
        grad_pair = ()
        for part in range(2):
            grad_pair = grad_pair_of(x_all, d_both, width, part, 2, grad_pair)
        grad_gate, grad_up = grad_pair

        grad_tokens, grad_logits = call(
            home_kernel,
            [((count, width), BF16), ((experts, count), F32)],
            [keep, got, select, base, coef],
            1 << 20,
            1 << 18,
        )
        return (
            grad_gate,
            grad_up,
            grad_down,
            grad_tokens,
            grad_logits.T,
            entropy.reshape(count),
            divergence.reshape(count),
        )

    return shards


def solution(mesh):
    in_specs = (
        P(("grp", "blk"), None),
        P(("grp", "blk"), None),
        P(None, "blk"),
        P(None, "blk"),
        P("blk", None),
        P(("grp", "blk"), None),
        P(("grp", "blk"), None),
        P(("grp", "blk"), None),
    )
    out_specs = (
        P("grp", "blk"),
        P("grp", "blk"),
        P(("grp", "blk"), None),
        P(("grp", "blk"), None),
        P(("grp", "blk"), None),
        P(("grp", "blk")),
        P(("grp", "blk")),
    )
    return jax.shard_map(
        make_shards(mesh.shape["blk"]),
        mesh=mesh,
        in_specs=in_specs,
        out_specs=out_specs,
        check_vma=False,
    )
```

```python
import functools

import jax
import jax.numpy as jnp
from jax import lax
from jax.experimental import pallas as pl
from jax.experimental.pallas import tpu as pltpu
from jax.sharding import PartitionSpec as P

F32 = jnp.float32
BF16 = jnp.bfloat16
LANES = 128
MIB = 1 << 20


def dot(left, right, dims):
    return lax.dot_general(left, right, (dims, ((), ())), preferred_element_type=F32)


def whole(count):
    return [pl.BlockSpec(memory_space=pltpu.VMEM)] * count


def call(kernel, outs, args, flops, moved, limit=8):
    return pl.pallas_call(
        kernel,
        out_shape=[jax.ShapeDtypeStruct(s, t) for s, t in outs],
        in_specs=whole(len(args)),
        out_specs=whole(len(outs)),
        compiler_params=pltpu.CompilerParams(vmem_limit_bytes=limit * MIB),
        cost_estimate=pl.CostEstimate(flops=flops, bytes_accessed=moved, transcendentals=0),
    )(*args)


def in_hbm(array):
    return pltpu.with_memory_space_constraint(array, pltpu.HBM)


def lane_pair(rows, first, second):
    lane = lax.broadcasted_iota(jnp.int32, (rows, LANES), 1)
    return jnp.where(lane == 0, first, jnp.where(lane == 1, second, 0.0))


def split_pair(value):
    high = value.astype(BF16).astype(F32)
    return lane_pair(value.shape[0], high, value - high)


def router_kernel(
    tokens_in,
    logits_in,
    ref_in,
    routes_in,
    send,
    entropy,
    divergence,
    base,
    coef,
    select_out,
    tokens,
    logits,
    ref_logits,
    routes,
    sems,
):
    sources = (logits_in, ref_in, routes_in, tokens_in)
    targets = (logits, ref_logits, routes, tokens)
    copies = [
        pltpu.make_async_copy(s, t, sems.at[i]) for i, (s, t) in enumerate(zip(sources, targets))
    ]
    for copy in copies:
        copy.start()
    for copy in copies[:3]:
        copy.wait()
    slots, width = send.shape[0], tokens.shape[1]
    experts, count = logits.shape
    x, r = logits[...], ref_logits[...]
    shifted = x - jnp.max(x, axis=0, keepdims=True)
    policy_log = shifted - jnp.log(jnp.sum(jnp.exp(shifted), axis=0, keepdims=True))
    shifted = r - jnp.max(r, axis=0, keepdims=True)
    frozen_log = shifted - jnp.log(jnp.sum(jnp.exp(shifted), axis=0, keepdims=True))
    probs = jnp.exp(policy_log)
    ratio = policy_log - frozen_log
    div = jnp.sum(probs * ratio, axis=0, keepdims=True)
    entropy[...] = -jnp.sum(probs * policy_log, axis=0, keepdims=True)
    divergence[...] = div
    base[...] = probs * (ratio - div)
    first, second = routes[0:1, :], routes[1:2, :]
    routed = jnp.where((first == 0) | (second == 0), 1.0, 0.0)
    expert = lax.broadcasted_iota(jnp.int32, (experts, count), 0)
    partner_hot = jnp.where(expert == first + second, 1.0, 0.0)
    partner_logit = jnp.sum(x * partner_hot, axis=0, keepdims=True)
    gate = jnp.where(routed > 0.0, jax.nn.sigmoid(x[0:1, :] - partner_logit), 0.0)
    coef[...] = (jnp.where(expert == 0, 1.0, 0.0) - partner_hot) * (gate * (1.0 - gate))
    token = lax.broadcasted_iota(jnp.int32, (1, count), 1)
    position = jnp.full((1, count), -1.0, F32)
    for t in range(count):
        position += jnp.where(token >= t, routed[:, t : t + 1], 0.0)
    slot = lax.broadcasted_iota(jnp.int32, (count, count), 0)
    hit = (slot == position.astype(jnp.int32)) & (routed > 0.0) & (slot < slots)
    select = jnp.where(hit, 1.0, 0.0)
    select_out[...] = select
    gate_low = gate.astype(BF16).astype(F32)
    g_slots = jnp.sum(select * gate_low, axis=1, keepdims=True)
    send[:, width:] = jnp.broadcast_to(g_slots[:slots], (slots, LANES)).astype(BF16)
    copies[3].wait()
    x_slots = dot(select.astype(BF16), tokens[...], ((1,), (0,)))
    send[:, :width] = x_slots[:slots].astype(BF16)


def back_kernel(y, down_in, back, down, sems):
    chunks, _, step = down.shape

    def copy(i):
        return pltpu.make_async_copy(down_in.at[:, pl.ds(i * step, step)], down.at[i], sems.at[i])

    for i in range(chunks):
        copy(i).start()
    for i in range(chunks):
        copy(i).wait()
        part = dot(y[:, i * step : (i + 1) * step], down[i], ((1,), (1,)))
        back[...] = part if i == 0 else back[...] + part


def expert_kernel(
    x, back, gate_in, up_in, send, keep, weighted, d_both, both_w, acc, sems
):
    rows, width, hidden_dim = x.shape[0], both_w.shape[0], gate_in.shape[1]
    half = rows // 2
    chunks = sems.shape[1]
    step = width // chunks

    def copy(k, i):
        at = pl.ds(i * step, step)
        source = (gate_in, up_in)[k]
        target = both_w.at[at, pl.ds(k * hidden_dim, hidden_dim)]
        return pltpu.make_async_copy(source.at[at], target, sems.at[k, i])

    for i in range(chunks):
        copy(0, i).start()
        copy(1, i).start()
    for i in range(chunks):
        at = pl.ds(i * step, step)
        copy(0, i).wait()
        copy(1, i).wait()
        part = dot(x[:, at], both_w[at, :], ((1,), (0,)))
        acc[...] = part if i == 0 else acc[...] + part
    pre_gate, pre_up = acc[:, :hidden_dim], acc[:, hidden_dim:]
    g = x[:, width:][:, 0:1].astype(F32)
    sig = jax.nn.sigmoid(pre_gate)
    act = pre_gate * sig
    hidden = act * pre_up
    weighted[...] = (g * hidden).astype(BF16)
    products = jnp.sum(hidden * back[...], axis=1, keepdims=True)
    scaled = g * back[...]
    d_both[:, :hidden_dim] = (
        scaled * pre_up * sig * (1.0 + pre_gate * (1.0 - sig))
    ).astype(BF16)
    d_both[:, hidden_dim:] = (scaled * act).astype(BF16)
    keep[:, width:] = lane_pair(half, products[:half], 0.0)
    send[:, width:] = split_pair(products[half:]).astype(BF16)
    wide = 1024
    for i in range(width // wide):
        at = pl.ds(i * wide, wide)
        part = dot(d_both[...], both_w[at, :], ((1,), (1,)))
        keep[:, at] = part[:half]
        send[:, at] = part[half:].astype(BF16)


def fold_kernel(have, got, keep, send):
    half = keep.shape[0]
    width = keep.shape[1] - LANES
    total = have[:, :width] + got[:, :width].astype(F32)
    keep[:, :width] = total[:half]
    send[:, :width] = total[half:].astype(BF16)
    tail = have[:, width:] + got[:, width:].astype(F32)
    value = tail[:, 0:1] + tail[:, 1:2]
    keep[:, width:] = lane_pair(half, value[:half], 0.0)
    send[:, width:] = split_pair(value[half:]).astype(BF16)


def home_kernel(have, got, select, base, coef, grad_tokens, grad_logits):
    slots = have.shape[0]
    width = have.shape[1] - LANES
    count = select.shape[0]
    total = (have[:, :width] + got[:, :width].astype(F32)).astype(BF16)
    padded = jnp.concatenate([total, jnp.zeros((count - slots, width), BF16)], axis=0)
    grad_tokens[...] = dot(select[...].astype(BF16), padded, ((0,), (0,))).astype(BF16)
    tail = have[:, width:] + got[:, width:].astype(F32)
    value = tail[:, 0:1] + tail[:, 1:2]
    token_products = jnp.sum(select[0:slots, :] * value, axis=0, keepdims=True)
    grad_logits[...] = base[...] + coef[...] * token_products


def down_kernel(weighted, y, out, buf, turned, sems):
    chunks, _, step = buf.shape

    def copy(i):
        at = pl.ds(pl.multiple_of(i * step, step), step)
        return pltpu.make_async_copy(buf.at[i], out.at[:, at], sems.at[i])

    def body(i, carry):
        at = pl.ds(pl.multiple_of(i * step, step), step)
        buf[i] = dot(turned[...], y[:, at], ((1,), (0,))).astype(BF16)
        copy(i).start()
        return carry

    def finish(i, carry):
        copy(i).wait()
        return carry

    turned[...] = weighted[...].astype(F32).T.astype(BF16)
    lax.fori_loop(0, chunks, body, 0)
    lax.fori_loop(0, chunks, finish, 0)


def pair_kernel(first_row, x, d_both, *refs):
    gate_out, up_out, gate_buf, up_buf, sems = refs[-5:]
    chunks, step, cols = gate_buf.shape

    def copy(k, i):
        at = pl.ds(pl.multiple_of(first_row + i * step, step), step)
        source, target = ((gate_buf, gate_out), (up_buf, up_out))[k]
        return pltpu.make_async_copy(source.at[i], target.at[at], sems.at[k, i])

    def body(i, carry):
        at = pl.ds(pl.multiple_of(first_row + i * step, step), step)
        both = dot(x[:, at], d_both[...], ((0,), (0,))).astype(BF16)
        gate_buf[i] = both[:, :cols]
        up_buf[i] = both[:, cols:]
        copy(0, i).start()
        copy(1, i).start()
        return carry

    def finish(i, carry):
        copy(0, i).wait()
        copy(1, i).wait()
        return carry

    lax.fori_loop(0, chunks, body, 0)
    lax.fori_loop(0, chunks, finish, 0)


def grad_down_of(weighted, y):
    hidden, width = weighted.shape[1], y.shape[1]
    step = 512
    return pl.pallas_call(
        down_kernel,
        out_shape=jax.ShapeDtypeStruct((hidden, width), BF16),
        in_specs=whole(2),
        out_specs=pl.BlockSpec(memory_space=pl.ANY),
        scratch_shapes=[
            pltpu.VMEM((width // step, hidden, step), BF16),
            pltpu.VMEM((hidden, weighted.shape[0]), BF16),
            pltpu.SemaphoreType.DMA((width // step,)),
        ],
        compiler_params=pltpu.CompilerParams(vmem_limit_bytes=16 * MIB),
        cost_estimate=pl.CostEstimate(
            flops=8 * weighted.size * width, bytes_accessed=2 * hidden * width, transcendentals=0
        ),
    )(weighted, y)


def grad_pair_of(x, d_both, width, part, parts, before):
    cols = d_both.shape[1] // 2
    step = 256
    rows = width // parts
    outs = [jax.ShapeDtypeStruct((width, cols), BF16)] * 2
    anywhere = pl.BlockSpec(memory_space=pl.ANY)
    return pl.pallas_call(
        functools.partial(pair_kernel, part * rows),
        out_shape=outs,
        in_specs=whole(2) + [anywhere] * len(before),
        out_specs=[anywhere] * 2,
        scratch_shapes=[
            pltpu.VMEM((rows // step, step, cols), BF16),
            pltpu.VMEM((rows // step, step, cols), BF16),
            pltpu.SemaphoreType.DMA((2, rows // step)),
        ],
        input_output_aliases={2 + i: i for i in range(len(before))},
        compiler_params=pltpu.CompilerParams(vmem_limit_bytes=16 * MIB),
        cost_estimate=pl.CostEstimate(
            flops=8 * x.shape[0] * rows * 2 * cols,
            bytes_accessed=4 * rows * cols,
            transcendentals=0,
        ),
    )(x, d_both, *before)


def make_shards(n):
    z_bits = []
    bit = n // 2
    while bit >= 4:
        z_bits.append(bit)
        bit //= 2
    nz = n // 4

    def swap(block, bit):
        return lax.ppermute(block, "blk", [(i, i ^ bit) for i in range(n)])

    def grow(block, bits):
        block = block[None]
        for bit in bits:
            block = lax.optimization_barrier(jnp.concatenate([block, swap(block, bit)]))
        return block

    def shards(
        tokens, cotangent, gate_weight, up_weight, down_weight, logits, ref_logits, routes
    ):
        count, width = tokens.shape
        slots = cotangent.shape[0]
        experts = logits.shape[1]
        hidden = down_weight.shape[0]
        rows = n * slots
        wide = width + LANES
        anywhere = pl.BlockSpec(memory_space=pl.ANY)

        send, entropy, divergence, base, coef, select = pl.pallas_call(
            router_kernel,
            out_shape=[
                jax.ShapeDtypeStruct((slots, wide), BF16),
                jax.ShapeDtypeStruct((1, count), F32),
                jax.ShapeDtypeStruct((1, count), F32),
                jax.ShapeDtypeStruct((experts, count), F32),
                jax.ShapeDtypeStruct((experts, count), F32),
                jax.ShapeDtypeStruct((count, count), F32),
            ],
            in_specs=[anywhere] * 4,
            out_specs=whole(6),
            scratch_shapes=[
                pltpu.VMEM((count, width), BF16),
                pltpu.VMEM((experts, count), F32),
                pltpu.VMEM((experts, count), F32),
                pltpu.VMEM((2, count), jnp.int32),
                pltpu.SemaphoreType.DMA((4,)),
            ],
            compiler_params=pltpu.CompilerParams(vmem_limit_bytes=8 * MIB),
            cost_estimate=pl.CostEstimate(
                flops=1 << 20, bytes_accessed=1 << 18, transcendentals=0
            ),
        )(in_hbm(tokens), in_hbm(logits.T), in_hbm(ref_logits.T), in_hbm(routes.T))

        y_part = grow(cotangent, z_bits[:-1] + [2, z_bits[-1]])
        y_part = y_part.reshape(2, 2, nz // 2, slots, width).transpose(1, 0, 2, 3, 4)
        y_part = y_part.reshape(rows // 2, width)
        y_all = jnp.concatenate([y_part, swap(y_part, 1)])
        x_part = grow(send, z_bits + [2]).reshape(rows // 2, wide)
        x_all = jnp.concatenate([x_part, swap(x_part, 1)])

        work = 2 * rows * width * hidden
        back = pl.pallas_call(
            back_kernel,
            out_shape=jax.ShapeDtypeStruct((rows, hidden), F32),
            in_specs=whole(1) + [anywhere],
            out_specs=whole(1)[0],
            scratch_shapes=[
                pltpu.VMEM((4, hidden, width // 4), BF16),
                pltpu.SemaphoreType.DMA((4,)),
            ],
            compiler_params=pltpu.CompilerParams(vmem_limit_bytes=24 * MIB),
            cost_estimate=pl.CostEstimate(
                flops=4 * work, bytes_accessed=2 * width * hidden, transcendentals=0
            ),
        )(y_all, in_hbm(down_weight))
        half = rows // 2
        low, keep, weighted, d_both = pl.pallas_call(
            expert_kernel,
            out_shape=[
                jax.ShapeDtypeStruct((half, wide), BF16),
                jax.ShapeDtypeStruct((half, wide), F32),
                jax.ShapeDtypeStruct((rows, hidden), BF16),
                jax.ShapeDtypeStruct((rows, 2 * hidden), BF16),
            ],
            in_specs=whole(2) + [anywhere] * 2,
            out_specs=whole(4),
            scratch_shapes=[
                pltpu.VMEM((width, 2 * hidden), BF16),
                pltpu.VMEM((rows, 2 * hidden), F32),
                pltpu.SemaphoreType.DMA((2, 4)),
            ],
            compiler_params=pltpu.CompilerParams(vmem_limit_bytes=32 * MIB),
            cost_estimate=pl.CostEstimate(
                flops=16 * work, bytes_accessed=4 * width * hidden, transcendentals=0
            ),
        )(x_all, back, in_hbm(gate_weight), in_hbm(up_weight))

        for bit in [1, 2] + z_bits[::-1]:
            got = swap(low, bit)
            if bit == z_bits[0]:
                break
            half //= 2
            keep, low = call(
                fold_kernel,
                [((half, wide), F32), ((half, wide), BF16)],
                [keep, got],
                4 * half * wide,
                16 * half * wide,
            )

        grad_down = grad_down_of(weighted, y_all)
        grad_pair = ()
        for part in range(2):
            grad_pair = grad_pair_of(x_all, d_both, width, part, 2, grad_pair)
        grad_gate, grad_up = grad_pair

        grad_tokens, grad_logits = call(
            home_kernel,
            [((count, width), BF16), ((experts, count), F32)],
            [keep, got, select, base, coef],
            1 << 20,
            1 << 18,
        )
        return (
            grad_gate,
            grad_up,
            grad_down,
            grad_tokens,
            grad_logits.T,
            entropy.reshape(count),
            divergence.reshape(count),
        )

    return shards


def solution(mesh):
    in_specs = (
        P(("grp", "blk"), None),
        P(("grp", "blk"), None),
        P(None, "blk"),
        P(None, "blk"),
        P("blk", None),
        P(("grp", "blk"), None),
        P(("grp", "blk"), None),
        P(("grp", "blk"), None),
    )
    out_specs = (
        P("grp", "blk"),
        P("grp", "blk"),
        P(("grp", "blk"), None),
        P(("grp", "blk"), None),
        P(("grp", "blk"), None),
        P(("grp", "blk")),
        P(("grp", "blk")),
    )
    return jax.shard_map(
        make_shards(mesh.shape["blk"]),
        mesh=mesh,
        in_specs=in_specs,
        out_specs=out_specs,
        check_vma=False,
    )
```

```python
import functools

import jax
import jax.numpy as jnp
from jax import lax
from jax.experimental import pallas as pl
from jax.experimental.pallas import tpu as pltpu
from jax.sharding import PartitionSpec as P

F32 = jnp.float32
BF16 = jnp.bfloat16
LANES = 128
MIB = 1 << 20


def dot(left, right, dims):
    return lax.dot_general(left, right, (dims, ((), ())), preferred_element_type=F32)


def whole(count):
    return [pl.BlockSpec(memory_space=pltpu.VMEM)] * count


def call(kernel, outs, args, flops, moved, limit=8):
    return pl.pallas_call(
        kernel,
        out_shape=[jax.ShapeDtypeStruct(s, t) for s, t in outs],
        in_specs=whole(len(args)),
        out_specs=whole(len(outs)),
        compiler_params=pltpu.CompilerParams(vmem_limit_bytes=limit * MIB),
        cost_estimate=pl.CostEstimate(flops=flops, bytes_accessed=moved, transcendentals=0),
    )(*args)


def in_hbm(array):
    return pltpu.with_memory_space_constraint(array, pltpu.HBM)


def lane_pair(rows, first, second):
    lane = lax.broadcasted_iota(jnp.int32, (rows, LANES), 1)
    return jnp.where(lane == 0, first, jnp.where(lane == 1, second, 0.0))


def split_pair(value):
    high = value.astype(BF16).astype(F32)
    return lane_pair(value.shape[0], high, value - high)


def router_kernel(
    tokens_in,
    logits_in,
    ref_in,
    routes_in,
    send,
    entropy,
    divergence,
    base,
    coef,
    select_out,
    tokens,
    logits,
    ref_logits,
    routes,
    sems,
):
    sources = (logits_in, ref_in, routes_in, tokens_in)
    targets = (logits, ref_logits, routes, tokens)
    copies = [
        pltpu.make_async_copy(s, t, sems.at[i]) for i, (s, t) in enumerate(zip(sources, targets))
    ]
    for copy in copies:
        copy.start()
    for copy in copies[:3]:
        copy.wait()
    slots, width = send.shape[0], tokens.shape[1]
    experts, count = logits.shape
    x, r = logits[...], ref_logits[...]
    shifted = x - jnp.max(x, axis=0, keepdims=True)
    policy_log = shifted - jnp.log(jnp.sum(jnp.exp(shifted), axis=0, keepdims=True))
    shifted = r - jnp.max(r, axis=0, keepdims=True)
    frozen_log = shifted - jnp.log(jnp.sum(jnp.exp(shifted), axis=0, keepdims=True))
    probs = jnp.exp(policy_log)
    ratio = policy_log - frozen_log
    div = jnp.sum(probs * ratio, axis=0, keepdims=True)
    entropy[...] = -jnp.sum(probs * policy_log, axis=0, keepdims=True)
    divergence[...] = div
    base[...] = probs * (ratio - div)
    first, second = routes[0:1, :], routes[1:2, :]
    routed = jnp.where((first == 0) | (second == 0), 1.0, 0.0)
    expert = lax.broadcasted_iota(jnp.int32, (experts, count), 0)
    partner_hot = jnp.where(expert == first + second, 1.0, 0.0)
    partner_logit = jnp.sum(x * partner_hot, axis=0, keepdims=True)
    gate = jnp.where(routed > 0.0, jax.nn.sigmoid(x[0:1, :] - partner_logit), 0.0)
    coef[...] = (jnp.where(expert == 0, 1.0, 0.0) - partner_hot) * (gate * (1.0 - gate))
    token = lax.broadcasted_iota(jnp.int32, (1, count), 1)
    position = jnp.full((1, count), -1.0, F32)
    for t in range(count):
        position += jnp.where(token >= t, routed[:, t : t + 1], 0.0)
    slot = lax.broadcasted_iota(jnp.int32, (count, count), 0)
    hit = (slot == position.astype(jnp.int32)) & (routed > 0.0) & (slot < slots)
    select = jnp.where(hit, 1.0, 0.0)
    select_out[...] = select
    gate_low = gate.astype(BF16).astype(F32)
    g_slots = jnp.sum(select * gate_low, axis=1, keepdims=True)
    send[:, width:] = jnp.broadcast_to(g_slots[:slots], (slots, LANES)).astype(BF16)
    copies[3].wait()
    x_slots = dot(select.astype(BF16), tokens[...], ((1,), (0,)))
    send[:, :width] = x_slots[:slots].astype(BF16)


def back_kernel(y, down_in, back, down, sems):
    chunks, _, step = down.shape

    def copy(i):
        return pltpu.make_async_copy(down_in.at[:, pl.ds(i * step, step)], down.at[i], sems.at[i])

    for i in range(chunks):
        copy(i).start()
    for i in range(chunks):
        copy(i).wait()
        part = dot(y[:, i * step : (i + 1) * step], down[i], ((1,), (1,)))
        back[...] = part if i == 0 else back[...] + part


def expert_kernel(
    x, back, gate_in, up_in, send, keep, weighted, d_gate, d_up, both_w, d_both, acc, sems
):
    rows, width, hidden_dim = x.shape[0], both_w.shape[0], gate_in.shape[1]
    half = rows // 2
    chunks = sems.shape[1]
    step = width // chunks

    def copy(k, i):
        at = pl.ds(i * step, step)
        source = (gate_in, up_in)[k]
        target = both_w.at[at, pl.ds(k * hidden_dim, hidden_dim)]
        return pltpu.make_async_copy(source.at[at], target, sems.at[k, i])

    for i in range(chunks):
        copy(0, i).start()
        copy(1, i).start()
    for i in range(chunks):
        at = pl.ds(i * step, step)
        copy(0, i).wait()
        copy(1, i).wait()
        part = dot(x[:, at], both_w[at, :], ((1,), (0,)))
        acc[...] = part if i == 0 else acc[...] + part
    pre_gate, pre_up = acc[:, :hidden_dim], acc[:, hidden_dim:]
    g = x[:, width:][:, 0:1].astype(F32)
    sig = jax.nn.sigmoid(pre_gate)
    act = pre_gate * sig
    hidden = act * pre_up
    weighted[...] = (g * hidden).astype(BF16)
    products = jnp.sum(hidden * back[...], axis=1, keepdims=True)
    scaled = g * back[...]
    d_gate[...] = (scaled * pre_up * sig * (1.0 + pre_gate * (1.0 - sig))).astype(BF16)
    d_up[...] = (scaled * act).astype(BF16)
    d_both[:, :hidden_dim] = d_gate[...]
    d_both[:, hidden_dim:] = d_up[...]
    keep[:, width:] = lane_pair(half, products[:half], 0.0)
    send[:, width:] = split_pair(products[half:]).astype(BF16)
    wide = 1024
    for i in range(width // wide):
        at = pl.ds(i * wide, wide)
        part = dot(d_both[...], both_w[at, :], ((1,), (1,)))
        keep[:, at] = part[:half]
        send[:, at] = part[half:].astype(BF16)


def fold_kernel(have, got, keep, send):
    half = keep.shape[0]
    width = keep.shape[1] - LANES
    total = have[:, :width] + got[:, :width].astype(F32)
    keep[:, :width] = total[:half]
    send[:, :width] = total[half:].astype(BF16)
    tail = have[:, width:] + got[:, width:].astype(F32)
    value = tail[:, 0:1] + tail[:, 1:2]
    keep[:, width:] = lane_pair(half, value[:half], 0.0)
    send[:, width:] = split_pair(value[half:]).astype(BF16)


def home_kernel(have, got, select, base, coef, grad_tokens, grad_logits):
    slots = have.shape[0]
    width = have.shape[1] - LANES
    count = select.shape[0]
    total = (have[:, :width] + got[:, :width].astype(F32)).astype(BF16)
    padded = jnp.concatenate([total, jnp.zeros((count - slots, width), BF16)], axis=0)
    grad_tokens[...] = dot(select[...].astype(BF16), padded, ((0,), (0,))).astype(BF16)
    tail = have[:, width:] + got[:, width:].astype(F32)
    value = tail[:, 0:1] + tail[:, 1:2]
    token_products = jnp.sum(select[0:slots, :] * value, axis=0, keepdims=True)
    grad_logits[...] = base[...] + coef[...] * token_products


def down_kernel(weighted, y, out, turned):
    step = 512
    turned[...] = weighted[...].astype(F32).T.astype(BF16)

    def body(i, carry):
        at = pl.ds(pl.multiple_of(i * step, step), step)
        out[:, at] = dot(turned[...], y[:, at], ((1,), (0,))).astype(BF16)
        return carry

    lax.fori_loop(0, out.shape[1] // step, body, 0)


def rows_kernel(x, d, out):
    step = 512

    def body(i, carry):
        at = pl.ds(pl.multiple_of(i * step, step), step)
        out[at, :] = dot(x[:, at], d[...], ((0,), (0,))).astype(BF16)
        return carry

    lax.fori_loop(0, out.shape[0] // step, body, 0)


def grad_of(kernel, left, right, shape, scratch):
    return pl.pallas_call(
        kernel,
        out_shape=pltpu.VMEM(shape, BF16),
        in_specs=whole(2),
        out_specs=pl.BlockSpec(memory_space=pltpu.VMEM),
        scratch_shapes=scratch,
        compiler_params=pltpu.CompilerParams(vmem_limit_bytes=8 * MIB),
        cost_estimate=pl.CostEstimate(
            flops=8 * left.shape[0] * shape[0] * shape[1],
            bytes_accessed=2 * shape[0] * shape[1],
            transcendentals=0,
        ),
    )(left, right)


def make_shards(n):
    z_bits = []
    bit = n // 2
    while bit >= 4:
        z_bits.append(bit)
        bit //= 2
    nz = n // 4

    def swap(block, bit):
        return lax.ppermute(block, "blk", [(i, i ^ bit) for i in range(n)])

    def grow(block, bits):
        block = block[None]
        for bit in bits:
            block = lax.optimization_barrier(jnp.concatenate([block, swap(block, bit)]))
        return block

    def shards(
        tokens, cotangent, gate_weight, up_weight, down_weight, logits, ref_logits, routes
    ):
        count, width = tokens.shape
        slots = cotangent.shape[0]
        experts = logits.shape[1]
        hidden = down_weight.shape[0]
        rows = n * slots
        wide = width + LANES
        anywhere = pl.BlockSpec(memory_space=pl.ANY)

        send, entropy, divergence, base, coef, select = pl.pallas_call(
            router_kernel,
            out_shape=[
                jax.ShapeDtypeStruct((slots, wide), BF16),
                jax.ShapeDtypeStruct((1, count), F32),
                jax.ShapeDtypeStruct((1, count), F32),
                jax.ShapeDtypeStruct((experts, count), F32),
                jax.ShapeDtypeStruct((experts, count), F32),
                jax.ShapeDtypeStruct((count, count), F32),
            ],
            in_specs=[anywhere] * 4,
            out_specs=whole(6),
            scratch_shapes=[
                pltpu.VMEM((count, width), BF16),
                pltpu.VMEM((experts, count), F32),
                pltpu.VMEM((experts, count), F32),
                pltpu.VMEM((2, count), jnp.int32),
                pltpu.SemaphoreType.DMA((4,)),
            ],
            compiler_params=pltpu.CompilerParams(vmem_limit_bytes=8 * MIB),
            cost_estimate=pl.CostEstimate(
                flops=1 << 20, bytes_accessed=1 << 18, transcendentals=0
            ),
        )(in_hbm(tokens), in_hbm(logits.T), in_hbm(ref_logits.T), in_hbm(routes.T))

        y_part = grow(cotangent, z_bits[:-1] + [2, z_bits[-1]])
        y_part = y_part.reshape(2, 2, nz // 2, slots, width).transpose(1, 0, 2, 3, 4)
        y_part = y_part.reshape(rows // 2, width)
        y_all = jnp.concatenate([y_part, swap(y_part, 1)])
        x_part = grow(send, z_bits + [2]).reshape(rows // 2, wide)
        x_all = jnp.concatenate([x_part, swap(x_part, 1)])

        work = 2 * rows * width * hidden
        back = pl.pallas_call(
            back_kernel,
            out_shape=jax.ShapeDtypeStruct((rows, hidden), F32),
            in_specs=whole(1) + [anywhere],
            out_specs=whole(1)[0],
            scratch_shapes=[
                pltpu.VMEM((4, hidden, width // 4), BF16),
                pltpu.SemaphoreType.DMA((4,)),
            ],
            compiler_params=pltpu.CompilerParams(vmem_limit_bytes=24 * MIB),
            cost_estimate=pl.CostEstimate(
                flops=4 * work, bytes_accessed=2 * width * hidden, transcendentals=0
            ),
        )(y_all, in_hbm(down_weight))
        half = rows // 2
        low, keep, weighted, d_gate, d_up = pl.pallas_call(
            expert_kernel,
            out_shape=[
                jax.ShapeDtypeStruct((half, wide), BF16),
                jax.ShapeDtypeStruct((half, wide), F32),
                jax.ShapeDtypeStruct((rows, hidden), BF16),
                jax.ShapeDtypeStruct((rows, hidden), BF16),
                jax.ShapeDtypeStruct((rows, hidden), BF16),
            ],
            in_specs=whole(2) + [anywhere] * 2,
            out_specs=whole(5),
            scratch_shapes=[
                pltpu.VMEM((width, 2 * hidden), BF16),
                pltpu.VMEM((rows, 2 * hidden), BF16),
                pltpu.VMEM((rows, 2 * hidden), F32),
                pltpu.SemaphoreType.DMA((2, 4)),
            ],
            compiler_params=pltpu.CompilerParams(vmem_limit_bytes=32 * MIB),
            cost_estimate=pl.CostEstimate(
                flops=16 * work, bytes_accessed=4 * width * hidden, transcendentals=0
            ),
        )(x_all, back, in_hbm(gate_weight), in_hbm(up_weight))

        for bit in [1, 2] + z_bits[::-1]:
            got = swap(low, bit)
            if bit == z_bits[0]:
                break
            half //= 2
            keep, low = call(
                fold_kernel,
                [((half, wide), F32), ((half, wide), BF16)],
                [keep, got],
                4 * half * wide,
                16 * half * wide,
            )

        grad_down = grad_of(
            down_kernel, weighted, y_all, (hidden, width), [pltpu.VMEM((hidden, rows), BF16)]
        )
        grad_gate = grad_of(rows_kernel, x_all, d_gate, (width, hidden), [])
        grad_up = grad_of(rows_kernel, x_all, d_up, (width, hidden), [])

        grad_tokens, grad_logits = call(
            home_kernel,
            [((count, width), BF16), ((experts, count), F32)],
            [keep, got, select, base, coef],
            1 << 20,
            1 << 18,
        )
        return (
            grad_gate,
            grad_up,
            grad_down,
            grad_tokens,
            grad_logits.T,
            entropy.reshape(count),
            divergence.reshape(count),
        )

    return shards


def solution(mesh):
    in_specs = (
        P(("grp", "blk"), None),
        P(("grp", "blk"), None),
        P(None, "blk"),
        P(None, "blk"),
        P("blk", None),
        P(("grp", "blk"), None),
        P(("grp", "blk"), None),
        P(("grp", "blk"), None),
    )
    out_specs = (
        P("grp", "blk"),
        P("grp", "blk"),
        P(("grp", "blk"), None),
        P(("grp", "blk"), None),
        P(("grp", "blk"), None),
        P(("grp", "blk")),
        P(("grp", "blk")),
    )
    return jax.shard_map(
        make_shards(mesh.shape["blk"]),
        mesh=mesh,
        in_specs=in_specs,
        out_specs=out_specs,
        check_vma=False,
    )
```

```python
import functools

import jax
import jax.numpy as jnp
from jax import lax
from jax.experimental import pallas as pl
from jax.experimental.pallas import tpu as pltpu
from jax.sharding import PartitionSpec as P

F32 = jnp.float32
BF16 = jnp.bfloat16
LANES = 128
MIB = 1 << 20


def dot(left, right, dims):
    return lax.dot_general(left, right, (dims, ((), ())), preferred_element_type=F32)


def whole(count):
    return [pl.BlockSpec(memory_space=pltpu.VMEM)] * count


def call(kernel, outs, args, flops, moved, limit=8):
    return pl.pallas_call(
        kernel,
        out_shape=[jax.ShapeDtypeStruct(s, t) for s, t in outs],
        in_specs=whole(len(args)),
        out_specs=whole(len(outs)),
        compiler_params=pltpu.CompilerParams(vmem_limit_bytes=limit * MIB),
        cost_estimate=pl.CostEstimate(flops=flops, bytes_accessed=moved, transcendentals=0),
    )(*args)


def in_hbm(array):
    return pltpu.with_memory_space_constraint(array, pltpu.HBM)


def lane_pair(rows, first, second):
    lane = lax.broadcasted_iota(jnp.int32, (rows, LANES), 1)
    return jnp.where(lane == 0, first, jnp.where(lane == 1, second, 0.0))


def split_pair(value):
    high = value.astype(BF16).astype(F32)
    return lane_pair(value.shape[0], high, value - high)


def router_kernel(
    tokens_in,
    logits_in,
    ref_in,
    routes_in,
    send,
    entropy,
    divergence,
    base,
    coef,
    select_out,
    tokens,
    logits,
    ref_logits,
    routes,
    sems,
):
    sources = (logits_in, ref_in, routes_in, tokens_in)
    targets = (logits, ref_logits, routes, tokens)
    copies = [
        pltpu.make_async_copy(s, t, sems.at[i]) for i, (s, t) in enumerate(zip(sources, targets))
    ]
    for copy in copies:
        copy.start()
    for copy in copies[:3]:
        copy.wait()
    slots, width = send.shape[0], tokens.shape[1]
    experts, count = logits.shape
    x, r = logits[...], ref_logits[...]
    shifted = x - jnp.max(x, axis=0, keepdims=True)
    policy_log = shifted - jnp.log(jnp.sum(jnp.exp(shifted), axis=0, keepdims=True))
    shifted = r - jnp.max(r, axis=0, keepdims=True)
    frozen_log = shifted - jnp.log(jnp.sum(jnp.exp(shifted), axis=0, keepdims=True))
    probs = jnp.exp(policy_log)
    ratio = policy_log - frozen_log
    div = jnp.sum(probs * ratio, axis=0, keepdims=True)
    entropy[...] = -jnp.sum(probs * policy_log, axis=0, keepdims=True)
    divergence[...] = div
    base[...] = probs * (ratio - div)
    first, second = routes[0:1, :], routes[1:2, :]
    routed = jnp.where((first == 0) | (second == 0), 1.0, 0.0)
    expert = lax.broadcasted_iota(jnp.int32, (experts, count), 0)
    partner_hot = jnp.where(expert == first + second, 1.0, 0.0)
    partner_logit = jnp.sum(x * partner_hot, axis=0, keepdims=True)
    gate = jnp.where(routed > 0.0, jax.nn.sigmoid(x[0:1, :] - partner_logit), 0.0)
    coef[...] = (jnp.where(expert == 0, 1.0, 0.0) - partner_hot) * (gate * (1.0 - gate))
    token = lax.broadcasted_iota(jnp.int32, (1, count), 1)
    position = jnp.full((1, count), -1.0, F32)
    for t in range(count):
        position += jnp.where(token >= t, routed[:, t : t + 1], 0.0)
    slot = lax.broadcasted_iota(jnp.int32, (count, count), 0)
    hit = (slot == position.astype(jnp.int32)) & (routed > 0.0) & (slot < slots)
    select = jnp.where(hit, 1.0, 0.0)
    select_out[...] = select
    gate_low = gate.astype(BF16).astype(F32)
    g_slots = jnp.sum(select * gate_low, axis=1, keepdims=True)
    send[:, width:] = jnp.broadcast_to(g_slots[:slots], (slots, LANES)).astype(BF16)
    copies[3].wait()
    x_slots = dot(select.astype(BF16), tokens[...], ((1,), (0,)))
    send[:, :width] = x_slots[:slots].astype(BF16)


def back_kernel(y, down_in, back, down, sems):
    chunks, _, step = down.shape

    def copy(i):
        return pltpu.make_async_copy(down_in.at[:, pl.ds(i * step, step)], down.at[i], sems.at[i])

    for i in range(chunks):
        copy(i).start()
    for i in range(chunks):
        copy(i).wait()
        part = dot(y[:, i * step : (i + 1) * step], down[i], ((1,), (1,)))
        back[...] = part if i == 0 else back[...] + part


def expert_kernel(
    x, back, gate_in, up_in, send, keep, weighted_t, d_both, x_t, both_w, acc, sems
):
    rows, width, hidden_dim = x.shape[0], both_w.shape[0], gate_in.shape[1]
    half = rows // 2
    chunks = sems.shape[1]
    step = width // chunks

    def copy(k, i):
        at = pl.ds(i * step, step)
        source = (gate_in, up_in)[k]
        target = both_w.at[at, pl.ds(k * hidden_dim, hidden_dim)]
        return pltpu.make_async_copy(source.at[at], target, sems.at[k, i])

    for i in range(chunks):
        copy(0, i).start()
        copy(1, i).start()
    for c in range(0, width, LANES):
        x_t[c : c + LANES, :] = x[:, c : c + LANES].astype(F32).T.astype(BF16)
    for i in range(chunks):
        at = pl.ds(i * step, step)
        copy(0, i).wait()
        copy(1, i).wait()
        part = dot(x[:, at], both_w[at, :], ((1,), (0,)))
        acc[...] = part if i == 0 else acc[...] + part
    pre_gate, pre_up = acc[:, :hidden_dim], acc[:, hidden_dim:]
    g = x[:, width:][:, 0:1].astype(F32)
    sig = jax.nn.sigmoid(pre_gate)
    act = pre_gate * sig
    hidden = act * pre_up
    weighted_t[...] = (g * hidden).T.astype(BF16)
    products = jnp.sum(hidden * back[...], axis=1, keepdims=True)
    scaled = g * back[...]
    d_both[:, :hidden_dim] = (
        scaled * pre_up * sig * (1.0 + pre_gate * (1.0 - sig))
    ).astype(BF16)
    d_both[:, hidden_dim:] = (scaled * act).astype(BF16)
    keep[:, width:] = lane_pair(half, products[:half], 0.0)
    send[:, width:] = split_pair(products[half:]).astype(BF16)
    wide = 1024
    for i in range(width // wide):
        at = pl.ds(i * wide, wide)
        part = dot(d_both[...], both_w[at, :], ((1,), (1,)))
        keep[:, at] = part[:half]
        send[:, at] = part[half:].astype(BF16)


def fold_kernel(have, got, keep, send):
    half = keep.shape[0]
    width = keep.shape[1] - LANES
    total = have[:, :width] + got[:, :width].astype(F32)
    keep[:, :width] = total[:half]
    send[:, :width] = total[half:].astype(BF16)
    tail = have[:, width:] + got[:, width:].astype(F32)
    value = tail[:, 0:1] + tail[:, 1:2]
    keep[:, width:] = lane_pair(half, value[:half], 0.0)
    send[:, width:] = split_pair(value[half:]).astype(BF16)


def home_kernel(have, got, select, base, coef, grad_tokens, grad_logits):
    slots = have.shape[0]
    width = have.shape[1] - LANES
    count = select.shape[0]
    total = (have[:, :width] + got[:, :width].astype(F32)).astype(BF16)
    padded = jnp.concatenate([total, jnp.zeros((count - slots, width), BF16)], axis=0)
    grad_tokens[...] = dot(select[...].astype(BF16), padded, ((0,), (0,))).astype(BF16)
    tail = have[:, width:] + got[:, width:].astype(F32)
    value = tail[:, 0:1] + tail[:, 1:2]
    token_products = jnp.sum(select[0:slots, :] * value, axis=0, keepdims=True)
    grad_logits[...] = base[...] + coef[...] * token_products


def tiles(out, left, right):
    for c in range(0, right.shape[1], 256):
        for r in range(0, left.shape[0], 128):
            part = dot(left[r : r + 128], right[:, c : c + 256], ((1,), (0,)))
            out[r : r + 128, c : c + 256] = part.astype(BF16)


def down_kernel(weighted_t, y, out, buf, sems):
    chunks, _, step = buf.shape

    def copy(i):
        at = pl.ds(pl.multiple_of(i * step, step), step)
        return pltpu.make_async_copy(buf.at[i], out.at[:, at], sems.at[i])

    def body(i, carry):
        at = pl.ds(pl.multiple_of(i * step, step), step)
        tiles(buf.at[i], weighted_t, y.at[:, at])
        copy(i).start()
        return carry

    def finish(i, carry):
        copy(i).wait()
        return carry

    lax.fori_loop(0, chunks, body, 0)
    lax.fori_loop(0, chunks, finish, 0)


def pair_kernel(first_row, x_t, d_both, *refs):
    gate_out, up_out, gate_buf, up_buf, sems = refs[-5:]
    chunks, step, cols = gate_buf.shape

    def copy(k, i):
        at = pl.ds(pl.multiple_of(first_row + i * step, step), step)
        source, target = ((gate_buf, gate_out), (up_buf, up_out))[k]
        return pltpu.make_async_copy(source.at[i], target.at[at], sems.at[k, i])

    def body(i, carry):
        at = pl.ds(pl.multiple_of(first_row + i * step, step), step)
        tiles(gate_buf.at[i], x_t.at[at], d_both.at[:, pl.ds(0, cols)])
        copy(0, i).start()
        tiles(up_buf.at[i], x_t.at[at], d_both.at[:, pl.ds(cols, cols)])
        copy(1, i).start()
        return carry

    def finish(i, carry):
        copy(0, i).wait()
        copy(1, i).wait()
        return carry

    lax.fori_loop(0, chunks, body, 0)
    lax.fori_loop(0, chunks, finish, 0)


def grad_down_of(weighted_t, y):
    hidden, width = weighted_t.shape[0], y.shape[1]
    step = 1024
    return pl.pallas_call(
        down_kernel,
        out_shape=jax.ShapeDtypeStruct((hidden, width), BF16),
        in_specs=whole(2),
        out_specs=pl.BlockSpec(memory_space=pl.ANY),
        scratch_shapes=[
            pltpu.VMEM((width // step, hidden, step), BF16),
            pltpu.SemaphoreType.DMA((width // step,)),
        ],
        compiler_params=pltpu.CompilerParams(vmem_limit_bytes=16 * MIB),
        cost_estimate=pl.CostEstimate(
            flops=8 * weighted_t.size * width,
            bytes_accessed=2 * hidden * width,
            transcendentals=0,
        ),
    )(weighted_t, y)


def grad_pair_of(x_t, d_both, part, parts, before):
    width, cols = x_t.shape[0], d_both.shape[1] // 2
    step = 512
    rows = width // parts
    outs = [jax.ShapeDtypeStruct((width, cols), BF16)] * 2
    anywhere = pl.BlockSpec(memory_space=pl.ANY)
    return pl.pallas_call(
        functools.partial(pair_kernel, part * rows),
        out_shape=outs,
        in_specs=whole(2) + [anywhere] * len(before),
        out_specs=[anywhere] * 2,
        scratch_shapes=[
            pltpu.VMEM((rows // step, step, cols), BF16),
            pltpu.VMEM((rows // step, step, cols), BF16),
            pltpu.SemaphoreType.DMA((2, rows // step)),
        ],
        input_output_aliases={2 + i: i for i in range(len(before))},
        compiler_params=pltpu.CompilerParams(vmem_limit_bytes=16 * MIB),
        cost_estimate=pl.CostEstimate(
            flops=8 * x_t.shape[1] * rows * 2 * cols,
            bytes_accessed=4 * rows * cols,
            transcendentals=0,
        ),
    )(x_t, d_both, *before)


def make_shards(n):
    levels = []
    bit = n // 2
    while bit > 4:
        levels.append((bit, bit))
        bit //= 2
    levels += [(4, 2), (2, 4)]

    def swap(block, bits):
        return lax.ppermute(block, "blk", [(i, i ^ bits[i % 2]) for i in range(n)])

    def gather(block):
        rows = n // 2 * block.shape[0]
        block = block[None]
        for bits in levels:
            block = lax.optimization_barrier(jnp.concatenate([block, swap(block, bits)]))
        block = block.reshape(rows, block.shape[2])
        return jnp.concatenate([block, swap(block, (1, 1))])

    def shards(
        tokens, cotangent, gate_weight, up_weight, down_weight, logits, ref_logits, routes
    ):
        count, width = tokens.shape
        slots = cotangent.shape[0]
        experts = logits.shape[1]
        hidden = down_weight.shape[0]
        rows = n * slots
        wide = width + LANES
        anywhere = pl.BlockSpec(memory_space=pl.ANY)

        send, entropy, divergence, base, coef, select = pl.pallas_call(
            router_kernel,
            out_shape=[
                jax.ShapeDtypeStruct((slots, wide), BF16),
                jax.ShapeDtypeStruct((1, count), F32),
                jax.ShapeDtypeStruct((1, count), F32),
                jax.ShapeDtypeStruct((experts, count), F32),
                jax.ShapeDtypeStruct((experts, count), F32),
                jax.ShapeDtypeStruct((count, count), F32),
            ],
            in_specs=[anywhere] * 4,
            out_specs=whole(6),
            scratch_shapes=[
                pltpu.VMEM((count, width), BF16),
                pltpu.VMEM((experts, count), F32),
                pltpu.VMEM((experts, count), F32),
                pltpu.VMEM((2, count), jnp.int32),
                pltpu.SemaphoreType.DMA((4,)),
            ],
            compiler_params=pltpu.CompilerParams(vmem_limit_bytes=8 * MIB),
            cost_estimate=pl.CostEstimate(
                flops=1 << 20, bytes_accessed=1 << 18, transcendentals=0
            ),
        )(in_hbm(tokens), in_hbm(logits.T), in_hbm(ref_logits.T), in_hbm(routes.T))

        y_all = gather(cotangent)
        x_all = gather(send)

        work = 2 * rows * width * hidden
        back = pl.pallas_call(
            back_kernel,
            out_shape=jax.ShapeDtypeStruct((rows, hidden), F32),
            in_specs=whole(1) + [anywhere],
            out_specs=whole(1)[0],
            scratch_shapes=[
                pltpu.VMEM((4, hidden, width // 4), BF16),
                pltpu.SemaphoreType.DMA((4,)),
            ],
            compiler_params=pltpu.CompilerParams(vmem_limit_bytes=24 * MIB),
            cost_estimate=pl.CostEstimate(
                flops=4 * work, bytes_accessed=2 * width * hidden, transcendentals=0
            ),
        )(y_all, in_hbm(down_weight))
        half = rows // 2
        low, keep, weighted_t, d_both, x_t = pl.pallas_call(
            expert_kernel,
            out_shape=[
                jax.ShapeDtypeStruct((half, wide), BF16),
                jax.ShapeDtypeStruct((half, wide), F32),
                jax.ShapeDtypeStruct((hidden, rows), BF16),
                jax.ShapeDtypeStruct((rows, 2 * hidden), BF16),
                jax.ShapeDtypeStruct((width, rows), BF16),
            ],
            in_specs=whole(2) + [anywhere] * 2,
            out_specs=whole(5),
            scratch_shapes=[
                pltpu.VMEM((width, 2 * hidden), BF16),
                pltpu.VMEM((rows, 2 * hidden), F32),
                pltpu.SemaphoreType.DMA((2, 4)),
            ],
            compiler_params=pltpu.CompilerParams(vmem_limit_bytes=32 * MIB),
            cost_estimate=pl.CostEstimate(
                flops=16 * work, bytes_accessed=4 * width * hidden, transcendentals=0
            ),
        )(x_all, back, in_hbm(gate_weight), in_hbm(up_weight))

        for bits in [(1, 1)] + levels[::-1]:
            got = swap(low, bits)
            if bits == levels[0]:
                break
            half //= 2
            keep, low = call(
                fold_kernel,
                [((half, wide), F32), ((half, wide), BF16)],
                [keep, got],
                4 * half * wide,
                16 * half * wide,
            )

        grad_down = grad_down_of(weighted_t, y_all)
        grad_pair = ()
        for part in range(2):
            grad_pair = grad_pair_of(x_t, d_both, part, 2, grad_pair)
        grad_gate, grad_up = grad_pair

        grad_tokens, grad_logits = call(
            home_kernel,
            [((count, width), BF16), ((experts, count), F32)],
            [keep, got, select, base, coef],
            1 << 20,
            1 << 18,
        )
        return (
            grad_gate,
            grad_up,
            grad_down,
            grad_tokens,
            grad_logits.T,
            entropy.reshape(count),
            divergence.reshape(count),
        )

    return shards


def solution(mesh):
    in_specs = (
        P(("grp", "blk"), None),
        P(("grp", "blk"), None),
        P(None, "blk"),
        P(None, "blk"),
        P("blk", None),
        P(("grp", "blk"), None),
        P(("grp", "blk"), None),
        P(("grp", "blk"), None),
    )
    out_specs = (
        P("grp", "blk"),
        P("grp", "blk"),
        P(("grp", "blk"), None),
        P(("grp", "blk"), None),
        P(("grp", "blk"), None),
        P(("grp", "blk")),
        P(("grp", "blk")),
    )
    return jax.shard_map(
        make_shards(mesh.shape["blk"]),
        mesh=mesh,
        in_specs=in_specs,
        out_specs=out_specs,
        check_vma=False,
    )
```

```python
import functools

import jax
import jax.numpy as jnp
from jax import lax
from jax.experimental import pallas as pl
from jax.experimental.pallas import tpu as pltpu
from jax.sharding import PartitionSpec as P

F32 = jnp.float32
BF16 = jnp.bfloat16
LANES = 128
MIB = 1 << 20


def dot(left, right, dims):
    return lax.dot_general(left, right, (dims, ((), ())), preferred_element_type=F32)


def whole(count):
    return [pl.BlockSpec(memory_space=pltpu.VMEM)] * count


def call(kernel, outs, args, flops, moved, limit=8):
    return pl.pallas_call(
        kernel,
        out_shape=[jax.ShapeDtypeStruct(s, t) for s, t in outs],
        in_specs=whole(len(args)),
        out_specs=whole(len(outs)),
        compiler_params=pltpu.CompilerParams(vmem_limit_bytes=limit * MIB),
        cost_estimate=pl.CostEstimate(flops=flops, bytes_accessed=moved, transcendentals=0),
    )(*args)


def in_hbm(array):
    return pltpu.with_memory_space_constraint(array, pltpu.HBM)


def lane_pair(rows, first, second):
    lane = lax.broadcasted_iota(jnp.int32, (rows, LANES), 1)
    return jnp.where(lane == 0, first, jnp.where(lane == 1, second, 0.0))


def split_pair(value):
    high = value.astype(BF16).astype(F32)
    return lane_pair(value.shape[0], high, value - high)


def router_kernel(
    tokens_in,
    logits_in,
    ref_in,
    routes_in,
    send,
    entropy,
    divergence,
    base,
    coef,
    select_out,
    tokens,
    logits,
    ref_logits,
    routes,
    sems,
):
    sources = (logits_in, ref_in, routes_in, tokens_in)
    targets = (logits, ref_logits, routes, tokens)
    copies = [
        pltpu.make_async_copy(s, t, sems.at[i]) for i, (s, t) in enumerate(zip(sources, targets))
    ]
    for copy in copies:
        copy.start()
    for copy in copies[:3]:
        copy.wait()
    slots, width = send.shape[0], tokens.shape[1]
    experts, count = logits.shape
    x, r = logits[...], ref_logits[...]
    shifted = x - jnp.max(x, axis=0, keepdims=True)
    policy_log = shifted - jnp.log(jnp.sum(jnp.exp(shifted), axis=0, keepdims=True))
    shifted = r - jnp.max(r, axis=0, keepdims=True)
    frozen_log = shifted - jnp.log(jnp.sum(jnp.exp(shifted), axis=0, keepdims=True))
    probs = jnp.exp(policy_log)
    ratio = policy_log - frozen_log
    div = jnp.sum(probs * ratio, axis=0, keepdims=True)
    entropy[...] = -jnp.sum(probs * policy_log, axis=0, keepdims=True)
    divergence[...] = div
    base[...] = probs * (ratio - div)
    first, second = routes[0:1, :], routes[1:2, :]
    routed = jnp.where((first == 0) | (second == 0), 1.0, 0.0)
    expert = lax.broadcasted_iota(jnp.int32, (experts, count), 0)
    partner_hot = jnp.where(expert == first + second, 1.0, 0.0)
    partner_logit = jnp.sum(x * partner_hot, axis=0, keepdims=True)
    gate = jnp.where(routed > 0.0, jax.nn.sigmoid(x[0:1, :] - partner_logit), 0.0)
    coef[...] = (jnp.where(expert == 0, 1.0, 0.0) - partner_hot) * (gate * (1.0 - gate))
    token = lax.broadcasted_iota(jnp.int32, (1, count), 1)
    position = jnp.full((1, count), -1.0, F32)
    for t in range(count):
        position += jnp.where(token >= t, routed[:, t : t + 1], 0.0)
    slot = lax.broadcasted_iota(jnp.int32, (count, count), 0)
    hit = (slot == position.astype(jnp.int32)) & (routed > 0.0) & (slot < slots)
    select = jnp.where(hit, 1.0, 0.0)
    select_out[...] = select
    gate_low = gate.astype(BF16).astype(F32)
    g_slots = jnp.sum(select * gate_low, axis=1, keepdims=True)
    send[:, width:] = jnp.broadcast_to(g_slots[:slots], (slots, LANES)).astype(BF16)
    copies[3].wait()
    x_slots = dot(select.astype(BF16), tokens[...], ((1,), (0,)))
    send[:, :width] = x_slots[:slots].astype(BF16)


def back_kernel(y, down_in, back, down, sems):
    chunks, _, step = down.shape

    def copy(i):
        return pltpu.make_async_copy(down_in.at[:, pl.ds(i * step, step)], down.at[i], sems.at[i])

    for i in range(chunks):
        copy(i).start()
    for i in range(chunks):
        copy(i).wait()
        part = dot(y[:, i * step : (i + 1) * step], down[i], ((1,), (1,)))
        back[...] = part if i == 0 else back[...] + part


def expert_kernel(
    x, back, gate_in, up_in, send, keep, weighted_t, d_both, x_t, both_w, acc, sems
):
    rows, width, hidden_dim = x.shape[0], both_w.shape[0], gate_in.shape[1]
    half = rows // 2
    chunks = sems.shape[1]
    step = width // chunks

    def copy(k, i):
        at = pl.ds(i * step, step)
        source = (gate_in, up_in)[k]
        target = both_w.at[at, pl.ds(k * hidden_dim, hidden_dim)]
        return pltpu.make_async_copy(source.at[at], target, sems.at[k, i])

    for i in range(chunks):
        copy(0, i).start()
        copy(1, i).start()
    for c in range(0, width, LANES):
        x_t[c : c + LANES, :] = x[:, c : c + LANES].astype(F32).T.astype(BF16)
    for i in range(chunks):
        at = pl.ds(i * step, step)
        copy(0, i).wait()
        copy(1, i).wait()
        part = dot(x[:, at], both_w[at, :], ((1,), (0,)))
        acc[...] = part if i == 0 else acc[...] + part
    pre_gate, pre_up = acc[:, :hidden_dim], acc[:, hidden_dim:]
    g = x[:, width:][:, 0:1].astype(F32)
    sig = jax.nn.sigmoid(pre_gate)
    act = pre_gate * sig
    hidden = act * pre_up
    weighted_t[...] = (g * hidden).T.astype(BF16)
    products = jnp.sum(hidden * back[...], axis=1, keepdims=True)
    scaled = g * back[...]
    d_both[:, :hidden_dim] = (
        scaled * pre_up * sig * (1.0 + pre_gate * (1.0 - sig))
    ).astype(BF16)
    d_both[:, hidden_dim:] = (scaled * act).astype(BF16)
    keep[:, width:] = lane_pair(half, products[:half], 0.0)
    send[:, width:] = split_pair(products[half:]).astype(BF16)
    wide = 1024
    for i in range(width // wide):
        at = pl.ds(i * wide, wide)
        part = dot(d_both[...], both_w[at, :], ((1,), (1,)))
        keep[:, at] = part[:half]
        send[:, at] = part[half:].astype(BF16)


def fold_kernel(have, got, keep, send):
    half = keep.shape[0]
    width = keep.shape[1] - LANES
    total = have[:, :width] + got[:, :width].astype(F32)
    keep[:, :width] = total[:half]
    send[:, :width] = total[half:].astype(BF16)
    tail = have[:, width:] + got[:, width:].astype(F32)
    value = tail[:, 0:1] + tail[:, 1:2]
    keep[:, width:] = lane_pair(half, value[:half], 0.0)
    send[:, width:] = split_pair(value[half:]).astype(BF16)


def home_kernel(have, got, select, base, coef, grad_tokens, grad_logits):
    slots = have.shape[0]
    width = have.shape[1] - LANES
    count = select.shape[0]
    total = (have[:, :width] + got[:, :width].astype(F32)).astype(BF16)
    padded = jnp.concatenate([total, jnp.zeros((count - slots, width), BF16)], axis=0)
    grad_tokens[...] = dot(select[...].astype(BF16), padded, ((0,), (0,))).astype(BF16)
    tail = have[:, width:] + got[:, width:].astype(F32)
    value = tail[:, 0:1] + tail[:, 1:2]
    token_products = jnp.sum(select[0:slots, :] * value, axis=0, keepdims=True)
    grad_logits[...] = base[...] + coef[...] * token_products


def tiles(out, left, right):
    for c in range(0, right.shape[1], 256):
        for r in range(0, left.shape[0], 128):
            part = dot(left[r : r + 128], right[:, c : c + 256], ((1,), (0,)))
            out[r : r + 128, c : c + 256] = part.astype(BF16)


def down_kernel(weighted_t, y, out, buf, sems):
    chunks, _, step = buf.shape

    def copy(i):
        at = pl.ds(pl.multiple_of(i * step, step), step)
        return pltpu.make_async_copy(buf.at[i], out.at[:, at], sems.at[i])

    def body(i, carry):
        at = pl.ds(pl.multiple_of(i * step, step), step)
        tiles(buf.at[i], weighted_t, y.at[:, at])
        copy(i).start()
        return carry

    def finish(i, carry):
        copy(i).wait()
        return carry

    lax.fori_loop(0, chunks, body, 0)
    lax.fori_loop(0, chunks, finish, 0)


def pair_kernel(first_row, x_t, d_both, *refs):
    gate_out, up_out, gate_buf, up_buf, sems = refs[-5:]
    chunks, step, cols = gate_buf.shape

    def copy(k, i):
        at = pl.ds(pl.multiple_of(first_row + i * step, step), step)
        source, target = ((gate_buf, gate_out), (up_buf, up_out))[k]
        return pltpu.make_async_copy(source.at[i], target.at[at], sems.at[k, i])

    def body(i, carry):
        at = pl.ds(pl.multiple_of(first_row + i * step, step), step)
        tiles(gate_buf.at[i], x_t.at[at], d_both.at[:, pl.ds(0, cols)])
        copy(0, i).start()
        tiles(up_buf.at[i], x_t.at[at], d_both.at[:, pl.ds(cols, cols)])
        copy(1, i).start()
        return carry

    def finish(i, carry):
        copy(0, i).wait()
        copy(1, i).wait()
        return carry

    lax.fori_loop(0, chunks, body, 0)
    lax.fori_loop(0, chunks, finish, 0)


def grad_down_of(weighted_t, y):
    hidden, width = weighted_t.shape[0], y.shape[1]
    step = 1024
    return pl.pallas_call(
        down_kernel,
        out_shape=jax.ShapeDtypeStruct((hidden, width), BF16),
        in_specs=whole(2),
        out_specs=pl.BlockSpec(memory_space=pl.ANY),
        scratch_shapes=[
            pltpu.VMEM((width // step, hidden, step), BF16),
            pltpu.SemaphoreType.DMA((width // step,)),
        ],
        compiler_params=pltpu.CompilerParams(vmem_limit_bytes=16 * MIB),
        cost_estimate=pl.CostEstimate(
            flops=8 * weighted_t.size * width,
            bytes_accessed=2 * hidden * width,
            transcendentals=0,
        ),
    )(weighted_t, y)


def grad_pair_of(x_t, d_both, part, parts, before):
    width, cols = x_t.shape[0], d_both.shape[1] // 2
    step = 512
    rows = width // parts
    outs = [jax.ShapeDtypeStruct((width, cols), BF16)] * 2
    anywhere = pl.BlockSpec(memory_space=pl.ANY)
    return pl.pallas_call(
        functools.partial(pair_kernel, part * rows),
        out_shape=outs,
        in_specs=whole(2) + [anywhere] * len(before),
        out_specs=[anywhere] * 2,
        scratch_shapes=[
            pltpu.VMEM((rows // step, step, cols), BF16),
            pltpu.VMEM((rows // step, step, cols), BF16),
            pltpu.SemaphoreType.DMA((2, rows // step)),
        ],
        input_output_aliases={2 + i: i for i in range(len(before))},
        compiler_params=pltpu.CompilerParams(vmem_limit_bytes=16 * MIB),
        cost_estimate=pl.CostEstimate(
            flops=8 * x_t.shape[1] * rows * 2 * cols,
            bytes_accessed=4 * rows * cols,
            transcendentals=0,
        ),
    )(x_t, d_both, *before)


def make_shards(n):
    levels = []
    bit = n // 2
    while bit > 4:
        levels.append((bit, bit))
        bit //= 2
    levels += [(4, 2), (2, 4)]

    def swap(block, bits):
        return lax.ppermute(block, "blk", [(i, i ^ bits[i % 2]) for i in range(n)])

    def gather(block):
        rows = n // 2 * block.shape[0]
        block = block[None]
        for bits in levels[:-2]:
            block = lax.optimization_barrier(jnp.concatenate([block, swap(block, bits)]))
        near = swap(block, levels[-2])
        parts = [block, near, swap(block, levels[-1]), swap(near, levels[-1])]
        block = jnp.concatenate(parts).reshape(rows, block.shape[2])
        return jnp.concatenate([block, swap(block, (1, 1))])

    def shards(
        tokens, cotangent, gate_weight, up_weight, down_weight, logits, ref_logits, routes
    ):
        count, width = tokens.shape
        slots = cotangent.shape[0]
        experts = logits.shape[1]
        hidden = down_weight.shape[0]
        rows = n * slots
        wide = width + LANES
        anywhere = pl.BlockSpec(memory_space=pl.ANY)

        send, entropy, divergence, base, coef, select = pl.pallas_call(
            router_kernel,
            out_shape=[
                jax.ShapeDtypeStruct((slots, wide), BF16),
                jax.ShapeDtypeStruct((1, count), F32),
                jax.ShapeDtypeStruct((1, count), F32),
                jax.ShapeDtypeStruct((experts, count), F32),
                jax.ShapeDtypeStruct((experts, count), F32),
                jax.ShapeDtypeStruct((count, count), F32),
            ],
            in_specs=[anywhere] * 4,
            out_specs=whole(6),
            scratch_shapes=[
                pltpu.VMEM((count, width), BF16),
                pltpu.VMEM((experts, count), F32),
                pltpu.VMEM((experts, count), F32),
                pltpu.VMEM((2, count), jnp.int32),
                pltpu.SemaphoreType.DMA((4,)),
            ],
            compiler_params=pltpu.CompilerParams(vmem_limit_bytes=8 * MIB),
            cost_estimate=pl.CostEstimate(
                flops=1 << 20, bytes_accessed=1 << 18, transcendentals=0
            ),
        )(in_hbm(tokens), in_hbm(logits.T), in_hbm(ref_logits.T), in_hbm(routes.T))

        y_all = gather(cotangent)
        x_all = gather(send)

        work = 2 * rows * width * hidden
        back = pl.pallas_call(
            back_kernel,
            out_shape=jax.ShapeDtypeStruct((rows, hidden), F32),
            in_specs=whole(1) + [anywhere],
            out_specs=whole(1)[0],
            scratch_shapes=[
                pltpu.VMEM((6, hidden, width // 6), BF16),
                pltpu.SemaphoreType.DMA((6,)),
            ],
            compiler_params=pltpu.CompilerParams(vmem_limit_bytes=24 * MIB),
            cost_estimate=pl.CostEstimate(
                flops=4 * work, bytes_accessed=2 * width * hidden, transcendentals=0
            ),
        )(y_all, in_hbm(down_weight))
        half = rows // 2
        low, keep, weighted_t, d_both, x_t = pl.pallas_call(
            expert_kernel,
            out_shape=[
                jax.ShapeDtypeStruct((half, wide), BF16),
                jax.ShapeDtypeStruct((half, wide), F32),
                jax.ShapeDtypeStruct((hidden, rows), BF16),
                jax.ShapeDtypeStruct((rows, 2 * hidden), BF16),
                jax.ShapeDtypeStruct((width, rows), BF16),
            ],
            in_specs=whole(2) + [anywhere] * 2,
            out_specs=whole(5),
            scratch_shapes=[
                pltpu.VMEM((width, 2 * hidden), BF16),
                pltpu.VMEM((rows, 2 * hidden), F32),
                pltpu.SemaphoreType.DMA((2, 8)),
            ],
            compiler_params=pltpu.CompilerParams(vmem_limit_bytes=32 * MIB),
            cost_estimate=pl.CostEstimate(
                flops=16 * work, bytes_accessed=4 * width * hidden, transcendentals=0
            ),
        )(x_all, back, in_hbm(gate_weight), in_hbm(up_weight))

        for bits in [(1, 1)] + levels[::-1]:
            got = swap(low, bits)
            if bits == levels[0]:
                break
            half //= 2
            keep, low = call(
                fold_kernel,
                [((half, wide), F32), ((half, wide), BF16)],
                [keep, got],
                4 * half * wide,
                16 * half * wide,
            )

        grad_down = grad_down_of(weighted_t, y_all)
        grad_pair = ()
        for part in range(2):
            grad_pair = grad_pair_of(x_t, d_both, part, 2, grad_pair)
        grad_gate, grad_up = grad_pair

        grad_tokens, grad_logits = call(
            home_kernel,
            [((count, width), BF16), ((experts, count), F32)],
            [keep, got, select, base, coef],
            1 << 20,
            1 << 18,
        )
        return (
            grad_gate,
            grad_up,
            grad_down,
            grad_tokens,
            grad_logits.T,
            entropy.reshape(count),
            divergence.reshape(count),
        )

    return shards


def solution(mesh):
    in_specs = (
        P(("grp", "blk"), None),
        P(("grp", "blk"), None),
        P(None, "blk"),
        P(None, "blk"),
        P("blk", None),
        P(("grp", "blk"), None),
        P(("grp", "blk"), None),
        P(("grp", "blk"), None),
    )
    out_specs = (
        P("grp", "blk"),
        P("grp", "blk"),
        P(("grp", "blk"), None),
        P(("grp", "blk"), None),
        P(("grp", "blk"), None),
        P(("grp", "blk")),
        P(("grp", "blk")),
    )
    return jax.shard_map(
        make_shards(mesh.shape["blk"]),
        mesh=mesh,
        in_specs=in_specs,
        out_specs=out_specs,
        check_vma=False,
    )
```

```python
import functools

import jax
import jax.numpy as jnp
from jax import lax
from jax.experimental import pallas as pl
from jax.experimental.pallas import tpu as pltpu
from jax.sharding import PartitionSpec as P

F32 = jnp.float32
BF16 = jnp.bfloat16
LANES = 128
MIB = 1 << 20


def dot(left, right, dims):
    return lax.dot_general(left, right, (dims, ((), ())), preferred_element_type=F32)


def whole(count):
    return [pl.BlockSpec(memory_space=pltpu.VMEM)] * count


def call(kernel, outs, args, flops, moved, limit=8):
    return pl.pallas_call(
        kernel,
        out_shape=[jax.ShapeDtypeStruct(s, t) for s, t in outs],
        in_specs=whole(len(args)),
        out_specs=whole(len(outs)),
        compiler_params=pltpu.CompilerParams(vmem_limit_bytes=limit * MIB),
        cost_estimate=pl.CostEstimate(flops=flops, bytes_accessed=moved, transcendentals=0),
    )(*args)


def in_hbm(array):
    return pltpu.with_memory_space_constraint(array, pltpu.HBM)


def in_vmem(array):
    return pltpu.with_memory_space_constraint(array, pltpu.VMEM)


def lane_pair(rows, first, second):
    lane = lax.broadcasted_iota(jnp.int32, (rows, LANES), 1)
    return jnp.where(lane == 0, first, jnp.where(lane == 1, second, 0.0))


def split_pair(value):
    high = value.astype(BF16).astype(F32)
    return lane_pair(value.shape[0], high, value - high)


def router_kernel(
    tokens_in,
    logits_in,
    ref_in,
    routes_in,
    send,
    entropy,
    divergence,
    base,
    coef,
    select_out,
    tokens,
    logits,
    ref_logits,
    routes,
    sems,
):
    sources = (logits_in, ref_in, routes_in, tokens_in)
    targets = (logits, ref_logits, routes, tokens)
    copies = [
        pltpu.make_async_copy(s, t, sems.at[i]) for i, (s, t) in enumerate(zip(sources, targets))
    ]
    for copy in copies:
        copy.start()
    for copy in copies[:3]:
        copy.wait()
    slots, width = send.shape[0], tokens.shape[1]
    experts, count = logits.shape
    x, r = logits[...], ref_logits[...]
    shifted = x - jnp.max(x, axis=0, keepdims=True)
    policy_log = shifted - jnp.log(jnp.sum(jnp.exp(shifted), axis=0, keepdims=True))
    shifted = r - jnp.max(r, axis=0, keepdims=True)
    frozen_log = shifted - jnp.log(jnp.sum(jnp.exp(shifted), axis=0, keepdims=True))
    probs = jnp.exp(policy_log)
    ratio = policy_log - frozen_log
    div = jnp.sum(probs * ratio, axis=0, keepdims=True)
    entropy[...] = -jnp.sum(probs * policy_log, axis=0, keepdims=True)
    divergence[...] = div
    base[...] = probs * (ratio - div)
    first, second = routes[0:1, :], routes[1:2, :]
    routed = jnp.where((first == 0) | (second == 0), 1.0, 0.0)
    expert = lax.broadcasted_iota(jnp.int32, (experts, count), 0)
    partner_hot = jnp.where(expert == first + second, 1.0, 0.0)
    partner_logit = jnp.sum(x * partner_hot, axis=0, keepdims=True)
    gate = jnp.where(routed > 0.0, jax.nn.sigmoid(x[0:1, :] - partner_logit), 0.0)
    coef[...] = (jnp.where(expert == 0, 1.0, 0.0) - partner_hot) * (gate * (1.0 - gate))
    token = lax.broadcasted_iota(jnp.int32, (1, count), 1)
    position = jnp.full((1, count), -1.0, F32)
    for t in range(count):
        position += jnp.where(token >= t, routed[:, t : t + 1], 0.0)
    slot = lax.broadcasted_iota(jnp.int32, (count, count), 0)
    hit = (slot == position.astype(jnp.int32)) & (routed > 0.0) & (slot < slots)
    select = jnp.where(hit, 1.0, 0.0)
    select_out[...] = select
    gate_low = gate.astype(BF16).astype(F32)
    g_slots = jnp.sum(select * gate_low, axis=1, keepdims=True)
    send[:, width:] = jnp.broadcast_to(g_slots[:slots], (slots, LANES)).astype(BF16)
    copies[3].wait()
    x_slots = dot(select.astype(BF16), tokens[...], ((1,), (0,)))
    send[:, :width] = x_slots[:slots].astype(BF16)


def fetch_kernel(source, after, target, sems):
    parts = sems.shape[0]
    step = source.shape[0] // parts
    copies = [
        pltpu.make_async_copy(
            source.at[pl.ds(i * step, step)], target.at[pl.ds(i * step, step)], sems.at[i]
        )
        for i in range(parts)
    ]
    for copy in copies:
        copy.start()
    for copy in copies:
        copy.wait()


def fetch(weight, after):
    anywhere = pl.BlockSpec(memory_space=pl.ANY)
    weight_in_vmem = pl.pallas_call(
        fetch_kernel,
        out_shape=pltpu.VMEM(weight.shape, weight.dtype),
        in_specs=[anywhere] * 2,
        out_specs=pl.BlockSpec(memory_space=pltpu.VMEM),
        scratch_shapes=[pltpu.SemaphoreType.DMA((4,))],
        compiler_params=pltpu.CompilerParams(vmem_limit_bytes=8 * MIB),
        cost_estimate=pl.CostEstimate(
            flops=0, bytes_accessed=2 * weight.size, transcendentals=0
        ),
    )(in_hbm(weight), after)
    return in_vmem(weight_in_vmem)


def back_kernel(y, down, back):
    back[...] = dot(y[...], down[...], ((1,), (1,)))


def expert_kernel(
    x, back, gate_w, up_w, send, keep, weighted_t, d_both, x_t
):
    rows, width, hidden_dim = x.shape[0], gate_w.shape[0], gate_w.shape[1]
    half = rows // 2
    for c in range(0, width, LANES):
        x_t[c : c + LANES, :] = x[:, c : c + LANES].astype(F32).T.astype(BF16)
    pre_gate = dot(x[:, :width], gate_w[...], ((1,), (0,)))
    pre_up = dot(x[:, :width], up_w[...], ((1,), (0,)))
    g = x[:, width:][:, 0:1].astype(F32)
    sig = jax.nn.sigmoid(pre_gate)
    act = pre_gate * sig
    hidden = act * pre_up
    weighted_t[...] = (g * hidden).T.astype(BF16)
    products = jnp.sum(hidden * back[...], axis=1, keepdims=True)
    scaled = g * back[...]
    d_both[:, :hidden_dim] = (
        scaled * pre_up * sig * (1.0 + pre_gate * (1.0 - sig))
    ).astype(BF16)
    d_both[:, hidden_dim:] = (scaled * act).astype(BF16)
    keep[:, width:] = lane_pair(half, products[:half], 0.0)
    send[:, width:] = split_pair(products[half:]).astype(BF16)
    wide = 1024
    for i in range(width // wide):
        at = pl.ds(i * wide, wide)
        part = dot(d_both[:, :hidden_dim], gate_w[at, :], ((1,), (1,)))
        part += dot(d_both[:, hidden_dim:], up_w[at, :], ((1,), (1,)))
        keep[:, at] = part[:half]
        send[:, at] = part[half:].astype(BF16)


def fold_kernel(have, got, keep, send):
    half = keep.shape[0]
    width = keep.shape[1] - LANES
    total = have[:, :width] + got[:, :width].astype(F32)
    keep[:, :width] = total[:half]
    send[:, :width] = total[half:].astype(BF16)
    tail = have[:, width:] + got[:, width:].astype(F32)
    value = tail[:, 0:1] + tail[:, 1:2]
    keep[:, width:] = lane_pair(half, value[:half], 0.0)
    send[:, width:] = split_pair(value[half:]).astype(BF16)


def home_kernel(have, got, select, base, coef, grad_tokens, grad_logits):
    slots = have.shape[0]
    width = have.shape[1] - LANES
    count = select.shape[0]
    total = (have[:, :width] + got[:, :width].astype(F32)).astype(BF16)
    padded = jnp.concatenate([total, jnp.zeros((count - slots, width), BF16)], axis=0)
    grad_tokens[...] = dot(select[...].astype(BF16), padded, ((0,), (0,))).astype(BF16)
    tail = have[:, width:] + got[:, width:].astype(F32)
    value = tail[:, 0:1] + tail[:, 1:2]
    token_products = jnp.sum(select[0:slots, :] * value, axis=0, keepdims=True)
    grad_logits[...] = base[...] + coef[...] * token_products


def tiles(out, left, right):
    tall = 256 if left.shape[0] % 256 == 0 else 128
    for c in range(0, right.shape[1], 256):
        for r in range(0, left.shape[0], tall):
            part = dot(left[r : r + tall], right[:, c : c + 256], ((1,), (0,)))
            out[r : r + tall, c : c + 256] = part.astype(BF16)


def loop(count, body):
    def step(i, carry):
        body(i)
        return carry

    lax.fori_loop(0, count, step, 0)


def grads_kernel(first_row, x_t, d_both, *refs):
    gate_out, up_out, gate_buf, up_buf, sems = refs[-5:]
    chunks, step, cols = gate_buf.shape

    def copy(k, i):
        at = pl.ds(pl.multiple_of(first_row + i * step, step), step)
        source, target = ((gate_buf, gate_out), (up_buf, up_out))[k]
        return pltpu.make_async_copy(source.at[i], target.at[at], sems.at[k, i])

    def body(i):
        at = pl.ds(pl.multiple_of(first_row + i * step, step), step)
        tiles(gate_buf.at[i], x_t.at[at], d_both.at[:, pl.ds(0, cols)])
        copy(0, i).start()
        tiles(up_buf.at[i], x_t.at[at], d_both.at[:, pl.ds(cols, cols)])
        copy(1, i).start()

    def finish(i):
        copy(0, i).wait()
        copy(1, i).wait()

    loop(chunks, body)
    loop(chunks, finish)


def first_kernel(weighted_t, y, x_t, d_both, down_out, gate_out, up_out, *scratch):
    down_buf, down_sems = scratch[:2]
    chunks, _, step = down_buf.shape

    def copy(i):
        at = pl.ds(pl.multiple_of(i * step, step), step)
        return pltpu.make_async_copy(down_buf.at[i], down_out.at[:, at], down_sems.at[i])

    def body(i):
        at = pl.ds(pl.multiple_of(i * step, step), step)
        tiles(down_buf.at[i], weighted_t, y.at[:, at])
        copy(i).start()

    loop(chunks, body)
    grads_kernel(0, x_t, d_both, gate_out, up_out, *scratch[2:])
    loop(chunks, lambda i: copy(i).wait())


def grads_of(x_t, d_both, first_row, rows, before, down=()):
    width, slots = x_t.shape
    cols = d_both.shape[1] // 2
    step = 256
    outs = [jax.ShapeDtypeStruct((width, cols), BF16)] * 2
    scratch = [
        pltpu.VMEM((rows // step, step, cols), BF16),
        pltpu.VMEM((rows // step, step, cols), BF16),
        pltpu.SemaphoreType.DMA((2, rows // step)),
    ]
    kernel = functools.partial(grads_kernel, first_row)
    if down:
        kernel = first_kernel
        wide = 1024
        outs = [jax.ShapeDtypeStruct((cols, width), BF16)] + outs
        scratch = [
            pltpu.VMEM((width // wide, cols, wide), BF16),
            pltpu.SemaphoreType.DMA((width // wide,)),
        ] + scratch
    anywhere = pl.BlockSpec(memory_space=pl.ANY)
    elements = 2 * rows * cols + (width * cols if down else 0)
    return pl.pallas_call(
        kernel,
        out_shape=outs,
        in_specs=whole(2 + len(down)) + [anywhere] * len(before),
        out_specs=[anywhere] * len(outs),
        scratch_shapes=scratch,
        input_output_aliases={2 + i: i for i in range(len(before))},
        compiler_params=pltpu.CompilerParams(vmem_limit_bytes=20 * MIB),
        cost_estimate=pl.CostEstimate(
            flops=8 * slots * elements, bytes_accessed=2 * elements, transcendentals=0
        ),
    )(*down, x_t, d_both, *before)


def make_shards(n):
    levels = []
    bit = n // 2
    while bit > 4:
        levels.append((bit, bit))
        bit //= 2
    levels += [(4, 2), (2, 4)]

    def swap(block, bits):
        return lax.ppermute(block, "blk", [(i, i ^ bits[i % 2]) for i in range(n)])

    def join(parts):
        block = jnp.concatenate(parts)
        block = block.reshape(block.shape[0] * block.shape[1], block.shape[2])
        return jnp.concatenate([block, swap(block, (1, 1))])

    def shards(
        tokens, cotangent, gate_weight, up_weight, down_weight, logits, ref_logits, routes
    ):
        count, width = tokens.shape
        slots = cotangent.shape[0]
        experts = logits.shape[1]
        hidden = down_weight.shape[0]
        rows = n * slots
        wide = width + LANES
        anywhere = pl.BlockSpec(memory_space=pl.ANY)

        send, entropy, divergence, base, coef, select = pl.pallas_call(
            router_kernel,
            out_shape=[
                jax.ShapeDtypeStruct((slots, wide), BF16),
                jax.ShapeDtypeStruct((1, count), F32),
                jax.ShapeDtypeStruct((1, count), F32),
                jax.ShapeDtypeStruct((experts, count), F32),
                jax.ShapeDtypeStruct((experts, count), F32),
                jax.ShapeDtypeStruct((count, count), F32),
            ],
            in_specs=[anywhere] * 4,
            out_specs=whole(6),
            scratch_shapes=[
                pltpu.VMEM((count, width), BF16),
                pltpu.VMEM((experts, count), F32),
                pltpu.VMEM((experts, count), F32),
                pltpu.VMEM((2, count), jnp.int32),
                pltpu.SemaphoreType.DMA((4,)),
            ],
            compiler_params=pltpu.CompilerParams(vmem_limit_bytes=8 * MIB),
            cost_estimate=pl.CostEstimate(
                flops=1 << 20, bytes_accessed=1 << 18, transcendentals=0
            ),
        )(in_hbm(tokens), in_hbm(logits.T), in_hbm(ref_logits.T), in_hbm(routes.T))

        x_own, y_own = send[None], cotangent[None]
        y_own = jnp.concatenate([y_own, swap(y_own, levels[0])])
        x_own = jnp.concatenate([x_own, swap(x_own, levels[0])])
        own = jnp.concatenate([x_own, y_own], axis=2)
        for bits in levels[1:-2]:
            own = jnp.concatenate([own, swap(own, bits)])
        own = lax.optimization_barrier(own)
        near = swap(own, levels[-2])
        far = swap(own, levels[-1])
        down_w = fetch(down_weight, send)
        gate_w = fetch(gate_weight, own)
        up_w = fetch(up_weight, near)
        y_all = join(
            [own[..., wide:], near[..., wide:], far[..., wide:], swap(near[..., wide:], levels[-1])]
        )
        x_all = join(
            [own[..., :wide], near[..., :wide], far[..., :wide], swap(near[..., :wide], levels[-1])]
        )

        work = 2 * rows * width * hidden
        back = pl.pallas_call(
            back_kernel,
            out_shape=jax.ShapeDtypeStruct((rows, hidden), F32),
            in_specs=whole(2),
            out_specs=whole(1)[0],
            compiler_params=pltpu.CompilerParams(vmem_limit_bytes=8 * MIB),
            cost_estimate=pl.CostEstimate(
                flops=4 * work, bytes_accessed=2 * width * hidden, transcendentals=0
            ),
        )(y_all, down_w)
        half = rows // 2
        low, keep, weighted_t, d_both, x_t = pl.pallas_call(
            expert_kernel,
            out_shape=[
                jax.ShapeDtypeStruct((half, wide), BF16),
                jax.ShapeDtypeStruct((half, wide), F32),
                jax.ShapeDtypeStruct((hidden, rows), BF16),
                jax.ShapeDtypeStruct((rows, 2 * hidden), BF16),
                jax.ShapeDtypeStruct((width, rows), BF16),
            ],
            in_specs=whole(4),
            out_specs=whole(5),
            compiler_params=pltpu.CompilerParams(vmem_limit_bytes=8 * MIB),
            cost_estimate=pl.CostEstimate(
                flops=16 * work, bytes_accessed=4 * width * hidden, transcendentals=0
            ),
        )(x_all, back, gate_w, up_w)

        for bits in [(1, 1)] + levels[::-1]:
            got = swap(low, bits)
            if bits == levels[0]:
                break
            half //= 2
            keep, low = call(
                fold_kernel,
                [((half, wide), F32), ((half, wide), BF16)],
                [keep, got],
                4 * half * wide,
                16 * half * wide,
            )

        cuts = (0, width // 4, width * 5 // 8, width)
        grad_down, *pair = grads_of(x_t, d_both, 0, cuts[1], (), (weighted_t, y_all))
        for start, stop in zip(cuts[1:], cuts[2:]):
            pair = grads_of(x_t, d_both, start, stop - start, tuple(pair))
        grad_gate, grad_up = pair

        grad_tokens, grad_logits = call(
            home_kernel,
            [((count, width), BF16), ((experts, count), F32)],
            [keep, got, select, base, coef],
            1 << 20,
            1 << 18,
        )
        return (
            grad_gate,
            grad_up,
            grad_down,
            grad_tokens,
            grad_logits.T,
            entropy.reshape(count),
            divergence.reshape(count),
        )

    return shards


def solution(mesh):
    in_specs = (
        P(("grp", "blk"), None),
        P(("grp", "blk"), None),
        P(None, "blk"),
        P(None, "blk"),
        P("blk", None),
        P(("grp", "blk"), None),
        P(("grp", "blk"), None),
        P(("grp", "blk"), None),
    )
    out_specs = (
        P("grp", "blk"),
        P("grp", "blk"),
        P(("grp", "blk"), None),
        P(("grp", "blk"), None),
        P(("grp", "blk"), None),
        P(("grp", "blk")),
        P(("grp", "blk")),
    )
    return jax.shard_map(
        make_shards(mesh.shape["blk"]),
        mesh=mesh,
        in_specs=in_specs,
        out_specs=out_specs,
        check_vma=False,
    )
```

```python
import functools

import jax
import jax.numpy as jnp
from jax import lax
from jax.experimental import pallas as pl
from jax.experimental.pallas import tpu as pltpu
from jax.sharding import PartitionSpec as P

F32 = jnp.float32
BF16 = jnp.bfloat16
LANES = 128
MIB = 1 << 20


def dot(left, right, dims):
    return lax.dot_general(left, right, (dims, ((), ())), preferred_element_type=F32)


def whole(count):
    return [pl.BlockSpec(memory_space=pltpu.VMEM)] * count


def call(kernel, outs, args, flops, moved, limit=8):
    return pl.pallas_call(
        kernel,
        out_shape=[jax.ShapeDtypeStruct(s, t) for s, t in outs],
        in_specs=whole(len(args)),
        out_specs=whole(len(outs)),
        compiler_params=pltpu.CompilerParams(vmem_limit_bytes=limit * MIB),
        cost_estimate=pl.CostEstimate(flops=flops, bytes_accessed=moved, transcendentals=0),
    )(*args)


def in_hbm(array):
    return pltpu.with_memory_space_constraint(array, pltpu.HBM)


def in_vmem(array):
    return pltpu.with_memory_space_constraint(array, pltpu.VMEM)


def lane_pair(rows, first, second):
    lane = lax.broadcasted_iota(jnp.int32, (rows, LANES), 1)
    return jnp.where(lane == 0, first, jnp.where(lane == 1, second, 0.0))


def split_pair(value):
    high = value.astype(BF16).astype(F32)
    return lane_pair(value.shape[0], high, value - high)


def router_kernel(
    tokens_in,
    logits_in,
    ref_in,
    routes_in,
    send,
    entropy,
    divergence,
    base,
    coef,
    select_out,
    tokens,
    logits,
    ref_logits,
    routes,
    sems,
):
    sources = (logits_in, ref_in, routes_in, tokens_in)
    targets = (logits, ref_logits, routes, tokens)
    copies = [
        pltpu.make_async_copy(s, t, sems.at[i]) for i, (s, t) in enumerate(zip(sources, targets))
    ]
    for copy in copies:
        copy.start()
    for copy in copies[:3]:
        copy.wait()
    slots, width = send.shape[0], tokens.shape[1]
    experts, count = logits.shape
    x, r = logits[...], ref_logits[...]
    shifted = x - jnp.max(x, axis=0, keepdims=True)
    policy_log = shifted - jnp.log(jnp.sum(jnp.exp(shifted), axis=0, keepdims=True))
    shifted = r - jnp.max(r, axis=0, keepdims=True)
    frozen_log = shifted - jnp.log(jnp.sum(jnp.exp(shifted), axis=0, keepdims=True))
    probs = jnp.exp(policy_log)
    ratio = policy_log - frozen_log
    div = jnp.sum(probs * ratio, axis=0, keepdims=True)
    entropy[...] = -jnp.sum(probs * policy_log, axis=0, keepdims=True)
    divergence[...] = div
    base[...] = probs * (ratio - div)
    first, second = routes[0:1, :], routes[1:2, :]
    routed = jnp.where((first == 0) | (second == 0), 1.0, 0.0)
    expert = lax.broadcasted_iota(jnp.int32, (experts, count), 0)
    partner_hot = jnp.where(expert == first + second, 1.0, 0.0)
    partner_logit = jnp.sum(x * partner_hot, axis=0, keepdims=True)
    gate = jnp.where(routed > 0.0, jax.nn.sigmoid(x[0:1, :] - partner_logit), 0.0)
    coef[...] = (jnp.where(expert == 0, 1.0, 0.0) - partner_hot) * (gate * (1.0 - gate))
    token = lax.broadcasted_iota(jnp.int32, (1, count), 1)
    position = jnp.full((1, count), -1.0, F32)
    for t in range(count):
        position += jnp.where(token >= t, routed[:, t : t + 1], 0.0)
    slot = lax.broadcasted_iota(jnp.int32, (count, count), 0)
    hit = (slot == position.astype(jnp.int32)) & (routed > 0.0) & (slot < slots)
    select = jnp.where(hit, 1.0, 0.0)
    select_out[...] = select
    gate_low = gate.astype(BF16).astype(F32)
    g_slots = jnp.sum(select * gate_low, axis=1, keepdims=True)
    send[:, width:] = jnp.broadcast_to(g_slots[:slots], (slots, LANES)).astype(BF16)
    copies[3].wait()
    x_slots = dot(select.astype(BF16), tokens[...], ((1,), (0,)))
    send[:, :width] = x_slots[:slots].astype(BF16)


def fetch_copies(sources, targets, sems):
    parts = sems.shape[1]
    copies = []
    for k, (source, target) in enumerate(zip(sources, targets)):
        step = source.shape[0] // parts
        for i in range(parts):
            at = pl.ds(i * step, step)
            copies.append(pltpu.make_async_copy(source.at[at], target.at[at], sems.at[k, i]))
    return copies


def fetch_kernel(count, has_block, *refs):
    sources, refs = refs[:count], refs[count + 1 :]
    if has_block:
        block, refs = refs[0], refs[1:]
    targets, refs = refs[:count], refs[count:]
    copies = fetch_copies(sources, targets, refs[-1])
    for copy in copies:
        copy.start()
    if has_block:
        refs[0][...] = block[...]
    for copy in copies:
        copy.wait()


def fetch(weights, after, block=None):
    anywhere = pl.BlockSpec(memory_space=pl.ANY)
    count, blocks = len(weights), [] if block is None else [block]
    out = pl.pallas_call(
        functools.partial(fetch_kernel, count, bool(blocks)),
        out_shape=[pltpu.VMEM(w.shape, w.dtype) for w in weights]
        + [jax.ShapeDtypeStruct(b.shape, b.dtype) for b in blocks],
        in_specs=[anywhere] * (count + 1) + whole(len(blocks)),
        out_specs=whole(count + len(blocks)),
        scratch_shapes=[pltpu.SemaphoreType.DMA((count, 4))],
        compiler_params=pltpu.CompilerParams(vmem_limit_bytes=8 * MIB),
        cost_estimate=pl.CostEstimate(
            flops=0, bytes_accessed=2 * sum(w.size for w in weights), transcendentals=0
        ),
    )(*[in_hbm(w) for w in weights], after, *blocks)
    return [in_vmem(w) for w in out[:count]] + list(out[count:])


def split_kernel(block, after, left, right):
    left[...] = block[:, : left.shape[1]]
    right[...] = block[:, left.shape[1] :]


def join_kernel(own, near, far, last_x, last_y, out_x, out_y):
    wide = out_x.shape[1]
    for out, last, first in ((out_x, last_x, 0), (out_y, last_y, wide)):
        cols = out.shape[1]
        parts = [ref[:, first : first + cols] for ref in (own, near, far)] + [last[...]]
        out[...] = jnp.concatenate([part.astype(F32) for part in parts]).astype(BF16)


def back_kernel(y, down, back):
    back[...] = dot(y[...], down[...], ((1,), (1,)))


def expert_kernel(
    x, back, gate_w, up_w, send, keep, weighted_t, d_both, x_t
):
    rows, width, hidden_dim = x.shape[0], gate_w.shape[0], gate_w.shape[1]
    half = rows // 2
    for c in range(0, width, LANES):
        x_t[c : c + LANES, :] = x[:, c : c + LANES].astype(F32).T.astype(BF16)
    pre_gate = dot(x[:, :width], gate_w[...], ((1,), (0,)))
    pre_up = dot(x[:, :width], up_w[...], ((1,), (0,)))
    g = x[:, width:][:, 0:1].astype(F32)
    sig = jax.nn.sigmoid(pre_gate)
    act = pre_gate * sig
    hidden = act * pre_up
    weighted_t[...] = (g * hidden).T.astype(BF16)
    products = jnp.sum(hidden * back[...], axis=1, keepdims=True)
    scaled = g * back[...]
    d_both[:, :hidden_dim] = (
        scaled * pre_up * sig * (1.0 + pre_gate * (1.0 - sig))
    ).astype(BF16)
    d_both[:, hidden_dim:] = (scaled * act).astype(BF16)
    keep[:, width:] = lane_pair(half, products[:half], 0.0)
    send[:, width:] = split_pair(products[half:]).astype(BF16)
    wide = 1024
    for i in range(width // wide):
        at = pl.ds(i * wide, wide)
        part = dot(d_both[:, :hidden_dim], gate_w[at, :], ((1,), (1,)))
        part += dot(d_both[:, hidden_dim:], up_w[at, :], ((1,), (1,)))
        keep[:, at] = part[:half]
        send[:, at] = part[half:].astype(BF16)


def fold_kernel(have, got, keep, send):
    half = keep.shape[0]
    width = keep.shape[1] - LANES
    total = have[:, :width] + got[:, :width].astype(F32)
    keep[:, :width] = total[:half]
    send[:, :width] = total[half:].astype(BF16)
    tail = have[:, width:] + got[:, width:].astype(F32)
    value = tail[:, 0:1] + tail[:, 1:2]
    keep[:, width:] = lane_pair(half, value[:half], 0.0)
    send[:, width:] = split_pair(value[half:]).astype(BF16)


def home_kernel(have, got, select, base, coef, grad_tokens, grad_logits):
    slots = have.shape[0]
    width = have.shape[1] - LANES
    count = select.shape[0]
    total = (have[:, :width] + got[:, :width].astype(F32)).astype(BF16)
    padded = jnp.concatenate([total, jnp.zeros((count - slots, width), BF16)], axis=0)
    grad_tokens[...] = dot(select[...].astype(BF16), padded, ((0,), (0,))).astype(BF16)
    tail = have[:, width:] + got[:, width:].astype(F32)
    value = tail[:, 0:1] + tail[:, 1:2]
    token_products = jnp.sum(select[0:slots, :] * value, axis=0, keepdims=True)
    grad_logits[...] = base[...] + coef[...] * token_products


def tiles(out, left, right):
    tall = 128
    for c in range(0, right.shape[1], 256):
        for r in range(0, left.shape[0], tall):
            part = dot(left[r : r + tall], right[:, c : c + 256], ((1,), (0,)))
            out[r : r + tall, c : c + 256] = part.astype(BF16)


def loop(count, body):
    for i in range(count):
        body(i)


def grads_kernel(first_row, x_t, d_both, *refs):
    gate_out, up_out, gate_buf, up_buf, sems = refs[-5:]
    chunks, step, cols = gate_buf.shape

    def copy(k, i):
        at = pl.ds(first_row + i * step, step)
        source, target = ((gate_buf, gate_out), (up_buf, up_out))[k]
        return pltpu.make_async_copy(source.at[i], target.at[at], sems.at[k, i])

    def body(i):
        at = pl.ds(first_row + i * step, step)
        tiles(gate_buf.at[i], x_t.at[at], d_both.at[:, pl.ds(0, cols)])
        copy(0, i).start()
        tiles(up_buf.at[i], x_t.at[at], d_both.at[:, pl.ds(cols, cols)])
        copy(1, i).start()

    def finish(i):
        copy(0, i).wait()
        copy(1, i).wait()

    loop(chunks, body)
    loop(chunks, finish)


def first_kernel(weighted_t, y, x_t, d_both, down_out, gate_out, up_out, *scratch):
    down_buf, down_sems = scratch[:2]
    chunks, _, step = down_buf.shape

    def copy(i):
        at = pl.ds(i * step, step)
        return pltpu.make_async_copy(down_buf.at[i], down_out.at[:, at], down_sems.at[i])

    def body(i):
        at = pl.ds(i * step, step)
        tiles(down_buf.at[i], weighted_t, y.at[:, at])
        copy(i).start()

    loop(chunks, body)
    grads_kernel(0, x_t, d_both, gate_out, up_out, *scratch[2:])
    loop(chunks, lambda i: copy(i).wait())


def grads_of(x_t, d_both, first_row, rows, before, down=()):
    width, slots = x_t.shape
    cols = d_both.shape[1] // 2
    step = 256
    outs = [jax.ShapeDtypeStruct((width, cols), BF16)] * 2
    scratch = [
        pltpu.VMEM((rows // step, step, cols), BF16),
        pltpu.VMEM((rows // step, step, cols), BF16),
        pltpu.SemaphoreType.DMA((2, rows // step)),
    ]
    kernel = functools.partial(grads_kernel, first_row)
    if down:
        kernel = first_kernel
        wide = 1024
        outs = [jax.ShapeDtypeStruct((cols, width), BF16)] + outs
        scratch = [
            pltpu.VMEM((width // wide, cols, wide), BF16),
            pltpu.SemaphoreType.DMA((width // wide,)),
        ] + scratch
    anywhere = pl.BlockSpec(memory_space=pl.ANY)
    elements = 2 * rows * cols + (width * cols if down else 0)
    return pl.pallas_call(
        kernel,
        out_shape=outs,
        in_specs=whole(2 + len(down)) + [anywhere] * len(before),
        out_specs=[anywhere] * len(outs),
        scratch_shapes=scratch,
        input_output_aliases={2 + i: i for i in range(len(before))},
        compiler_params=pltpu.CompilerParams(vmem_limit_bytes=20 * MIB),
        cost_estimate=pl.CostEstimate(
            flops=8 * slots * elements, bytes_accessed=2 * elements, transcendentals=0
        ),
    )(*down, x_t, d_both, *before)


def make_shards(n):
    levels = []
    bit = n // 2
    while bit > 4:
        levels.append((bit, bit))
        bit //= 2
    levels += [(4, 2), (2, 4)]

    def swap(block, bits):
        return lax.ppermute(block, "blk", [(i, i ^ bits[i % 2]) for i in range(n)])

    def shards(
        tokens, cotangent, gate_weight, up_weight, down_weight, logits, ref_logits, routes
    ):
        count, width = tokens.shape
        slots = cotangent.shape[0]
        experts = logits.shape[1]
        hidden = down_weight.shape[0]
        rows = n * slots
        wide = width + LANES
        anywhere = pl.BlockSpec(memory_space=pl.ANY)

        send, entropy, divergence, base, coef, select = pl.pallas_call(
            router_kernel,
            out_shape=[
                jax.ShapeDtypeStruct((slots, wide), BF16),
                jax.ShapeDtypeStruct((1, count), F32),
                jax.ShapeDtypeStruct((1, count), F32),
                jax.ShapeDtypeStruct((experts, count), F32),
                jax.ShapeDtypeStruct((experts, count), F32),
                jax.ShapeDtypeStruct((count, count), F32),
            ],
            in_specs=[anywhere] * 4,
            out_specs=whole(6),
            scratch_shapes=[
                pltpu.VMEM((count, width), BF16),
                pltpu.VMEM((experts, count), F32),
                pltpu.VMEM((experts, count), F32),
                pltpu.VMEM((2, count), jnp.int32),
                pltpu.SemaphoreType.DMA((4,)),
            ],
            compiler_params=pltpu.CompilerParams(vmem_limit_bytes=8 * MIB),
            cost_estimate=pl.CostEstimate(
                flops=1 << 20, bytes_accessed=1 << 24, transcendentals=0
            ),
        )(in_hbm(tokens), in_hbm(logits.T), in_hbm(ref_logits.T), in_hbm(routes.T))

        y_got = swap(cotangent, levels[0])
        x_got = swap(send, levels[0])
        gate_w, y_own = fetch([gate_weight], send, cotangent)
        own = jnp.concatenate(
            [jnp.concatenate([send, y_own], axis=1), jnp.concatenate([x_got, y_got], axis=1)]
        )
        for bits in levels[1:-2]:
            own = jnp.concatenate([own, swap(own, bits)])
        near = swap(own, levels[-2])
        far = swap(own, levels[-1])
        up_w, down_w = fetch([up_weight, down_weight], own)
        few = own.shape[0]
        near_x, near_y = pl.pallas_call(
            split_kernel,
            out_shape=[
                jax.ShapeDtypeStruct((few, wide), BF16),
                jax.ShapeDtypeStruct((few, width), BF16),
            ],
            in_specs=whole(1) + [anywhere],
            out_specs=whole(2),
            compiler_params=pltpu.CompilerParams(vmem_limit_bytes=8 * MIB),
            cost_estimate=pl.CostEstimate(
                flops=0, bytes_accessed=1 << 18, transcendentals=0
            ),
        )(near, up_w)

        last_y = swap(near_y, levels[-1])
        last_x = swap(near_x, levels[-1])
        x_half, y_half = call(
            join_kernel,
            [((rows // 2, wide), BF16), ((rows // 2, width), BF16)],
            [own, near, far, last_x, last_y],
            0,
            1 << 18,
        )
        y_all = jnp.concatenate([y_half, swap(y_half, (1, 1))])
        x_all = jnp.concatenate([x_half, swap(x_half, (1, 1))])

        work = 2 * rows * width * hidden
        back = pl.pallas_call(
            back_kernel,
            out_shape=jax.ShapeDtypeStruct((rows, hidden), F32),
            in_specs=whole(2),
            out_specs=whole(1)[0],
            compiler_params=pltpu.CompilerParams(vmem_limit_bytes=8 * MIB),
            cost_estimate=pl.CostEstimate(
                flops=4 * work, bytes_accessed=2 * width * hidden, transcendentals=0
            ),
        )(y_all, down_w)
        half = rows // 2
        low, keep, weighted_t, d_both, x_t = pl.pallas_call(
            expert_kernel,
            out_shape=[
                jax.ShapeDtypeStruct((half, wide), BF16),
                jax.ShapeDtypeStruct((half, wide), F32),
                jax.ShapeDtypeStruct((hidden, rows), BF16),
                jax.ShapeDtypeStruct((rows, 2 * hidden), BF16),
                jax.ShapeDtypeStruct((width, rows), BF16),
            ],
            in_specs=whole(4),
            out_specs=whole(5),
            compiler_params=pltpu.CompilerParams(vmem_limit_bytes=8 * MIB),
            cost_estimate=pl.CostEstimate(
                flops=16 * work, bytes_accessed=4 * width * hidden, transcendentals=0
            ),
        )(x_all, back, gate_w, up_w)

        for bits in [(1, 1)] + levels[::-1]:
            got = swap(low, bits)
            if bits == levels[0]:
                break
            half //= 2
            keep, low = call(
                fold_kernel,
                [((half, wide), F32), ((half, wide), BF16)],
                [keep, got],
                4 * half * wide,
                16 * half * wide,
            )

        cuts = (0, width // 4, width * 5 // 8, width)
        grad_down, *pair = grads_of(x_t, d_both, 0, cuts[1], (), (weighted_t, y_all))
        for start, stop in zip(cuts[1:], cuts[2:]):
            pair = grads_of(x_t, d_both, start, stop - start, tuple(pair))
        grad_gate, grad_up = pair

        grad_tokens, grad_logits = call(
            home_kernel,
            [((count, width), BF16), ((experts, count), F32)],
            [keep, got, select, base, coef],
            1 << 20,
            1 << 18,
        )
        return (
            grad_gate,
            grad_up,
            grad_down,
            grad_tokens,
            grad_logits.T,
            entropy.reshape(count),
            divergence.reshape(count),
        )

    return shards


def solution(mesh):
    in_specs = (
        P(("grp", "blk"), None),
        P(("grp", "blk"), None),
        P(None, "blk"),
        P(None, "blk"),
        P("blk", None),
        P(("grp", "blk"), None),
        P(("grp", "blk"), None),
        P(("grp", "blk"), None),
    )
    out_specs = (
        P("grp", "blk"),
        P("grp", "blk"),
        P(("grp", "blk"), None),
        P(("grp", "blk"), None),
        P(("grp", "blk"), None),
        P(("grp", "blk")),
        P(("grp", "blk")),
    )
    return jax.shard_map(
        make_shards(mesh.shape["blk"]),
        mesh=mesh,
        in_specs=in_specs,
        out_specs=out_specs,
        check_vma=False,
    )
```

```python
import functools

import jax
import jax.numpy as jnp
from jax import lax
from jax.experimental import pallas as pl
from jax.experimental.pallas import tpu as pltpu
from jax.sharding import PartitionSpec as P

F32 = jnp.float32
BF16 = jnp.bfloat16
LANES = 128
MIB = 1 << 20


def dot(left, right, dims):
    return lax.dot_general(left, right, (dims, ((), ())), preferred_element_type=F32)


def whole(count):
    return [pl.BlockSpec(memory_space=pltpu.VMEM)] * count


def call(kernel, outs, args, flops, moved, limit=8):
    return pl.pallas_call(
        kernel,
        out_shape=[jax.ShapeDtypeStruct(s, t) for s, t in outs],
        in_specs=whole(len(args)),
        out_specs=whole(len(outs)),
        compiler_params=pltpu.CompilerParams(vmem_limit_bytes=limit * MIB),
        cost_estimate=pl.CostEstimate(flops=flops, bytes_accessed=moved, transcendentals=0),
    )(*args)


def in_hbm(array):
    return pltpu.with_memory_space_constraint(array, pltpu.HBM)


def in_vmem(array):
    return pltpu.with_memory_space_constraint(array, pltpu.VMEM)


def lane_pair(rows, first, second):
    lane = lax.broadcasted_iota(jnp.int32, (rows, LANES), 1)
    return jnp.where(lane == 0, first, jnp.where(lane == 1, second, 0.0))


def split_pair(value):
    high = value.astype(BF16).astype(F32)
    return lane_pair(value.shape[0], high, value - high)


def router_kernel(
    tokens_in,
    logits_in,
    ref_in,
    routes_in,
    y_in,
    send,
    entropy,
    divergence,
    base,
    coef,
    select_out,
    tokens,
    logits,
    ref_logits,
    routes,
    y,
    sems,
):
    sources = (logits_in, ref_in, routes_in, tokens_in, y_in)
    targets = (logits, ref_logits, routes, tokens, y)
    copies = [
        pltpu.make_async_copy(s, t, sems.at[i]) for i, (s, t) in enumerate(zip(sources, targets))
    ]
    for copy in copies:
        copy.start()
    for copy in copies[:3]:
        copy.wait()
    slots, width = send.shape[0], tokens.shape[1]
    experts, count = logits.shape
    x, r = logits[...], ref_logits[...]
    shifted = x - jnp.max(x, axis=0, keepdims=True)
    policy_log = shifted - jnp.log(jnp.sum(jnp.exp(shifted), axis=0, keepdims=True))
    shifted = r - jnp.max(r, axis=0, keepdims=True)
    frozen_log = shifted - jnp.log(jnp.sum(jnp.exp(shifted), axis=0, keepdims=True))
    probs = jnp.exp(policy_log)
    ratio = policy_log - frozen_log
    div = jnp.sum(probs * ratio, axis=0, keepdims=True)
    entropy[...] = -jnp.sum(probs * policy_log, axis=0, keepdims=True)
    divergence[...] = div
    base[...] = probs * (ratio - div)
    first, second = routes[0:1, :], routes[1:2, :]
    routed = jnp.where((first == 0) | (second == 0), 1.0, 0.0)
    expert = lax.broadcasted_iota(jnp.int32, (experts, count), 0)
    partner_hot = jnp.where(expert == first + second, 1.0, 0.0)
    partner_logit = jnp.sum(x * partner_hot, axis=0, keepdims=True)
    gate = jnp.where(routed > 0.0, jax.nn.sigmoid(x[0:1, :] - partner_logit), 0.0)
    coef[...] = (jnp.where(expert == 0, 1.0, 0.0) - partner_hot) * (gate * (1.0 - gate))
    token = lax.broadcasted_iota(jnp.int32, (1, count), 1)
    position = jnp.full((1, count), -1.0, F32)
    for t in range(count):
        position += jnp.where(token >= t, routed[:, t : t + 1], 0.0)
    slot = lax.broadcasted_iota(jnp.int32, (count, count), 0)
    hit = (slot == position.astype(jnp.int32)) & (routed > 0.0) & (slot < slots)
    select = jnp.where(hit, 1.0, 0.0)
    select_out[...] = select
    gate_low = gate.astype(BF16).astype(F32)
    g_slots = jnp.sum(select * gate_low, axis=1, keepdims=True)
    wide = width + LANES
    send[:, width:wide] = jnp.broadcast_to(g_slots[:slots], (slots, LANES)).astype(BF16)
    copies[3].wait()
    x_slots = dot(select.astype(BF16), tokens[...], ((1,), (0,)))
    send[:, :width] = x_slots[:slots].astype(BF16)
    copies[4].wait()
    send[:, wide:] = y[...]


def fetch_copies(sources, targets, sems):
    parts = sems.shape[1]
    copies = []
    for k, (source, target) in enumerate(zip(sources, targets)):
        step = source.shape[0] // parts
        for i in range(parts):
            at = pl.ds(i * step, step)
            copies.append(pltpu.make_async_copy(source.at[at], target.at[at], sems.at[k, i]))
    return copies


def fetch_kernel(count, *refs):
    sources, block, refs = refs[:count], refs[count], refs[count + 1 :]
    targets, out, sems = refs[:count], refs[count], refs[count + 1]
    copies = fetch_copies(sources, targets, sems)
    for copy in copies:
        copy.start()
    out[...] = block[...]
    for copy in copies:
        copy.wait()


def fetch(weights, block):
    count = len(weights)
    out = pl.pallas_call(
        functools.partial(fetch_kernel, count),
        out_shape=[pltpu.VMEM(w.shape, w.dtype) for w in weights]
        + [jax.ShapeDtypeStruct(block.shape, block.dtype)],
        in_specs=[pl.BlockSpec(memory_space=pl.ANY)] * count + whole(1),
        out_specs=whole(count + 1),
        scratch_shapes=[pltpu.SemaphoreType.DMA((count, 4))],
        compiler_params=pltpu.CompilerParams(vmem_limit_bytes=8 * MIB),
        cost_estimate=pl.CostEstimate(
            flops=0, bytes_accessed=2 * sum(w.size for w in weights), transcendentals=0
        ),
    )(*[in_hbm(w) for w in weights], block)
    return [in_vmem(w) for w in out[:count]] + [out[count]]


def join_kernel(own, near, far, most):
    parts = [ref[...].astype(F32) for ref in (own, near, far)]
    most[...] = jnp.concatenate(parts).astype(BF16)


def split_kernel(near, far, near_x, far_y):
    near_x[...] = near[:, : near_x.shape[1]]
    far_y[...] = far[:, near_x.shape[1] :]


def expert_kernel(*refs):
    pieces, (down_w, gate_w, up_w), refs = refs[:6], refs[6:9], refs[9:]
    send, keep, weighted_t, d_both, x_t, y, x = refs
    rows, width, hidden_dim = x.shape[0], gate_w.shape[0], gate_w.shape[1]
    wide = width + LANES
    half = rows // 2
    own, last_x, last_y, other, other_x, other_y = pieces
    for c in range(0, wide, LANES):
        at = pl.ds(c, LANES)
        parts = [ref[:, at].astype(F32) for ref in (own, last_x, other, other_x)]
        block = jnp.concatenate(parts)
        x[:, at] = block.astype(BF16)
        if c < width:
            x_t[at, :] = block.T.astype(BF16)
    for c in range(0, width, LANES):
        at, from_wide = pl.ds(c, LANES), pl.ds(wide + c, LANES)
        parts = [own[:, from_wide], last_y[:, at], other[:, from_wide], other_y[:, at]]
        y[:, at] = jnp.concatenate([part.astype(F32) for part in parts]).astype(BF16)
    pre_gate = dot(x[:, :width], gate_w[...], ((1,), (0,)))
    pre_up = dot(x[:, :width], up_w[...], ((1,), (0,)))
    back = dot(y[...], down_w[...], ((1,), (1,)))
    g = x[:, width:][:, 0:1].astype(F32)
    sig = jax.nn.sigmoid(pre_gate)
    act = pre_gate * sig
    hidden = act * pre_up
    weighted_t[...] = (g * hidden).T.astype(BF16)
    products = jnp.sum(hidden * back, axis=1, keepdims=True)
    scaled = g * back
    d_both[:, :hidden_dim] = (
        scaled * pre_up * sig * (1.0 + pre_gate * (1.0 - sig))
    ).astype(BF16)
    d_both[:, hidden_dim:] = (scaled * act).astype(BF16)
    keep[:, width:] = lane_pair(half, products[:half], 0.0)
    send[:, width:] = split_pair(products[half:]).astype(BF16)
    wide = 1024
    for i in range(width // wide):
        at = pl.ds(i * wide, wide)
        part = dot(d_both[:, :hidden_dim], gate_w[at, :], ((1,), (1,)))
        part += dot(d_both[:, hidden_dim:], up_w[at, :], ((1,), (1,)))
        keep[:, at] = part[:half]
        send[:, at] = part[half:].astype(BF16)


def fold_kernel(have, got, keep, send):
    half = keep.shape[0]
    width = keep.shape[1] - LANES
    total = have[:, :width] + got[:, :width].astype(F32)
    keep[:, :width] = total[:half]
    send[:, :width] = total[half:].astype(BF16)
    tail = have[:, width:] + got[:, width:].astype(F32)
    value = tail[:, 0:1] + tail[:, 1:2]
    keep[:, width:] = lane_pair(half, value[:half], 0.0)
    send[:, width:] = split_pair(value[half:]).astype(BF16)


def home_kernel(
    row, have, got, select, base, coef, *refs
):
    rest, grad_tokens, grad_logits, gate_out, up_out, sems = refs[:2], *refs[-5:]
    late = late_copies(row, rest, (gate_out, up_out), sems)
    for copy in late:
        copy.start()
    slots = have.shape[0]
    width = have.shape[1] - LANES
    count = select.shape[0]
    total = (have[:, :width] + got[:, :width].astype(F32)).astype(BF16)
    padded = jnp.concatenate([total, jnp.zeros((count - slots, width), BF16)], axis=0)
    grad_tokens[...] = dot(select[...].astype(BF16), padded, ((0,), (0,))).astype(BF16)
    tail = have[:, width:] + got[:, width:].astype(F32)
    value = tail[:, 0:1] + tail[:, 1:2]
    token_products = jnp.sum(select[0:slots, :] * value, axis=0, keepdims=True)
    grad_logits[...] = base[...] + coef[...] * token_products
    for copy in late:
        copy.wait()


def tiles(out, left, right):
    tall = 128
    for c in range(0, right.shape[1], 256):
        for r in range(0, left.shape[0], tall):
            part = dot(left[r : r + tall], right[:, c : c + 256], ((1,), (0,)))
            out[r : r + tall, c : c + 256] = part.astype(BF16)


def loop(count, body):
    for i in range(count):
        body(i)


def late_copies(row, sources, targets, sems):
    step = sources[0].shape[0]
    return [
        pltpu.make_async_copy(source, target.at[pl.ds(row, step)], sems.at[k])
        for k, (source, target) in enumerate(zip(sources, targets))
    ]


def grads_kernel(first_row, x_t, d_both, *refs):
    gate_out, up_out, gate_left, up_left, gate_buf, up_buf, sems = refs[-7:]
    chunks, step, cols = gate_buf.shape
    copies = []
    if first_row:
        copies += late_copies(first_row - step, refs[:2], (gate_out, up_out), sems.at[chunks])
        for copy in copies:
            copy.start()
    for i in range(chunks + 1):
        at = pl.ds(first_row + i * step, step)
        outs = (gate_buf, up_buf) if i < chunks else (gate_left, up_left)
        for k, target in enumerate((gate_out, up_out)):
            tile = outs[k].at[i] if i < chunks else outs[k]
            tiles(tile, x_t.at[at], d_both.at[:, pl.ds(k * cols, cols)])
            if i < chunks:
                copy = pltpu.make_async_copy(tile, target.at[at], sems.at[i, k])
                copy.start()
                copies.append(copy)
    for copy in copies:
        copy.wait()


def first_kernel(weighted_t, y, x_t, d_both, down_out, *refs):
    down_buf, down_sems = refs[4:6]
    chunks, _, step = down_buf.shape
    copies = []
    for i in range(chunks):
        at = pl.ds(i * step, step)
        tiles(down_buf.at[i], weighted_t, y.at[:, at])
        copies.append(pltpu.make_async_copy(down_buf.at[i], down_out.at[:, at], down_sems.at[i]))
        copies[i].start()
    grads_kernel(0, x_t, d_both, *refs[:4], *refs[6:])
    for copy in copies:
        copy.wait()


def grads_of(x_t, d_both, first_row, rows, before, down=()):
    width, slots = x_t.shape
    cols = d_both.shape[1] // 2
    step = 256
    chunks = rows // step - 1
    anywhere = pl.BlockSpec(memory_space=pl.ANY)
    outs = [jax.ShapeDtypeStruct((width, cols), BF16)] * 2
    outs += [jax.ShapeDtypeStruct((step, cols), BF16)] * 2
    out_specs = [anywhere] * 2 + whole(2)
    scratch = [
        pltpu.VMEM((chunks, step, cols), BF16),
        pltpu.VMEM((chunks, step, cols), BF16),
        pltpu.SemaphoreType.DMA((chunks + 1, 2)),
    ]
    kernel = functools.partial(grads_kernel, first_row)
    if down:
        kernel = first_kernel
        wide = 1024
        outs = [jax.ShapeDtypeStruct((cols, width), BF16)] + outs
        out_specs = [anywhere] + out_specs
        scratch = [
            pltpu.VMEM((width // wide, cols, wide), BF16),
            pltpu.SemaphoreType.DMA((width // wide,)),
        ] + scratch
    elements = 2 * rows * cols + (width * cols if down else 0)
    return pl.pallas_call(
        kernel,
        out_shape=outs,
        in_specs=whole(2 + len(down)) + (whole(2) + [anywhere] * 2 if before else []),
        out_specs=out_specs,
        scratch_shapes=scratch,
        input_output_aliases={4: 0, 5: 1} if before else {},
        compiler_params=pltpu.CompilerParams(vmem_limit_bytes=20 * MIB),
        cost_estimate=pl.CostEstimate(
            flops=8 * slots * elements, bytes_accessed=2 * elements, transcendentals=0
        ),
    )(*down, x_t, d_both, *before[2:], *before[:2])


def make_shards(n):
    levels = []
    bit = n // 2
    while bit > 4:
        levels.append((bit, bit))
        bit //= 2
    levels += [(4, 2), (2, 4)]

    def swap(block, bits):
        return lax.ppermute(block, "blk", [(i, i ^ bits[i % 2]) for i in range(n)])

    def shards(
        tokens, cotangent, gate_weight, up_weight, down_weight, logits, ref_logits, routes
    ):
        count, width = tokens.shape
        slots = cotangent.shape[0]
        experts = logits.shape[1]
        hidden = down_weight.shape[0]
        rows = n * slots
        wide = width + LANES
        anywhere = pl.BlockSpec(memory_space=pl.ANY)

        send, entropy, divergence, base, coef, select = pl.pallas_call(
            router_kernel,
            out_shape=[
                jax.ShapeDtypeStruct((slots, wide + width), BF16),
                jax.ShapeDtypeStruct((1, count), F32),
                jax.ShapeDtypeStruct((1, count), F32),
                jax.ShapeDtypeStruct((experts, count), F32),
                jax.ShapeDtypeStruct((experts, count), F32),
                jax.ShapeDtypeStruct((count, count), F32),
            ],
            in_specs=[anywhere] * 5,
            out_specs=whole(6),
            scratch_shapes=[
                pltpu.VMEM((count, width), BF16),
                pltpu.VMEM((experts, count), F32),
                pltpu.VMEM((experts, count), F32),
                pltpu.VMEM((2, count), jnp.int32),
                pltpu.VMEM((slots, width), BF16),
                pltpu.SemaphoreType.DMA((5,)),
            ],
            compiler_params=pltpu.CompilerParams(vmem_limit_bytes=8 * MIB),
            cost_estimate=pl.CostEstimate(
                flops=1 << 20, bytes_accessed=1 << 24, transcendentals=0
            ),
        )(*[in_hbm(a) for a in (tokens, logits.T, ref_logits.T, routes.T, cotangent)])

        got = swap(send, levels[0])
        gate_w, own = fetch([gate_weight], send)
        own = jnp.concatenate([own, got])
        for bits in levels[1:-2]:
            own = jnp.concatenate([own, swap(own, bits)])
        near = swap(own, levels[-2])
        far = swap(own, levels[-1])
        up_w, down_w, own = fetch([up_weight, down_weight], own)
        few = own.shape[0]
        near_x, far_y = call(
            split_kernel, [((few, wide), BF16), ((few, width), BF16)], [near, far], 0, 1 << 18
        )
        (most,) = call(
            join_kernel, [((3 * few, wide + width), BF16)], [own, near, far], 0, 1 << 23
        )
        last_x = swap(near_x, levels[-1])
        last_y = swap(far_y, levels[-2])
        pieces = [most, last_x, last_y]
        pieces += [swap(piece, (1, 1)) for piece in pieces]

        work = 2 * rows * width * hidden
        half = rows // 2
        low, keep, weighted_t, d_both, x_t, y_all = pl.pallas_call(
            expert_kernel,
            out_shape=[
                jax.ShapeDtypeStruct((half, wide), BF16),
                jax.ShapeDtypeStruct((half, wide), F32),
                jax.ShapeDtypeStruct((hidden, rows), BF16),
                jax.ShapeDtypeStruct((rows, 2 * hidden), BF16),
                jax.ShapeDtypeStruct((width, rows), BF16),
                jax.ShapeDtypeStruct((rows, width), BF16),
            ],
            in_specs=whole(9),
            out_specs=whole(6),
            scratch_shapes=[pltpu.VMEM((rows, wide), BF16)],
            compiler_params=pltpu.CompilerParams(vmem_limit_bytes=16 * MIB),
            cost_estimate=pl.CostEstimate(
                flops=16 * work, bytes_accessed=4 * width * hidden, transcendentals=0
            ),
        )(*pieces, down_w, gate_w, up_w)

        for bits in [(1, 1)] + levels[::-1]:
            got = swap(low, bits)
            if bits == levels[0]:
                break
            half //= 2
            keep, low = call(
                fold_kernel,
                [((half, wide), F32), ((half, wide), BF16)],
                [keep, got],
                4 * half * wide,
                16 * half * wide,
            )

        cuts = [0, width // 3, 2 * width // 3, width]
        grad_down, *pair = grads_of(x_t, d_both, 0, cuts[1], (), (weighted_t, y_all))
        for start, stop in zip(cuts[1:], cuts[2:]):
            pair = grads_of(x_t, d_both, start, stop - start, tuple(pair))
        grad_gate, grad_up, *rest = pair

        grad_tokens, grad_logits, grad_gate, grad_up = pl.pallas_call(
            functools.partial(home_kernel, width - rest[0].shape[0]),
            out_shape=[
                jax.ShapeDtypeStruct((count, width), BF16),
                jax.ShapeDtypeStruct((experts, count), F32),
                jax.ShapeDtypeStruct(grad_gate.shape, BF16),
                jax.ShapeDtypeStruct(grad_up.shape, BF16),
            ],
            in_specs=whole(7) + [anywhere] * 2,
            out_specs=whole(2) + [anywhere] * 2,
            scratch_shapes=[pltpu.SemaphoreType.DMA((2,))],
            input_output_aliases={7: 2, 8: 3},
            compiler_params=pltpu.CompilerParams(vmem_limit_bytes=8 * MIB),
            cost_estimate=pl.CostEstimate(
                flops=1 << 20, bytes_accessed=1 << 18, transcendentals=0
            ),
        )(keep, got, select, base, coef, *rest, grad_gate, grad_up)
        return (
            grad_gate,
            grad_up,
            grad_down,
            grad_tokens,
            grad_logits.T,
            entropy.reshape(count),
            divergence.reshape(count),
        )

    return shards


def solution(mesh):
    in_specs = (
        P(("grp", "blk"), None),
        P(("grp", "blk"), None),
        P(None, "blk"),
        P(None, "blk"),
        P("blk", None),
        P(("grp", "blk"), None),
        P(("grp", "blk"), None),
        P(("grp", "blk"), None),
    )
    out_specs = (
        P("grp", "blk"),
        P("grp", "blk"),
        P(("grp", "blk"), None),
        P(("grp", "blk"), None),
        P(("grp", "blk"), None),
        P(("grp", "blk")),
        P(("grp", "blk")),
    )
    return jax.shard_map(
        make_shards(mesh.shape["blk"]),
        mesh=mesh,
        in_specs=in_specs,
        out_specs=out_specs,
        check_vma=False,
    )
```

```python
import functools

import jax
import jax.numpy as jnp
from jax import lax
from jax.experimental import pallas as pl
from jax.experimental.pallas import tpu as pltpu
from jax.sharding import PartitionSpec as P

F32 = jnp.float32
BF16 = jnp.bfloat16
LANES = 128
MIB = 1 << 20


def dot(left, right, dims):
    return lax.dot_general(left, right, (dims, ((), ())), preferred_element_type=F32)


def whole(count):
    return [pl.BlockSpec(memory_space=pltpu.VMEM)] * count


def call(kernel, outs, args, flops, moved, limit=8):
    return pl.pallas_call(
        kernel,
        out_shape=[jax.ShapeDtypeStruct(s, t) for s, t in outs],
        in_specs=whole(len(args)),
        out_specs=whole(len(outs)),
        compiler_params=pltpu.CompilerParams(vmem_limit_bytes=limit * MIB),
        cost_estimate=pl.CostEstimate(flops=flops, bytes_accessed=moved, transcendentals=0),
    )(*args)


def in_hbm(array):
    return pltpu.with_memory_space_constraint(array, pltpu.HBM)


def in_vmem(array):
    return pltpu.with_memory_space_constraint(array, pltpu.VMEM)


def lane_pair(rows, first, second):
    lane = lax.broadcasted_iota(jnp.int32, (rows, LANES), 1)
    return jnp.where(lane == 0, first, jnp.where(lane == 1, second, 0.0))


def split_pair(value):
    high = value.astype(BF16).astype(F32)
    return lane_pair(value.shape[0], high, value - high)


def router_kernel(
    tokens_in,
    logits_in,
    ref_in,
    routes_in,
    y_in,
    send,
    entropy,
    divergence,
    base,
    coef,
    select_out,
    tokens,
    logits,
    ref_logits,
    routes,
    y,
    sems,
):
    sources = (logits_in, ref_in, routes_in, tokens_in, y_in)
    targets = (logits, ref_logits, routes, tokens, y)
    copies = [
        pltpu.make_async_copy(s, t, sems.at[i]) for i, (s, t) in enumerate(zip(sources, targets))
    ]
    for copy in copies:
        copy.start()
    for copy in copies[:3]:
        copy.wait()
    slots, width = send.shape[0], tokens.shape[1]
    experts, count = logits.shape
    x, r = logits[...], ref_logits[...]
    shifted = x - jnp.max(x, axis=0, keepdims=True)
    policy_log = shifted - jnp.log(jnp.sum(jnp.exp(shifted), axis=0, keepdims=True))
    shifted = r - jnp.max(r, axis=0, keepdims=True)
    frozen_log = shifted - jnp.log(jnp.sum(jnp.exp(shifted), axis=0, keepdims=True))
    probs = jnp.exp(policy_log)
    ratio = policy_log - frozen_log
    div = jnp.sum(probs * ratio, axis=0, keepdims=True)
    entropy[...] = -jnp.sum(probs * policy_log, axis=0, keepdims=True)
    divergence[...] = div
    base[...] = probs * (ratio - div)
    first, second = routes[0:1, :], routes[1:2, :]
    routed = jnp.where((first == 0) | (second == 0), 1.0, 0.0)
    expert = lax.broadcasted_iota(jnp.int32, (experts, count), 0)
    partner_hot = jnp.where(expert == first + second, 1.0, 0.0)
    partner_logit = jnp.sum(x * partner_hot, axis=0, keepdims=True)
    gate = jnp.where(routed > 0.0, jax.nn.sigmoid(x[0:1, :] - partner_logit), 0.0)
    coef[...] = (jnp.where(expert == 0, 1.0, 0.0) - partner_hot) * (gate * (1.0 - gate))
    token = lax.broadcasted_iota(jnp.int32, (1, count), 1)
    position = jnp.full((1, count), -1.0, F32)
    for t in range(count):
        position += jnp.where(token >= t, routed[:, t : t + 1], 0.0)
    slot = lax.broadcasted_iota(jnp.int32, (count, count), 0)
    hit = (slot == position.astype(jnp.int32)) & (routed > 0.0) & (slot < slots)
    select = jnp.where(hit, 1.0, 0.0)
    select_out[...] = select
    gate_low = gate.astype(BF16).astype(F32)
    g_slots = jnp.sum(select * gate_low, axis=1, keepdims=True)
    wide = width + LANES
    send[:, width:wide] = jnp.broadcast_to(g_slots[:slots], (slots, LANES)).astype(BF16)
    copies[3].wait()
    x_slots = dot(select.astype(BF16), tokens[...], ((1,), (0,)))
    send[:, :width] = x_slots[:slots].astype(BF16)
    copies[4].wait()
    send[:, wide:] = y[...]


def fetch_copies(sources, targets, sems):
    parts = sems.shape[1]
    copies = []
    for k, (source, target) in enumerate(zip(sources, targets)):
        step = source.shape[0] // parts
        for i in range(parts):
            at = pl.ds(i * step, step)
            copies.append(pltpu.make_async_copy(source.at[at], target.at[at], sems.at[k, i]))
    return copies


def fetch_kernel(source, after, target, sems):
    copies = fetch_copies([source], [target], sems)
    for copy in copies:
        copy.start()
    for copy in copies:
        copy.wait()


def fetch(weight, after):
    anywhere = pl.BlockSpec(memory_space=pl.ANY)
    out = pl.pallas_call(
        fetch_kernel,
        out_shape=pltpu.VMEM(weight.shape, weight.dtype),
        in_specs=[anywhere] * 2,
        out_specs=whole(1)[0],
        scratch_shapes=[pltpu.SemaphoreType.DMA((1, 4))],
        compiler_params=pltpu.CompilerParams(vmem_limit_bytes=8 * MIB),
        cost_estimate=pl.CostEstimate(
            flops=0, bytes_accessed=2 * weight.size, transcendentals=0
        ),
    )(in_hbm(weight), after)
    return in_vmem(out)


def relay_kernel(block, *refs):
    refs[-1][...] = block[...]


def relay(block, *after):
    return pl.pallas_call(
        relay_kernel,
        out_shape=jax.ShapeDtypeStruct(block.shape, block.dtype),
        in_specs=whole(1) + [pl.BlockSpec(memory_space=pl.ANY)] * len(after),
        out_specs=whole(1)[0],
        compiler_params=pltpu.CompilerParams(vmem_limit_bytes=8 * MIB),
        cost_estimate=pl.CostEstimate(
            flops=0, bytes_accessed=4 * block.size, transcendentals=0
        ),
    )(block, *after)


def expert_kernel(*refs):
    pieces, (down_in, gate_w, up_w), refs = refs[:4], refs[4:7], refs[7:]
    send, keep, weighted_t, d_both, x_t, y, x, down_w, sems = refs
    rows, width, hidden_dim = x.shape[0], gate_w.shape[0], gate_w.shape[1]
    wide = width + LANES
    half = rows // 2
    copies = fetch_copies([down_in], [down_w], sems)
    for copy in copies:
        copy.start()
    for c in range(0, wide, LANES):
        at = pl.ds(c, LANES)
        block = jnp.concatenate([ref[:, at].astype(F32) for ref in pieces])
        x[:, at] = block.astype(BF16)
        if c < width:
            x_t[at, :] = block.T.astype(BF16)
    quarter = rows // 4
    for i, ref in enumerate(pieces):
        y[i * quarter : (i + 1) * quarter, :] = ref[:, wide:]
    pre_gate = dot(x[:, :width], gate_w[...], ((1,), (0,)))
    pre_up = dot(x[:, :width], up_w[...], ((1,), (0,)))
    for copy in copies:
        copy.wait()
    back = dot(y[...], down_w[...], ((1,), (1,)))
    g = x[:, width:][:, 0:1].astype(F32)
    sig = jax.nn.sigmoid(pre_gate)
    act = pre_gate * sig
    hidden = act * pre_up
    weighted_t[...] = (g * hidden).T.astype(BF16)
    products = jnp.sum(hidden * back, axis=1, keepdims=True)
    scaled = g * back
    d_both[:, :hidden_dim] = (
        scaled * pre_up * sig * (1.0 + pre_gate * (1.0 - sig))
    ).astype(BF16)
    d_both[:, hidden_dim:] = (scaled * act).astype(BF16)
    keep[:, width:] = lane_pair(half, products[:half], 0.0)
    send[:, width:] = split_pair(products[half:]).astype(BF16)
    wide = 1024
    for i in range(width // wide):
        at = pl.ds(i * wide, wide)
        part = dot(d_both[:, :hidden_dim], gate_w[at, :], ((1,), (1,)))
        part += dot(d_both[:, hidden_dim:], up_w[at, :], ((1,), (1,)))
        keep[:, at] = part[:half]
        send[:, at] = part[half:].astype(BF16)


def fold_kernel(have, got, keep, send):
    half = keep.shape[0]
    width = keep.shape[1] - LANES
    total = have[:, :width] + got[:, :width].astype(F32)
    keep[:, :width] = total[:half]
    send[:, :width] = total[half:].astype(BF16)
    tail = have[:, width:] + got[:, width:].astype(F32)
    value = tail[:, 0:1] + tail[:, 1:2]
    keep[:, width:] = lane_pair(half, value[:half], 0.0)
    send[:, width:] = split_pair(value[half:]).astype(BF16)


def home_kernel(have, got, select, base, coef, grad_tokens, grad_logits):
    slots = have.shape[0]
    width = have.shape[1] - LANES
    count = select.shape[0]
    total = (have[:, :width] + got[:, :width].astype(F32)).astype(BF16)
    padded = jnp.concatenate([total, jnp.zeros((count - slots, width), BF16)], axis=0)
    grad_tokens[...] = dot(select[...].astype(BF16), padded, ((0,), (0,))).astype(BF16)
    tail = have[:, width:] + got[:, width:].astype(F32)
    value = tail[:, 0:1] + tail[:, 1:2]
    token_products = jnp.sum(select[0:slots, :] * value, axis=0, keepdims=True)
    grad_logits[...] = base[...] + coef[...] * token_products


def tiles(out, left, right):
    tall = 128
    for c in range(0, right.shape[1], 256):
        for r in range(0, left.shape[0], tall):
            part = dot(left[r : r + tall], right[:, c : c + 256], ((1,), (0,)))
            out[r : r + tall, c : c + 256] = part.astype(BF16)


def loop(count, body):
    for i in range(count):
        body(i)


def late_copies(row, sources, targets, sems):
    step = sources[0].shape[0]
    return [
        pltpu.make_async_copy(source, target.at[pl.ds(row, step)], sems.at[k])
        for k, (source, target) in enumerate(zip(sources, targets))
    ]


def grads_kernel(first_row, last, x_t, d_both, *refs):
    left = refs[:2] if first_row else ()
    gate_buf, up_buf, sems = refs[-3:]
    outs = refs[-5:-3] if last else refs[-7:-5]
    kept = () if last else refs[-5:-3]
    chunks, step, cols = gate_buf.shape
    copies = late_copies(first_row - step, left, outs, sems.at[chunks]) if left else []
    for copy in copies:
        copy.start()
    for i in range(chunks if last else chunks + 1):
        at = pl.ds(first_row + i * step, step)
        for k, target in enumerate(outs):
            tile = (gate_buf, up_buf)[k].at[i] if i < chunks else kept[k]
            tiles(tile, x_t.at[at], d_both.at[:, pl.ds(k * cols, cols)])
            if i < chunks:
                copy = pltpu.make_async_copy(tile, target.at[at], sems.at[i, k])
                copy.start()
                copies.append(copy)
    for copy in copies:
        copy.wait()


def first_kernel(weighted_t, y, x_t, d_both, down_out, *refs):
    down_buf, down_sems = refs[4:6]
    chunks, _, step = down_buf.shape
    copies = []
    for i in range(chunks):
        at = pl.ds(i * step, step)
        tiles(down_buf.at[i], weighted_t, y.at[:, at])
        copies.append(pltpu.make_async_copy(down_buf.at[i], down_out.at[:, at], down_sems.at[i]))
        copies[i].start()
    grads_kernel(0, False, x_t, d_both, *refs[:4], *refs[6:])
    for copy in copies:
        copy.wait()


def grads_of(x_t, d_both, first_row, rows, before, down=()):
    width, slots = x_t.shape
    cols = d_both.shape[1] // 2
    step = 256
    last = first_row + rows == width
    chunks = rows // step - (0 if last else 1)
    anywhere = pl.BlockSpec(memory_space=pl.ANY)
    outs = [jax.ShapeDtypeStruct((width, cols), BF16)] * 2
    outs += [] if last else [jax.ShapeDtypeStruct((step, cols), BF16)] * 2
    out_specs = [anywhere] * 2 + whole(len(outs) - 2)
    scratch = [
        pltpu.VMEM((chunks, step, cols), BF16),
        pltpu.VMEM((chunks, step, cols), BF16),
        pltpu.SemaphoreType.DMA((chunks + 1, 2)),
    ]
    kernel = functools.partial(grads_kernel, first_row, last)
    if down:
        kernel = first_kernel
        wide = 1024
        outs = [jax.ShapeDtypeStruct((cols, width), BF16)] + outs
        out_specs = [anywhere] + out_specs
        scratch = [
            pltpu.VMEM((width // wide, cols, wide), BF16),
            pltpu.SemaphoreType.DMA((width // wide,)),
        ] + scratch
    elements = 2 * rows * cols + (width * cols if down else 0)
    return pl.pallas_call(
        kernel,
        out_shape=outs,
        in_specs=whole(2 + len(down)) + (whole(2) + [anywhere] * 2 if before else []),
        out_specs=out_specs,
        scratch_shapes=scratch,
        input_output_aliases={4: 0, 5: 1} if before else {},
        compiler_params=pltpu.CompilerParams(vmem_limit_bytes=20 * MIB),
        cost_estimate=pl.CostEstimate(
            flops=8 * slots * elements, bytes_accessed=2 * elements, transcendentals=0
        ),
    )(*down, x_t, d_both, *before[2:], *before[:2])


def make_shards(n):
    levels = []
    bit = n // 2
    while bit > 4:
        levels.append((bit, bit))
        bit //= 2
    levels += [(4, 2), (2, 4)]

    def swap(block, bits):
        return lax.ppermute(block, "blk", [(i, i ^ bits[i % 2]) for i in range(n)])

    def shards(
        tokens, cotangent, gate_weight, up_weight, down_weight, logits, ref_logits, routes
    ):
        count, width = tokens.shape
        slots = cotangent.shape[0]
        experts = logits.shape[1]
        hidden = down_weight.shape[0]
        rows = n * slots
        wide = width + LANES
        anywhere = pl.BlockSpec(memory_space=pl.ANY)

        send, entropy, divergence, base, coef, select = pl.pallas_call(
            router_kernel,
            out_shape=[
                jax.ShapeDtypeStruct((slots, wide + width), BF16),
                jax.ShapeDtypeStruct((1, count), F32),
                jax.ShapeDtypeStruct((1, count), F32),
                jax.ShapeDtypeStruct((experts, count), F32),
                jax.ShapeDtypeStruct((experts, count), F32),
                jax.ShapeDtypeStruct((count, count), F32),
            ],
            in_specs=[anywhere] * 5,
            out_specs=whole(6),
            scratch_shapes=[
                pltpu.VMEM((count, width), BF16),
                pltpu.VMEM((experts, count), F32),
                pltpu.VMEM((experts, count), F32),
                pltpu.VMEM((2, count), jnp.int32),
                pltpu.VMEM((slots, width), BF16),
                pltpu.SemaphoreType.DMA((5,)),
            ],
            compiler_params=pltpu.CompilerParams(vmem_limit_bytes=8 * MIB),
            cost_estimate=pl.CostEstimate(
                flops=1 << 20, bytes_accessed=1 << 24, transcendentals=0
            ),
        )(*[in_hbm(a) for a in (tokens, logits.T, ref_logits.T, routes.T, cotangent)])

        own = send
        for bits in levels[:-3]:
            own = jnp.concatenate([own, swap(own, bits)])
        first, second, third = levels[-3:]
        block_1 = swap(own, first)
        block_2 = swap(own, second)
        block_3 = swap(own, third)
        gate_w = fetch(gate_weight, own)
        block_1 = relay(block_1, gate_w, block_2)
        block_12 = swap(block_1, second)
        block_13 = swap(block_1, third)
        block_23 = swap(block_3, second)
        up_w = fetch(up_weight, block_1)
        block_12 = relay(block_12, up_w)
        block_123 = swap(block_12, third)
        low_half = jnp.concatenate([own, block_1, block_2, block_12])
        high_half = jnp.concatenate([block_3, block_13, block_23, block_123])
        pieces = [low_half, high_half]
        pieces += [swap(piece, (1, 1)) for piece in pieces]

        work = 2 * rows * width * hidden
        half = rows // 2
        low, keep, weighted_t, d_both, x_t, y_all = pl.pallas_call(
            expert_kernel,
            out_shape=[
                jax.ShapeDtypeStruct((half, wide), BF16),
                jax.ShapeDtypeStruct((half, wide), F32),
                jax.ShapeDtypeStruct((hidden, rows), BF16),
                jax.ShapeDtypeStruct((rows, 2 * hidden), BF16),
                jax.ShapeDtypeStruct((width, rows), BF16),
                jax.ShapeDtypeStruct((rows, width), BF16),
            ],
            in_specs=whole(4) + [anywhere] + whole(2),
            out_specs=whole(6),
            scratch_shapes=[
                pltpu.VMEM((rows, wide), BF16),
                pltpu.VMEM((hidden, width), BF16),
                pltpu.SemaphoreType.DMA((1, 4)),
            ],
            compiler_params=pltpu.CompilerParams(vmem_limit_bytes=24 * MIB),
            cost_estimate=pl.CostEstimate(
                flops=16 * work, bytes_accessed=4 * width * hidden, transcendentals=0
            ),
        )(*pieces, in_hbm(down_weight), gate_w, up_w)

        for bits in [(1, 1)] + levels[::-1]:
            got = swap(low, bits)
            if bits == levels[0]:
                break
            half //= 2
            keep, low = call(
                fold_kernel,
                [((half, wide), F32), ((half, wide), BF16)],
                [keep, got],
                4 * half * wide,
                16 * half * wide,
            )

        cuts = [0, width // 3, 2 * width // 3, width]
        grad_down, *pair = grads_of(x_t, d_both, 0, cuts[1], (), (weighted_t, y_all))
        for start, stop in zip(cuts[1:], cuts[2:]):
            pair = grads_of(x_t, d_both, start, stop - start, tuple(pair))
        grad_gate, grad_up = pair

        grad_tokens, grad_logits = call(
            home_kernel,
            [((count, width), BF16), ((experts, count), F32)],
            [keep, got, select, base, coef],
            1 << 20,
            1 << 18,
        )
        return (
            grad_gate,
            grad_up,
            grad_down,
            grad_tokens,
            grad_logits.T,
            entropy.reshape(count),
            divergence.reshape(count),
        )

    return shards


def solution(mesh):
    in_specs = (
        P(("grp", "blk"), None),
        P(("grp", "blk"), None),
        P(None, "blk"),
        P(None, "blk"),
        P("blk", None),
        P(("grp", "blk"), None),
        P(("grp", "blk"), None),
        P(("grp", "blk"), None),
    )
    out_specs = (
        P("grp", "blk"),
        P("grp", "blk"),
        P(("grp", "blk"), None),
        P(("grp", "blk"), None),
        P(("grp", "blk"), None),
        P(("grp", "blk")),
        P(("grp", "blk")),
    )
    return jax.shard_map(
        make_shards(mesh.shape["blk"]),
        mesh=mesh,
        in_specs=in_specs,
        out_specs=out_specs,
        check_vma=False,
    )
```

```python
import functools

import jax
import jax.numpy as jnp
from jax import lax
from jax.experimental import pallas as pl
from jax.experimental.pallas import tpu as pltpu
from jax.sharding import PartitionSpec as P

F32 = jnp.float32
BF16 = jnp.bfloat16
LANES = 128
MIB = 1 << 20


def dot(left, right, dims):
    return lax.dot_general(left, right, (dims, ((), ())), preferred_element_type=F32)


def whole(count):
    return [pl.BlockSpec(memory_space=pltpu.VMEM)] * count


def call(kernel, outs, args, flops, moved, limit=8, after=()):
    return pl.pallas_call(
        kernel,
        out_shape=[jax.ShapeDtypeStruct(s, t) for s, t in outs],
        in_specs=whole(len(args)) + [pl.BlockSpec(memory_space=pl.ANY)] * len(after),
        out_specs=whole(len(outs)),
        compiler_params=pltpu.CompilerParams(vmem_limit_bytes=limit * MIB),
        cost_estimate=pl.CostEstimate(flops=flops, bytes_accessed=moved, transcendentals=0),
    )(*args, *after)


def in_hbm(array):
    return pltpu.with_memory_space_constraint(array, pltpu.HBM)


def in_vmem(array):
    return pltpu.with_memory_space_constraint(array, pltpu.VMEM)


def lane_pair(rows, first, second):
    lane = lax.broadcasted_iota(jnp.int32, (rows, LANES), 1)
    return jnp.where(lane == 0, first, jnp.where(lane == 1, second, 0.0))


def split_pair(value):
    high = value.astype(BF16).astype(F32)
    return lane_pair(value.shape[0], high, value - high)


def router_kernel(
    tokens_in,
    logits_in,
    ref_in,
    routes_in,
    y_in,
    send,
    entropy,
    divergence,
    base,
    coef,
    select_out,
    tokens,
    logits,
    ref_logits,
    routes,
    y,
    sems,
):
    sources = (logits_in, ref_in, routes_in, tokens_in, y_in)
    targets = (logits, ref_logits, routes, tokens, y)
    copies = [
        pltpu.make_async_copy(s, t, sems.at[i]) for i, (s, t) in enumerate(zip(sources, targets))
    ]
    for copy in copies:
        copy.start()
    for copy in copies[:3]:
        copy.wait()
    slots, width = send.shape[0], tokens.shape[1]
    experts, count = logits.shape
    x, r = logits[...], ref_logits[...]
    shifted = x - jnp.max(x, axis=0, keepdims=True)
    policy_log = shifted - jnp.log(jnp.sum(jnp.exp(shifted), axis=0, keepdims=True))
    shifted = r - jnp.max(r, axis=0, keepdims=True)
    frozen_log = shifted - jnp.log(jnp.sum(jnp.exp(shifted), axis=0, keepdims=True))
    probs = jnp.exp(policy_log)
    ratio = policy_log - frozen_log
    div = jnp.sum(probs * ratio, axis=0, keepdims=True)
    entropy[...] = -jnp.sum(probs * policy_log, axis=0, keepdims=True)
    divergence[...] = div
    base[...] = probs * (ratio - div)
    first, second = routes[0:1, :], routes[1:2, :]
    routed = jnp.where((first == 0) | (second == 0), 1.0, 0.0)
    expert = lax.broadcasted_iota(jnp.int32, (experts, count), 0)
    partner_hot = jnp.where(expert == first + second, 1.0, 0.0)
    partner_logit = jnp.sum(x * partner_hot, axis=0, keepdims=True)
    gate = jnp.where(routed > 0.0, jax.nn.sigmoid(x[0:1, :] - partner_logit), 0.0)
    coef[...] = (jnp.where(expert == 0, 1.0, 0.0) - partner_hot) * (gate * (1.0 - gate))
    token = lax.broadcasted_iota(jnp.int32, (1, count), 1)
    position = jnp.full((1, count), -1.0, F32)
    for t in range(count):
        position += jnp.where(token >= t, routed[:, t : t + 1], 0.0)
    slot = lax.broadcasted_iota(jnp.int32, (count, count), 0)
    hit = (slot == position.astype(jnp.int32)) & (routed > 0.0) & (slot < slots)
    select = jnp.where(hit, 1.0, 0.0)
    select_out[...] = select
    gate_low = gate.astype(BF16).astype(F32)
    g_slots = jnp.sum(select * gate_low, axis=1, keepdims=True)
    wide = width + LANES
    send[:, width:wide] = jnp.broadcast_to(g_slots[:slots], (slots, LANES)).astype(BF16)
    copies[3].wait()
    x_slots = dot(select.astype(BF16), tokens[...], ((1,), (0,)))
    send[:, :width] = x_slots[:slots].astype(BF16)
    copies[4].wait()
    send[:, wide:] = y[...]


def fetch_copies(sources, targets, sems):
    parts = sems.shape[1]
    copies = []
    for k, ((source, row), target) in enumerate(zip(sources, targets)):
        step = target.shape[0] // parts
        for i in range(parts):
            copies.append(
                pltpu.make_async_copy(
                    source.at[pl.ds(row + i * step, step)],
                    target.at[pl.ds(i * step, step)],
                    sems.at[k, i],
                )
            )
    return copies


def fetch_kernel(count, *refs):
    sources, targets, sems = refs[:count], refs[count + 1 : -1], refs[-1]
    copies = fetch_copies([(source, 0) for source in sources], targets, sems)
    for copy in copies:
        copy.start()
    for copy in copies:
        copy.wait()


def fetch(weights, rows, after):
    anywhere = pl.BlockSpec(memory_space=pl.ANY)
    count = len(weights)
    out = pl.pallas_call(
        functools.partial(fetch_kernel, count),
        out_shape=[pltpu.VMEM((r, w.shape[1]), w.dtype) for w, r in zip(weights, rows)],
        in_specs=[anywhere] * (count + 1),
        out_specs=whole(count),
        scratch_shapes=[pltpu.SemaphoreType.DMA((count, 4))],
        compiler_params=pltpu.CompilerParams(vmem_limit_bytes=8 * MIB),
        cost_estimate=pl.CostEstimate(
            flops=0, bytes_accessed=2 * sum(w.size for w in weights), transcendentals=0
        ),
    )(*[in_hbm(w) for w in weights], after)
    return [in_vmem(w) for w in out]


def relay_kernel(block, *refs):
    refs[-1][...] = block[...]


def relay(block, *after):
    return pl.pallas_call(
        relay_kernel,
        out_shape=jax.ShapeDtypeStruct(block.shape, block.dtype),
        in_specs=whole(1) + [pl.BlockSpec(memory_space=pl.ANY)] * len(after),
        out_specs=whole(1)[0],
        compiler_params=pltpu.CompilerParams(vmem_limit_bytes=8 * MIB),
        cost_estimate=pl.CostEstimate(
            flops=0, bytes_accessed=4 * block.size, transcendentals=0
        ),
    )(block, *after)


def expert_kernel(*refs):
    pieces, (down_in, up_in, gate_w, up_head), refs = refs[:4], refs[4:8], refs[8:]
    send, keep, weighted_t, d_both, x_t, y, x, down_w, up_tail, up_sems, down_sems = refs
    rows, width, hidden_dim = x.shape[0], gate_w.shape[0], gate_w.shape[1]
    wide, cut = width + LANES, up_head.shape[0]
    half = rows // 2
    up_copies = fetch_copies([(up_in, cut)], [up_tail], up_sems)
    down_copies = fetch_copies([(down_in, 0)], [down_w], down_sems)
    for copy in up_copies + down_copies:
        copy.start()
    for c in range(0, wide, LANES):
        at = pl.ds(c, LANES)
        block = jnp.concatenate([ref[:, at].astype(F32) for ref in pieces])
        x[:, at] = block.astype(BF16)
        if c < width:
            x_t[at, :] = block.T.astype(BF16)
    for c in range(0, width, LANES):
        parts = [ref[:, wide + c : wide + c + LANES].astype(F32) for ref in pieces]
        y[:, c : c + LANES] = jnp.concatenate(parts).astype(BF16)
    pre_gate = dot(x[:, :width], gate_w[...], ((1,), (0,)))
    pre_up = dot(x[:, :cut], up_head[...], ((1,), (0,)))
    for copy in up_copies:
        copy.wait()
    pre_up += dot(x[:, cut:width], up_tail[...], ((1,), (0,)))
    part = hidden_dim // len(down_copies)
    back = []
    for i, copy in enumerate(down_copies):
        copy.wait()
        back.append(dot(y[...], down_w[i * part : (i + 1) * part, :], ((1,), (1,))))
    back = jnp.concatenate(back, axis=1)
    g = x[:, width:][:, 0:1].astype(F32)
    sig = jax.nn.sigmoid(pre_gate)
    act = pre_gate * sig
    hidden = act * pre_up
    weighted_t[...] = (g * hidden).T.astype(BF16)
    products = jnp.sum(hidden * back, axis=1, keepdims=True)
    scaled = g * back
    d_both[:, :hidden_dim] = (
        scaled * pre_up * sig * (1.0 + pre_gate * (1.0 - sig))
    ).astype(BF16)
    d_both[:, hidden_dim:] = (scaled * act).astype(BF16)
    keep[:, width:] = lane_pair(half, products[:half], 0.0)
    send[:, width:] = split_pair(products[half:]).astype(BF16)
    wide = 1024
    for i in range(width // wide):
        at = pl.ds(i * wide, wide)
        up_rows = up_head[at, :] if i * wide < cut else up_tail[pl.ds(i * wide - cut, wide), :]
        part = dot(d_both[:, :hidden_dim], gate_w[at, :], ((1,), (1,)))
        part += dot(d_both[:, hidden_dim:], up_rows, ((1,), (1,)))
        keep[:, at] = part[:half]
        send[:, at] = part[half:].astype(BF16)


def folded(have, got):
    width = have.shape[1] - LANES
    tail = have[:, width:] + got[:, width:].astype(F32)
    return have[:, :width] + got[:, :width].astype(F32), tail[:, 0:1] + tail[:, 1:2]


def put_keep(out, row, total, value):
    rows, width = total.shape
    out[row : row + rows, :width] = total
    out[row : row + rows, width:] = lane_pair(rows, value, 0.0)


def put_send(out, total, value):
    width = total.shape[1]
    out[:, :width] = total.astype(BF16)
    out[:, width:] = split_pair(value).astype(BF16)


def core_fold_kernel(have, got, *refs):
    keep, over_second, over_third = refs[-3:]
    total, value = folded(have, got)
    half, part = have.shape[0] // 2, have.shape[0] // 4
    put_keep(keep, 0, total[:half], value[:half])
    put_send(over_second, total[half : half + part], value[half : half + part])
    put_send(over_third, total[half + part :], value[half + part :])


def pair_fold_kernel(have, got_second, got_third, *refs):
    keep, over_second, over_third = refs[-3:]
    half, part = have.shape[0] // 2, have.shape[0] // 4
    total, value = folded(have[:half], got_second)
    put_keep(keep, 0, total[:part], value[:part])
    put_send(over_third, total[part:], value[part:])
    total, value = folded(have[half:], got_third)
    put_keep(keep, part, total[:part], value[:part])
    put_send(over_second, total[part:], value[part:])


def last_fold_kernel(have, got_second, got_third, *refs):
    keep, over_first = refs[-2:]
    part = have.shape[0] // 2
    put_keep(keep, 0, *folded(have[:part], got_third))
    put_send(over_first, *folded(have[part:], got_second))


def fold_kernel(have, got, keep, send):
    half = keep.shape[0]
    total, value = folded(have, got)
    put_keep(keep, 0, total[:half], value[:half])
    put_send(send, total[half:], value[half:])


def home_kernel(have, got, select, base, coef, grad_tokens, grad_logits):
    slots = have.shape[0]
    width = have.shape[1] - LANES
    count = select.shape[0]
    total, value = folded(have, got)
    total = total.astype(BF16)
    padded = jnp.concatenate([total, jnp.zeros((count - slots, width), BF16)], axis=0)
    grad_tokens[...] = dot(select[...].astype(BF16), padded, ((0,), (0,))).astype(BF16)
    token_products = jnp.sum(select[0:slots, :] * value, axis=0, keepdims=True)
    grad_logits[...] = base[...] + coef[...] * token_products


def tiles(out, left, right):
    tall = 128
    for c in range(0, right.shape[1], 256):
        for r in range(0, left.shape[0], tall):
            part = dot(left[r : r + tall], right[:, c : c + 256], ((1,), (0,)))
            out[r : r + tall, c : c + 256] = part.astype(BF16)


def loop(count, body):
    for i in range(count):
        body(i)


def grads_kernel(plan, before, *refs):
    (downs, downs_here), (pairs, pairs_here) = plan
    weighted_t, y, x_t, d_both = refs[:4]
    left_downs, left_pairs = refs[4:6] if before else (None, None)
    down_buf, pair_buf, down_sems, pair_sems = refs[-4:]
    down_out, gate_out, up_out, down_kept, pair_kept = refs[-9:-4]
    wide, step, cols = down_buf.shape[2], pair_buf.shape[2], pair_buf.shape[3]
    copies = []

    def write_down(block, i):
        at, sem = pl.ds(i * wide, wide), down_sems.at[len(copies)]
        copies.append(pltpu.make_async_copy(block, down_out.at[:, at], sem))
        copies[-1].start()

    def write_pair(block, i):
        for k, out in enumerate((gate_out, up_out)):
            at, sem = pl.ds(i * step, step), pair_sems.at[len(copies)]
            copies.append(pltpu.make_async_copy(block.at[k], out.at[at], sem))
            copies[-1].start()

    if before:
        for j, i in enumerate(before[0]):
            write_down(left_downs.at[j], i)
        for j, i in enumerate(before[1]):
            write_pair(left_pairs.at[j], i)
    for j, i in enumerate(downs):
        here = j < downs_here
        block = down_buf.at[j] if here else down_kept.at[j - downs_here]
        tiles(block, weighted_t, y.at[:, pl.ds(i * wide, wide)])
        if here:
            write_down(block, i)
    for j, i in enumerate(pairs):
        here = j < pairs_here
        block = pair_buf.at[j] if here else pair_kept.at[j - pairs_here]
        for k in range(2):
            at = pl.ds(k * cols, cols)
            tiles(block.at[k], x_t.at[pl.ds(i * step, step)], d_both.at[:, at])
        if here:
            write_pair(block, i)
    for copy in copies:
        copy.wait()


def grads_of(weighted_t, y, x_t, d_both, wide, step, plan, before, state):
    (downs, downs_here), (pairs, pairs_here) = plan
    width, slots = x_t.shape
    cols = weighted_t.shape[0]
    anywhere = pl.BlockSpec(memory_space=pl.ANY)

    def down_blocks(count):
        return (max(count, 1), cols, wide)

    def pair_blocks(count):
        return (max(count, 1), 2, step, cols)

    kept = len(downs) - downs_here, len(pairs) - pairs_here
    outs = [jax.ShapeDtypeStruct((cols, width), BF16)]
    outs += [jax.ShapeDtypeStruct((width, cols), BF16)] * 2
    outs += [jax.ShapeDtypeStruct(down_blocks(kept[0]), BF16)]
    outs += [jax.ShapeDtypeStruct(pair_blocks(kept[1]), BF16)]
    sems = 2 * (len(pairs) + len(downs) + sum(len(b) for b in before)) + 2
    elements = len(downs) * cols * wide + 2 * len(pairs) * step * cols
    operands = [weighted_t, y, x_t, d_both, *state[3:], *state[:3]]
    return pl.pallas_call(
        functools.partial(grads_kernel, plan, before),
        out_shape=outs,
        in_specs=whole(4 + len(state[3:])) + [anywhere] * len(state[:3]),
        out_specs=[anywhere] * 3 + whole(2),
        scratch_shapes=[
            pltpu.VMEM(down_blocks(downs_here), BF16),
            pltpu.VMEM(pair_blocks(pairs_here), BF16),
            pltpu.SemaphoreType.DMA((sems,)),
            pltpu.SemaphoreType.DMA((sems,)),
        ],
        input_output_aliases={6: 0, 7: 1, 8: 2} if state else {},
        compiler_params=pltpu.CompilerParams(vmem_limit_bytes=24 * MIB),
        cost_estimate=pl.CostEstimate(
            flops=8 * slots * elements, bytes_accessed=2 * elements, transcendentals=0
        ),
    )(*operands)


def make_shards(n):
    levels = []
    bit = n // 2
    while bit > 4:
        levels.append((bit, bit))
        bit //= 2
    levels += [(4, 2), (2, 4)]

    def swap(block, bits):
        return lax.ppermute(block, "blk", [(i, i ^ bits[i % 2]) for i in range(n)])

    def shards(
        tokens, cotangent, gate_weight, up_weight, down_weight, logits, ref_logits, routes
    ):
        count, width = tokens.shape
        slots = cotangent.shape[0]
        experts = logits.shape[1]
        hidden = down_weight.shape[0]
        rows = n * slots
        wide = width + LANES
        anywhere = pl.BlockSpec(memory_space=pl.ANY)

        send, entropy, divergence, base, coef, select = pl.pallas_call(
            router_kernel,
            out_shape=[
                jax.ShapeDtypeStruct((slots, wide + width), BF16),
                jax.ShapeDtypeStruct((1, count), F32),
                jax.ShapeDtypeStruct((1, count), F32),
                jax.ShapeDtypeStruct((experts, count), F32),
                jax.ShapeDtypeStruct((experts, count), F32),
                jax.ShapeDtypeStruct((count, count), F32),
            ],
            in_specs=[anywhere] * 5,
            out_specs=whole(6),
            scratch_shapes=[
                pltpu.VMEM((count, width), BF16),
                pltpu.VMEM((experts, count), F32),
                pltpu.VMEM((experts, count), F32),
                pltpu.VMEM((2, count), jnp.int32),
                pltpu.VMEM((slots, width), BF16),
                pltpu.SemaphoreType.DMA((5,)),
            ],
            compiler_params=pltpu.CompilerParams(vmem_limit_bytes=8 * MIB),
            cost_estimate=pl.CostEstimate(
                flops=1 << 20, bytes_accessed=1 << 24, transcendentals=0
            ),
        )(*[in_hbm(a) for a in (tokens, logits.T, ref_logits.T, routes.T, cotangent)])

        own = send
        for bits in levels[:-3]:
            own = jnp.concatenate([own, swap(own, bits)])
        first, second, third = levels[-3:]
        block_1 = swap(own, first)
        block_2 = swap(own, second)
        block_3 = swap(own, third)
        cut = width // 3 * 2
        gate_w, up_head = fetch([gate_weight, up_weight], [width, cut], own)
        block_1 = relay(block_1, gate_w, block_2)
        block_12 = swap(block_1, second)
        block_13 = swap(block_1, third)
        block_23 = swap(block_3, second)
        block_123 = swap(block_12, third)
        early = jnp.concatenate([own, block_3, block_1, block_12, block_2, block_23])
        late = jnp.concatenate([block_13, block_123])
        pieces = [early, late]
        pieces += [swap(piece, (1, 1)) for piece in pieces]

        work = 2 * rows * width * hidden
        half = rows // 2
        low, keep, weighted_t, d_both, x_t, y_all = pl.pallas_call(
            expert_kernel,
            out_shape=[
                jax.ShapeDtypeStruct((half, wide), BF16),
                jax.ShapeDtypeStruct((half, wide), F32),
                jax.ShapeDtypeStruct((hidden, rows), BF16),
                jax.ShapeDtypeStruct((rows, 2 * hidden), BF16),
                jax.ShapeDtypeStruct((width, rows), BF16),
                jax.ShapeDtypeStruct((rows, width), BF16),
            ],
            in_specs=whole(4) + [anywhere] * 2 + whole(2),
            out_specs=whole(6),
            scratch_shapes=[
                pltpu.VMEM((rows, wide), BF16),
                pltpu.VMEM((hidden, width), BF16),
                pltpu.VMEM((width - cut, hidden), BF16),
                pltpu.SemaphoreType.DMA((1, 2)),
                pltpu.SemaphoreType.DMA((1, 2)),
            ],
            compiler_params=pltpu.CompilerParams(vmem_limit_bytes=28 * MIB),
            cost_estimate=pl.CostEstimate(
                flops=16 * work, bytes_accessed=4 * width * hidden, transcendentals=0
            ),
        )(*pieces, in_hbm(down_weight), in_hbm(up_weight), gate_w, up_head)

        wide_block, step = width // 6, width // 24
        plans = (
            ((range(0, 4), 2), (range(0), 0)),
            ((range(4, 6), 2), (range(0, 10), 6)),
            ((range(0), 0), (range(10, 19), 5)),
            ((range(0), 0), (range(19, 24), 5)),
        )
        state, before, states = (), (), []
        for plan in plans:
            state = grads_of(
                weighted_t, y_all, x_t, d_both, wide_block, step, plan, before, tuple(state)
            )
            before = tuple(blocks[here:] for blocks, here in plan)
            states.append(state[3])
        grad_down, grad_gate, grad_up = state[:3]

        few = own.shape[0]

        def fold(kernel, kept, sent, args, after):
            outs = [((kept, wide), F32)] + [((count, wide), BF16) for count in sent]
            return call(kernel, outs, args, 4 * kept * wide, 16 * kept * wide, after=after)

        got = swap(low, (1, 1))
        keep, over_second, over_third = fold(
            core_fold_kernel, 4 * few, (2 * few, 2 * few), [keep, got], [states[0]]
        )
        got = swap(over_second, second), swap(over_third, third)
        keep, over_second, over_third = fold(
            pair_fold_kernel, 2 * few, (few, few), [keep, *got], [states[1]]
        )
        got = swap(over_second, second), swap(over_third, third)
        keep, low = fold(last_fold_kernel, few, (few,), [keep, *got], [states[2]])
        got = swap(low, first)
        for bits in levels[:-3][::-1]:
            few //= 2
            keep, low = fold(fold_kernel, few, (few,), [keep, got], [])
            got = swap(low, bits)

        grad_tokens, grad_logits = call(
            home_kernel,
            [((count, width), BF16), ((experts, count), F32)],
            [keep, got, select, base, coef],
            1 << 20,
            1 << 18,
        )
        return (
            grad_gate,
            grad_up,
            grad_down,
            grad_tokens,
            grad_logits.T,
            entropy.reshape(count),
            divergence.reshape(count),
        )

    return shards


def solution(mesh):
    in_specs = (
        P(("grp", "blk"), None),
        P(("grp", "blk"), None),
        P(None, "blk"),
        P(None, "blk"),
        P("blk", None),
        P(("grp", "blk"), None),
        P(("grp", "blk"), None),
        P(("grp", "blk"), None),
    )
    out_specs = (
        P("grp", "blk"),
        P("grp", "blk"),
        P(("grp", "blk"), None),
        P(("grp", "blk"), None),
        P(("grp", "blk"), None),
        P(("grp", "blk")),
        P(("grp", "blk")),
    )
    return jax.shard_map(
        make_shards(mesh.shape["blk"]),
        mesh=mesh,
        in_specs=in_specs,
        out_specs=out_specs,
        check_vma=False,
    )
```

```python
import functools

import jax
import jax.numpy as jnp
from jax import lax
from jax.experimental import pallas as pl
from jax.experimental.pallas import tpu as pltpu
from jax.sharding import PartitionSpec as P

F32 = jnp.float32
BF16 = jnp.bfloat16
LANES = 128
MIB = 1 << 20


def dot(left, right, dims):
    return lax.dot_general(left, right, (dims, ((), ())), preferred_element_type=F32)


def whole(count):
    return [pl.BlockSpec(memory_space=pltpu.VMEM)] * count


def call(kernel, outs, args, flops, moved, limit=8):
    return pl.pallas_call(
        kernel,
        out_shape=[jax.ShapeDtypeStruct(s, t) for s, t in outs],
        in_specs=whole(len(args)),
        out_specs=whole(len(outs)),
        compiler_params=pltpu.CompilerParams(vmem_limit_bytes=limit * MIB),
        cost_estimate=pl.CostEstimate(flops=flops, bytes_accessed=moved, transcendentals=0),
    )(*args)


def in_hbm(array):
    return pltpu.with_memory_space_constraint(array, pltpu.HBM)


def in_vmem(array):
    return pltpu.with_memory_space_constraint(array, pltpu.VMEM)


def lane_pair(rows, first, second):
    lane = lax.broadcasted_iota(jnp.int32, (rows, LANES), 1)
    return jnp.where(lane == 0, first, jnp.where(lane == 1, second, 0.0))


def split_pair(value):
    high = value.astype(BF16).astype(F32)
    return lane_pair(value.shape[0], high, value - high)


def router_kernel(
    tokens_in,
    logits_in,
    ref_in,
    routes_in,
    y_in,
    send,
    entropy,
    divergence,
    base,
    coef,
    select_out,
    tokens,
    logits,
    ref_logits,
    routes,
    y,
    sems,
):
    sources = (logits_in, ref_in, routes_in, tokens_in, y_in)
    targets = (logits, ref_logits, routes, tokens, y)
    copies = [
        pltpu.make_async_copy(s, t, sems.at[i]) for i, (s, t) in enumerate(zip(sources, targets))
    ]
    for copy in copies:
        copy.start()
    for copy in copies[:3]:
        copy.wait()
    slots, width = send.shape[0], tokens.shape[1]
    experts, count = logits.shape
    x, r = logits[...], ref_logits[...]
    shifted = x - jnp.max(x, axis=0, keepdims=True)
    policy_log = shifted - jnp.log(jnp.sum(jnp.exp(shifted), axis=0, keepdims=True))
    shifted = r - jnp.max(r, axis=0, keepdims=True)
    frozen_log = shifted - jnp.log(jnp.sum(jnp.exp(shifted), axis=0, keepdims=True))
    probs = jnp.exp(policy_log)
    ratio = policy_log - frozen_log
    div = jnp.sum(probs * ratio, axis=0, keepdims=True)
    entropy[...] = -jnp.sum(probs * policy_log, axis=0, keepdims=True)
    divergence[...] = div
    base[...] = probs * (ratio - div)
    first, second = routes[0:1, :], routes[1:2, :]
    routed = jnp.where((first == 0) | (second == 0), 1.0, 0.0)
    expert = lax.broadcasted_iota(jnp.int32, (experts, count), 0)
    partner_hot = jnp.where(expert == first + second, 1.0, 0.0)
    partner_logit = jnp.sum(x * partner_hot, axis=0, keepdims=True)
    gate = jnp.where(routed > 0.0, jax.nn.sigmoid(x[0:1, :] - partner_logit), 0.0)
    coef[...] = (jnp.where(expert == 0, 1.0, 0.0) - partner_hot) * (gate * (1.0 - gate))
    token = lax.broadcasted_iota(jnp.int32, (1, count), 1)
    position = jnp.full((1, count), -1.0, F32)
    for t in range(count):
        position += jnp.where(token >= t, routed[:, t : t + 1], 0.0)
    slot = lax.broadcasted_iota(jnp.int32, (count, count), 0)
    hit = (slot == position.astype(jnp.int32)) & (routed > 0.0) & (slot < slots)
    select = jnp.where(hit, 1.0, 0.0)
    select_out[...] = select
    gate_low = gate.astype(BF16).astype(F32)
    g_slots = jnp.sum(select * gate_low, axis=1, keepdims=True)
    wide = width + LANES
    send[:, width:wide] = jnp.broadcast_to(g_slots[:slots], (slots, LANES)).astype(BF16)
    copies[3].wait()
    x_slots = dot(select.astype(BF16), tokens[...], ((1,), (0,)))
    send[:, :width] = x_slots[:slots].astype(BF16)
    copies[4].wait()
    send[:, wide:] = y[...]


def fetch_copies(sources, targets, sems):
    parts = sems.shape[1]
    copies = []
    for k, ((source, row), target) in enumerate(zip(sources, targets)):
        step = target.shape[0] // parts
        for i in range(parts):
            copies.append(
                pltpu.make_async_copy(
                    source.at[pl.ds(row + i * step, step)],
                    target.at[pl.ds(i * step, step)],
                    sems.at[k, i],
                )
            )
    return copies


def fetch_kernel(count, *refs):
    sources, targets, sems = refs[:count], refs[count + 1 : -1], refs[-1]
    copies = fetch_copies([(source, 0) for source in sources], targets, sems)
    for copy in copies:
        copy.start()
    for copy in copies:
        copy.wait()


def fetch(weights, rows, after):
    anywhere = pl.BlockSpec(memory_space=pl.ANY)
    count = len(weights)
    out = pl.pallas_call(
        functools.partial(fetch_kernel, count),
        out_shape=[pltpu.VMEM((r, w.shape[1]), w.dtype) for w, r in zip(weights, rows)],
        in_specs=[anywhere] * (count + 1),
        out_specs=whole(count),
        scratch_shapes=[pltpu.SemaphoreType.DMA((count, 4))],
        compiler_params=pltpu.CompilerParams(vmem_limit_bytes=8 * MIB),
        cost_estimate=pl.CostEstimate(
            flops=0, bytes_accessed=2 * sum(w.size for w in weights), transcendentals=0
        ),
    )(*[in_hbm(w) for w in weights], after)
    return [in_vmem(w) for w in out]


def relay_kernel(block, *refs):
    refs[-1][...] = block[...]


def relay(block, *after):
    return pl.pallas_call(
        relay_kernel,
        out_shape=jax.ShapeDtypeStruct(block.shape, block.dtype),
        in_specs=whole(1) + [pl.BlockSpec(memory_space=pl.ANY)] * len(after),
        out_specs=whole(1)[0],
        compiler_params=pltpu.CompilerParams(vmem_limit_bytes=8 * MIB),
        cost_estimate=pl.CostEstimate(
            flops=0, bytes_accessed=4 * block.size, transcendentals=0
        ),
    )(block, *after)


def expert_kernel(*refs):
    pieces, (down_in, gate_w, up_w), refs = refs[:6], refs[6:9], refs[9:]
    send, keep, weighted_t, d_both, x_t, y, x, down_w, sems = refs
    rows, width, hidden_dim = x.shape[0], gate_w.shape[0], gate_w.shape[1]
    wide = width + LANES
    half = rows // 2
    copies = fetch_copies([(down_in, 0)], [down_w], sems)
    for copy in copies:
        copy.start()
    for c in range(0, wide, LANES):
        at = pl.ds(c, LANES)
        block = jnp.concatenate([ref[:, at].astype(F32) for ref in pieces])
        x[:, at] = block.astype(BF16)
        if c < width:
            x_t[at, :] = block.T.astype(BF16)
    for c in range(0, width, LANES):
        parts = [ref[:, wide + c : wide + c + LANES].astype(F32) for ref in pieces]
        y[:, c : c + LANES] = jnp.concatenate(parts).astype(BF16)
    pre_gate = dot(x[:, :width], gate_w[...], ((1,), (0,)))
    pre_up = dot(x[:, :width], up_w[...], ((1,), (0,)))
    for copy in copies:
        copy.wait()
    back = dot(y[...], down_w[...], ((1,), (1,)))
    g = x[:, width:][:, 0:1].astype(F32)
    sig = jax.nn.sigmoid(pre_gate)
    act = pre_gate * sig
    hidden = act * pre_up
    weighted_t[...] = (g * hidden).T.astype(BF16)
    products = jnp.sum(hidden * back, axis=1, keepdims=True)
    scaled = g * back
    d_both[:, :hidden_dim] = (
        scaled * pre_up * sig * (1.0 + pre_gate * (1.0 - sig))
    ).astype(BF16)
    d_both[:, hidden_dim:] = (scaled * act).astype(BF16)
    keep[:, width:] = lane_pair(half, products[:half], 0.0)
    send[:, width:] = split_pair(products[half:]).astype(BF16)
    wide = 1024
    for i in range(width // wide):
        at = pl.ds(i * wide, wide)
        part = dot(d_both[:, :hidden_dim], gate_w[at, :], ((1,), (1,)))
        part += dot(d_both[:, hidden_dim:], up_w[at, :], ((1,), (1,)))
        keep[:, at] = part[:half]
        send[:, at] = part[half:].astype(BF16)


def fold_kernel(have, got, keep, send):
    half = keep.shape[0]
    width = keep.shape[1] - LANES
    total = have[:, :width] + got[:, :width].astype(F32)
    keep[:, :width] = total[:half]
    send[:, :width] = total[half:].astype(BF16)
    tail = have[:, width:] + got[:, width:].astype(F32)
    value = tail[:, 0:1] + tail[:, 1:2]
    keep[:, width:] = lane_pair(half, value[:half], 0.0)
    send[:, width:] = split_pair(value[half:]).astype(BF16)


def home_kernel(have, got, select, base, coef, grad_tokens, grad_logits):
    slots = have.shape[0]
    width = have.shape[1] - LANES
    count = select.shape[0]
    total = (have[:, :width] + got[:, :width].astype(F32)).astype(BF16)
    padded = jnp.concatenate([total, jnp.zeros((count - slots, width), BF16)], axis=0)
    grad_tokens[...] = dot(select[...].astype(BF16), padded, ((0,), (0,))).astype(BF16)
    tail = have[:, width:] + got[:, width:].astype(F32)
    value = tail[:, 0:1] + tail[:, 1:2]
    token_products = jnp.sum(select[0:slots, :] * value, axis=0, keepdims=True)
    grad_logits[...] = base[...] + coef[...] * token_products


def tiles(out, left, right):
    tall = 128
    for c in range(0, right.shape[1], 256):
        for r in range(0, left.shape[0], tall):
            part = dot(left[r : r + tall], right[:, c : c + 256], ((1,), (0,)))
            out[r : r + tall, c : c + 256] = part.astype(BF16)


def loop(count, body):
    for i in range(count):
        body(i)


def late_copies(row, sources, targets, sems):
    step = sources[0].shape[0]
    return [
        pltpu.make_async_copy(source, target.at[pl.ds(row, step)], sems.at[k])
        for k, (source, target) in enumerate(zip(sources, targets))
    ]


def grads_kernel(first_row, last, x_t, d_both, *refs):
    left = refs[:2] if first_row else ()
    gate_buf, up_buf, sems = refs[-3:]
    outs = refs[-5:-3] if last else refs[-7:-5]
    kept = () if last else refs[-5:-3]
    chunks, step, cols = gate_buf.shape
    copies = late_copies(first_row - step, left, outs, sems.at[chunks]) if left else []
    for copy in copies:
        copy.start()
    for i in range(chunks if last else chunks + 1):
        at = pl.ds(first_row + i * step, step)
        for k, target in enumerate(outs):
            tile = (gate_buf, up_buf)[k].at[i] if i < chunks else kept[k]
            tiles(tile, x_t.at[at], d_both.at[:, pl.ds(k * cols, cols)])
            if i < chunks:
                copy = pltpu.make_async_copy(tile, target.at[at], sems.at[i, k])
                copy.start()
                copies.append(copy)
    for copy in copies:
        copy.wait()


def first_kernel(weighted_t, y, x_t, d_both, down_out, *refs):
    down_buf, down_sems = refs[4:6]
    chunks, _, step = down_buf.shape
    copies = []
    for i in range(chunks):
        at = pl.ds(i * step, step)
        tiles(down_buf.at[i], weighted_t, y.at[:, at])
        copies.append(pltpu.make_async_copy(down_buf.at[i], down_out.at[:, at], down_sems.at[i]))
        copies[i].start()
    grads_kernel(0, False, x_t, d_both, *refs[:4], *refs[6:])
    for copy in copies:
        copy.wait()


def grads_of(x_t, d_both, first_row, rows, before, down=()):
    width, slots = x_t.shape
    cols = d_both.shape[1] // 2
    step = 256
    last = first_row + rows == width
    chunks = rows // step - (0 if last else 1)
    anywhere = pl.BlockSpec(memory_space=pl.ANY)
    outs = [jax.ShapeDtypeStruct((width, cols), BF16)] * 2
    outs += [] if last else [jax.ShapeDtypeStruct((step, cols), BF16)] * 2
    out_specs = [anywhere] * 2 + whole(len(outs) - 2)
    scratch = [
        pltpu.VMEM((chunks, step, cols), BF16),
        pltpu.VMEM((chunks, step, cols), BF16),
        pltpu.SemaphoreType.DMA((chunks + 1, 2)),
    ]
    kernel = functools.partial(grads_kernel, first_row, last)
    if down:
        kernel = first_kernel
        wide = 1024
        outs = [jax.ShapeDtypeStruct((cols, width), BF16)] + outs
        out_specs = [anywhere] + out_specs
        scratch = [
            pltpu.VMEM((width // wide, cols, wide), BF16),
            pltpu.SemaphoreType.DMA((width // wide,)),
        ] + scratch
    elements = 2 * rows * cols + (width * cols if down else 0)
    return pl.pallas_call(
        kernel,
        out_shape=outs,
        in_specs=whole(2 + len(down)) + (whole(2) + [anywhere] * 2 if before else []),
        out_specs=out_specs,
        scratch_shapes=scratch,
        input_output_aliases={4: 0, 5: 1} if before else {},
        compiler_params=pltpu.CompilerParams(vmem_limit_bytes=20 * MIB),
        cost_estimate=pl.CostEstimate(
            flops=8 * slots * elements, bytes_accessed=2 * elements, transcendentals=0
        ),
    )(*down, x_t, d_both, *before[2:], *before[:2])


def make_shards(n):
    levels = []
    bit = n // 2
    while bit > 4:
        levels.append((bit, bit))
        bit //= 2
    levels += [(4, 2), (2, 4)]

    def swap(block, bits):
        return lax.ppermute(block, "blk", [(i, i ^ bits[i % 2]) for i in range(n)])

    def shards(
        tokens, cotangent, gate_weight, up_weight, down_weight, logits, ref_logits, routes
    ):
        count, width = tokens.shape
        slots = cotangent.shape[0]
        experts = logits.shape[1]
        hidden = down_weight.shape[0]
        rows = n * slots
        wide = width + LANES
        anywhere = pl.BlockSpec(memory_space=pl.ANY)

        send, entropy, divergence, base, coef, select = pl.pallas_call(
            router_kernel,
            out_shape=[
                jax.ShapeDtypeStruct((slots, wide + width), BF16),
                jax.ShapeDtypeStruct((1, count), F32),
                jax.ShapeDtypeStruct((1, count), F32),
                jax.ShapeDtypeStruct((experts, count), F32),
                jax.ShapeDtypeStruct((experts, count), F32),
                jax.ShapeDtypeStruct((count, count), F32),
            ],
            in_specs=[anywhere] * 5,
            out_specs=whole(6),
            scratch_shapes=[
                pltpu.VMEM((count, width), BF16),
                pltpu.VMEM((experts, count), F32),
                pltpu.VMEM((experts, count), F32),
                pltpu.VMEM((2, count), jnp.int32),
                pltpu.VMEM((slots, width), BF16),
                pltpu.SemaphoreType.DMA((5,)),
            ],
            compiler_params=pltpu.CompilerParams(vmem_limit_bytes=8 * MIB),
            cost_estimate=pl.CostEstimate(
                flops=1 << 20, bytes_accessed=1 << 24, transcendentals=0
            ),
        )(*[in_hbm(a) for a in (tokens, logits.T, ref_logits.T, routes.T, cotangent)])

        own = send
        for bits in levels[:-3]:
            own = jnp.concatenate([own, swap(own, bits)])
        first, second, third = levels[-3:]
        block_1 = swap(own, first)
        block_2 = swap(own, second)
        block_3 = swap(own, third)
        gate_w, up_w = fetch([gate_weight, up_weight], [width, width], own)
        block_1 = relay(block_1, gate_w, block_2)
        block_12 = swap(block_1, second)
        block_13 = swap(block_1, third)
        block_23 = swap(block_3, second)
        block_123 = swap(block_12, third)
        pieces = [
            jnp.concatenate([own, block_1, block_2, block_12]),
            jnp.concatenate([block_3, block_13]),
            jnp.concatenate([block_23, block_123]),
        ]
        pieces += [swap(piece, (1, 1)) for piece in pieces]

        work = 2 * rows * width * hidden
        half = rows // 2
        low, keep, weighted_t, d_both, x_t, y_all = pl.pallas_call(
            expert_kernel,
            out_shape=[
                jax.ShapeDtypeStruct((half, wide), BF16),
                jax.ShapeDtypeStruct((half, wide), F32),
                jax.ShapeDtypeStruct((hidden, rows), BF16),
                jax.ShapeDtypeStruct((rows, 2 * hidden), BF16),
                jax.ShapeDtypeStruct((width, rows), BF16),
                jax.ShapeDtypeStruct((rows, width), BF16),
            ],
            in_specs=whole(6) + [anywhere] + whole(2),
            out_specs=whole(6),
            scratch_shapes=[
                pltpu.VMEM((rows, wide), BF16),
                pltpu.VMEM((hidden, width), BF16),
                pltpu.SemaphoreType.DMA((1, 4)),
            ],
            compiler_params=pltpu.CompilerParams(vmem_limit_bytes=24 * MIB),
            cost_estimate=pl.CostEstimate(
                flops=16 * work, bytes_accessed=4 * width * hidden, transcendentals=0
            ),
        )(*pieces, in_hbm(down_weight), gate_w, up_w)

        for bits in [(1, 1)] + levels[::-1]:
            got = swap(low, bits)
            if bits == levels[0]:
                break
            half //= 2
            keep, low = call(
                fold_kernel,
                [((half, wide), F32), ((half, wide), BF16)],
                [keep, got],
                4 * half * wide,
                16 * half * wide,
            )

        cuts = [0, width // 3, 2 * width // 3, width]
        grad_down, *pair = grads_of(x_t, d_both, 0, cuts[1], (), (weighted_t, y_all))
        for start, stop in zip(cuts[1:], cuts[2:]):
            pair = grads_of(x_t, d_both, start, stop - start, tuple(pair))
        grad_gate, grad_up = pair

        grad_tokens, grad_logits = call(
            home_kernel,
            [((count, width), BF16), ((experts, count), F32)],
            [keep, got, select, base, coef],
            1 << 20,
            1 << 18,
        )
        return (
            grad_gate,
            grad_up,
            grad_down,
            grad_tokens,
            grad_logits.T,
            entropy.reshape(count),
            divergence.reshape(count),
        )

    return shards


def solution(mesh):
    in_specs = (
        P(("grp", "blk"), None),
        P(("grp", "blk"), None),
        P(None, "blk"),
        P(None, "blk"),
        P("blk", None),
        P(("grp", "blk"), None),
        P(("grp", "blk"), None),
        P(("grp", "blk"), None),
    )
    out_specs = (
        P("grp", "blk"),
        P("grp", "blk"),
        P(("grp", "blk"), None),
        P(("grp", "blk"), None),
        P(("grp", "blk"), None),
        P(("grp", "blk")),
        P(("grp", "blk")),
    )
    return jax.shard_map(
        make_shards(mesh.shape["blk"]),
        mesh=mesh,
        in_specs=in_specs,
        out_specs=out_specs,
        check_vma=False,
    )
```

```python
import functools

import jax
import jax.numpy as jnp
from jax import lax
from jax.experimental import pallas as pl
from jax.experimental.pallas import tpu as pltpu
from jax.sharding import PartitionSpec as P

F32 = jnp.float32
BF16 = jnp.bfloat16
LANES = 128
MIB = 1 << 20


def dot(left, right, dims):
    return lax.dot_general(left, right, (dims, ((), ())), preferred_element_type=F32)


def whole(count):
    return [pl.BlockSpec(memory_space=pltpu.VMEM)] * count


def call(kernel, outs, args, flops, moved, limit=8):
    return pl.pallas_call(
        kernel,
        out_shape=[jax.ShapeDtypeStruct(s, t) for s, t in outs],
        in_specs=whole(len(args)),
        out_specs=whole(len(outs)),
        compiler_params=pltpu.CompilerParams(vmem_limit_bytes=limit * MIB),
        cost_estimate=pl.CostEstimate(flops=flops, bytes_accessed=moved, transcendentals=0),
    )(*args)


def in_hbm(array):
    return pltpu.with_memory_space_constraint(array, pltpu.HBM)


def in_vmem(array):
    return pltpu.with_memory_space_constraint(array, pltpu.VMEM)


def lane_pair(rows, first, second):
    lane = lax.broadcasted_iota(jnp.int32, (rows, LANES), 1)
    return jnp.where(lane == 0, first, jnp.where(lane == 1, second, 0.0))


def split_pair(value):
    high = value.astype(BF16).astype(F32)
    return lane_pair(value.shape[0], high, value - high)


def router_kernel(
    tokens_in,
    logits_in,
    ref_in,
    routes_in,
    y_in,
    send,
    entropy,
    divergence,
    base,
    coef,
    select_out,
    tokens,
    logits,
    ref_logits,
    routes,
    y,
    sems,
):
    sources = (logits_in, ref_in, routes_in, tokens_in, y_in)
    targets = (logits, ref_logits, routes, tokens, y)
    copies = [
        pltpu.make_async_copy(s, t, sems.at[i]) for i, (s, t) in enumerate(zip(sources, targets))
    ]
    for copy in copies:
        copy.start()
    for copy in copies[:3]:
        copy.wait()
    slots, width = send.shape[0], tokens.shape[1]
    experts, count = logits.shape
    x, r = logits[...], ref_logits[...]
    shifted = x - jnp.max(x, axis=0, keepdims=True)
    policy_log = shifted - jnp.log(jnp.sum(jnp.exp(shifted), axis=0, keepdims=True))
    shifted = r - jnp.max(r, axis=0, keepdims=True)
    frozen_log = shifted - jnp.log(jnp.sum(jnp.exp(shifted), axis=0, keepdims=True))
    probs = jnp.exp(policy_log)
    ratio = policy_log - frozen_log
    div = jnp.sum(probs * ratio, axis=0, keepdims=True)
    entropy[...] = -jnp.sum(probs * policy_log, axis=0, keepdims=True)
    divergence[...] = div
    base[...] = probs * (ratio - div)
    first, second = routes[0:1, :], routes[1:2, :]
    routed = jnp.where((first == 0) | (second == 0), 1.0, 0.0)
    expert = lax.broadcasted_iota(jnp.int32, (experts, count), 0)
    partner_hot = jnp.where(expert == first + second, 1.0, 0.0)
    partner_logit = jnp.sum(x * partner_hot, axis=0, keepdims=True)
    gate = jnp.where(routed > 0.0, jax.nn.sigmoid(x[0:1, :] - partner_logit), 0.0)
    coef[...] = (jnp.where(expert == 0, 1.0, 0.0) - partner_hot) * (gate * (1.0 - gate))
    token = lax.broadcasted_iota(jnp.int32, (1, count), 1)
    position = jnp.full((1, count), -1.0, F32)
    for t in range(count):
        position += jnp.where(token >= t, routed[:, t : t + 1], 0.0)
    slot = lax.broadcasted_iota(jnp.int32, (count, count), 0)
    hit = (slot == position.astype(jnp.int32)) & (routed > 0.0) & (slot < slots)
    select = jnp.where(hit, 1.0, 0.0)
    select_out[...] = select
    gate_low = gate.astype(BF16).astype(F32)
    g_slots = jnp.sum(select * gate_low, axis=1, keepdims=True)
    wide = width + LANES
    send[:, width:wide] = jnp.broadcast_to(g_slots[:slots], (slots, LANES)).astype(BF16)
    copies[3].wait()
    x_slots = dot(select.astype(BF16), tokens[...], ((1,), (0,)))
    send[:, :width] = x_slots[:slots].astype(BF16)
    copies[4].wait()
    send[:, wide:] = y[...]


def fetch_copies(sources, targets, sems):
    parts = sems.shape[1]
    copies = []
    for k, (source, target) in enumerate(zip(sources, targets)):
        step = source.shape[0] // parts
        for i in range(parts):
            at = pl.ds(i * step, step)
            copies.append(pltpu.make_async_copy(source.at[at], target.at[at], sems.at[k, i]))
    return copies


def fetch_kernel(source, after, target, sems):
    copies = fetch_copies([source], [target], sems)
    for copy in copies:
        copy.start()
    for copy in copies:
        copy.wait()


def fetch(weight, after):
    anywhere = pl.BlockSpec(memory_space=pl.ANY)
    out = pl.pallas_call(
        fetch_kernel,
        out_shape=pltpu.VMEM(weight.shape, weight.dtype),
        in_specs=[anywhere] * 2,
        out_specs=whole(1)[0],
        scratch_shapes=[pltpu.SemaphoreType.DMA((1, 4))],
        compiler_params=pltpu.CompilerParams(vmem_limit_bytes=8 * MIB),
        cost_estimate=pl.CostEstimate(
            flops=0, bytes_accessed=2 * weight.size, transcendentals=0
        ),
    )(in_hbm(weight), after)
    return in_vmem(out)


def relay_kernel(block, *refs):
    refs[-1][...] = block[...]


def relay(block, *after):
    return pl.pallas_call(
        relay_kernel,
        out_shape=jax.ShapeDtypeStruct(block.shape, block.dtype),
        in_specs=whole(1) + [pl.BlockSpec(memory_space=pl.ANY)] * len(after),
        out_specs=whole(1)[0],
        compiler_params=pltpu.CompilerParams(vmem_limit_bytes=8 * MIB),
        cost_estimate=pl.CostEstimate(
            flops=0, bytes_accessed=4 * MIB, transcendentals=0
        ),
    )(block, *after)


def expert_kernel(*refs):
    pieces, (up_in, gate_w, down_w), refs = refs[:4], refs[4:7], refs[7:]
    send, keep, weighted_t, d_both, x_t, y, x, up_w, sems = refs
    rows, width, hidden_dim = x.shape[0], gate_w.shape[0], gate_w.shape[1]
    wide = width + LANES
    half = rows // 2
    copies = fetch_copies([up_in], [up_w], sems)
    for copy in copies:
        copy.start()
    for c in range(0, wide, LANES):
        at = pl.ds(c, LANES)
        block = jnp.concatenate([ref[:, at].astype(F32) for ref in pieces])
        x[:, at] = block.astype(BF16)
        if c < width:
            x_t[at, :] = block.T.astype(BF16)
    quarter = rows // 4
    for i, ref in enumerate(pieces):
        y[i * quarter : (i + 1) * quarter, :] = ref[:, wide:]
    pre_gate = dot(x[:, :width], gate_w[...], ((1,), (0,)))
    back = dot(y[...], down_w[...], ((1,), (1,)))
    for copy in copies:
        copy.wait()
    pre_up = dot(x[:, :width], up_w[...], ((1,), (0,)))
    g = x[:, width:][:, 0:1].astype(F32)
    sig = jax.nn.sigmoid(pre_gate)
    act = pre_gate * sig
    hidden = act * pre_up
    weighted_t[...] = (g * hidden).T.astype(BF16)
    products = jnp.sum(hidden * back, axis=1, keepdims=True)
    scaled = g * back
    d_both[:, :hidden_dim] = (
        scaled * pre_up * sig * (1.0 + pre_gate * (1.0 - sig))
    ).astype(BF16)
    d_both[:, hidden_dim:] = (scaled * act).astype(BF16)
    keep[:, width:] = lane_pair(half, products[:half], 0.0)
    send[:, width:] = split_pair(products[half:]).astype(BF16)
    wide = 1024
    for i in range(width // wide):
        at = pl.ds(i * wide, wide)
        part = dot(d_both[:, :hidden_dim], gate_w[at, :], ((1,), (1,)))
        part += dot(d_both[:, hidden_dim:], up_w[at, :], ((1,), (1,)))
        keep[:, at] = part[:half]
        send[:, at] = part[half:].astype(BF16)


def fold_kernel(have, got, keep, send):
    half = keep.shape[0]
    width = keep.shape[1] - LANES
    total = have[:, :width] + got[:, :width].astype(F32)
    keep[:, :width] = total[:half]
    send[:, :width] = total[half:].astype(BF16)
    tail = have[:, width:] + got[:, width:].astype(F32)
    value = tail[:, 0:1] + tail[:, 1:2]
    keep[:, width:] = lane_pair(half, value[:half], 0.0)
    send[:, width:] = split_pair(value[half:]).astype(BF16)


def home_kernel(have, got, select, base, coef, grad_tokens, grad_logits):
    slots = have.shape[0]
    width = have.shape[1] - LANES
    count = select.shape[0]
    total = (have[:, :width] + got[:, :width].astype(F32)).astype(BF16)
    padded = jnp.concatenate([total, jnp.zeros((count - slots, width), BF16)], axis=0)
    grad_tokens[...] = dot(select[...].astype(BF16), padded, ((0,), (0,))).astype(BF16)
    tail = have[:, width:] + got[:, width:].astype(F32)
    value = tail[:, 0:1] + tail[:, 1:2]
    token_products = jnp.sum(select[0:slots, :] * value, axis=0, keepdims=True)
    grad_logits[...] = base[...] + coef[...] * token_products


def tiles(out, left, right):
    tall = 128
    for c in range(0, right.shape[1], 256):
        for r in range(0, left.shape[0], tall):
            part = dot(left[r : r + tall], right[:, c : c + 256], ((1,), (0,)))
            out[r : r + tall, c : c + 256] = part.astype(BF16)


def loop(count, body):
    for i in range(count):
        body(i)


def late_copies(row, sources, targets, sems):
    step = sources[0].shape[0]
    return [
        pltpu.make_async_copy(source, target.at[pl.ds(row, step)], sems.at[k])
        for k, (source, target) in enumerate(zip(sources, targets))
    ]


def grads_kernel(first_row, last, x_t, d_both, *refs):
    left = refs[:2] if first_row else ()
    gate_buf, up_buf, sems = refs[-3:]
    outs = refs[-5:-3] if last else refs[-7:-5]
    kept = () if last else refs[-5:-3]
    chunks, step, cols = gate_buf.shape
    copies = late_copies(first_row - step, left, outs, sems.at[chunks]) if left else []
    for copy in copies:
        copy.start()
    for i in range(chunks if last else chunks + 1):
        at = pl.ds(first_row + i * step, step)
        for k, target in enumerate(outs):
            tile = (gate_buf, up_buf)[k].at[i] if i < chunks else kept[k]
            tiles(tile, x_t.at[at], d_both.at[:, pl.ds(k * cols, cols)])
            if i < chunks:
                copy = pltpu.make_async_copy(tile, target.at[at], sems.at[i, k])
                copy.start()
                copies.append(copy)
    for copy in copies:
        copy.wait()


def first_kernel(weighted_t, y, x_t, d_both, down_out, *refs):
    down_buf, down_sems = refs[4:6]
    chunks, _, step = down_buf.shape
    copies = []
    for i in range(chunks):
        at = pl.ds(i * step, step)
        tiles(down_buf.at[i], weighted_t, y.at[:, at])
        copies.append(pltpu.make_async_copy(down_buf.at[i], down_out.at[:, at], down_sems.at[i]))
        copies[i].start()
    grads_kernel(0, False, x_t, d_both, *refs[:4], *refs[6:])
    for copy in copies:
        copy.wait()


def grads_of(x_t, d_both, first_row, rows, before, down=()):
    width, slots = x_t.shape
    cols = d_both.shape[1] // 2
    step = 256
    last = first_row + rows == width
    chunks = rows // step - (0 if last else 1)
    anywhere = pl.BlockSpec(memory_space=pl.ANY)
    outs = [jax.ShapeDtypeStruct((width, cols), BF16)] * 2
    outs += [] if last else [jax.ShapeDtypeStruct((step, cols), BF16)] * 2
    out_specs = [anywhere] * 2 + whole(len(outs) - 2)
    scratch = [
        pltpu.VMEM((chunks, step, cols), BF16),
        pltpu.VMEM((chunks, step, cols), BF16),
        pltpu.SemaphoreType.DMA((chunks + 1, 2)),
    ]
    kernel = functools.partial(grads_kernel, first_row, last)
    if down:
        kernel = first_kernel
        wide = 1024
        outs = [jax.ShapeDtypeStruct((cols, width), BF16)] + outs
        out_specs = [anywhere] + out_specs
        scratch = [
            pltpu.VMEM((width // wide, cols, wide), BF16),
            pltpu.SemaphoreType.DMA((width // wide,)),
        ] + scratch
    elements = 2 * rows * cols + (width * cols if down else 0)
    return pl.pallas_call(
        kernel,
        out_shape=outs,
        in_specs=whole(2 + len(down)) + (whole(2) + [anywhere] * 2 if before else []),
        out_specs=out_specs,
        scratch_shapes=scratch,
        input_output_aliases={4: 0, 5: 1} if before else {},
        compiler_params=pltpu.CompilerParams(vmem_limit_bytes=20 * MIB),
        cost_estimate=pl.CostEstimate(
            flops=8 * slots * elements, bytes_accessed=2 * elements, transcendentals=0
        ),
    )(*down, x_t, d_both, *before[2:], *before[:2])


def make_shards(n):
    levels = []
    bit = n // 2
    while bit > 4:
        levels.append((bit, bit))
        bit //= 2
    levels += [(4, 2), (2, 4)]

    def swap(block, bits):
        return lax.ppermute(block, "blk", [(i, i ^ bits[i % 2]) for i in range(n)])

    def shards(
        tokens, cotangent, gate_weight, up_weight, down_weight, logits, ref_logits, routes
    ):
        count, width = tokens.shape
        slots = cotangent.shape[0]
        experts = logits.shape[1]
        hidden = down_weight.shape[0]
        rows = n * slots
        wide = width + LANES
        anywhere = pl.BlockSpec(memory_space=pl.ANY)

        send, entropy, divergence, base, coef, select = pl.pallas_call(
            router_kernel,
            out_shape=[
                jax.ShapeDtypeStruct((slots, wide + width), BF16),
                jax.ShapeDtypeStruct((1, count), F32),
                jax.ShapeDtypeStruct((1, count), F32),
                jax.ShapeDtypeStruct((experts, count), F32),
                jax.ShapeDtypeStruct((experts, count), F32),
                jax.ShapeDtypeStruct((count, count), F32),
            ],
            in_specs=[anywhere] * 5,
            out_specs=whole(6),
            scratch_shapes=[
                pltpu.VMEM((count, width), BF16),
                pltpu.VMEM((experts, count), F32),
                pltpu.VMEM((experts, count), F32),
                pltpu.VMEM((2, count), jnp.int32),
                pltpu.VMEM((slots, width), BF16),
                pltpu.SemaphoreType.DMA((5,)),
            ],
            compiler_params=pltpu.CompilerParams(vmem_limit_bytes=8 * MIB),
            cost_estimate=pl.CostEstimate(
                flops=1 << 20, bytes_accessed=1 << 24, transcendentals=0
            ),
        )(*[in_hbm(a) for a in (tokens, logits.T, ref_logits.T, routes.T, cotangent)])

        own = send
        for bits in levels[:-3]:
            own = jnp.concatenate([own, swap(own, bits)])
        first, second, third = levels[-3:]
        block_1 = relay(relay(swap(own, first)))
        block_2 = swap(own, second)
        block_3 = swap(own, third)
        gate_w = fetch(gate_weight, own)
        block_1 = relay(block_1, gate_w, block_2, block_3)
        block_12 = swap(block_1, second)
        again = relay(block_1)
        block_13 = swap(again, third)
        down_w = fetch(down_weight, again)
        block_12 = relay(block_12, down_w)
        block_123 = relay(swap(block_12, third))
        block_23 = swap(relay(block_3, block_12), second)
        low_half = jnp.concatenate([own, block_1, block_2, block_12])
        high_half = jnp.concatenate([block_3, block_13, block_23, block_123])
        pieces = [low_half, high_half]
        pieces += [swap(piece, (1, 1)) for piece in pieces]

        work = 2 * rows * width * hidden
        half = rows // 2
        low, keep, weighted_t, d_both, x_t, y_all = pl.pallas_call(
            expert_kernel,
            out_shape=[
                jax.ShapeDtypeStruct((half, wide), BF16),
                jax.ShapeDtypeStruct((half, wide), F32),
                jax.ShapeDtypeStruct((hidden, rows), BF16),
                jax.ShapeDtypeStruct((rows, 2 * hidden), BF16),
                jax.ShapeDtypeStruct((width, rows), BF16),
                jax.ShapeDtypeStruct((rows, width), BF16),
            ],
            in_specs=whole(4) + [anywhere] + whole(2),
            out_specs=whole(6),
            scratch_shapes=[
                pltpu.VMEM((rows, wide), BF16),
                pltpu.VMEM((width, hidden), BF16),
                pltpu.SemaphoreType.DMA((1, 4)),
            ],
            compiler_params=pltpu.CompilerParams(vmem_limit_bytes=24 * MIB),
            cost_estimate=pl.CostEstimate(
                flops=16 * work, bytes_accessed=4 * width * hidden, transcendentals=0
            ),
        )(*pieces, in_hbm(up_weight), gate_w, down_w)

        for bits in [(1, 1)] + levels[::-1]:
            got = swap(low, bits)
            if bits == levels[0]:
                break
            half //= 2
            keep, low = call(
                fold_kernel,
                [((half, wide), F32), ((half, wide), BF16)],
                [keep, got],
                4 * half * wide,
                16 * half * wide,
            )

        cuts = [0, width // 3, 2 * width // 3, width]
        grad_down, *pair = grads_of(x_t, d_both, 0, cuts[1], (), (weighted_t, y_all))
        for start, stop in zip(cuts[1:], cuts[2:]):
            pair = grads_of(x_t, d_both, start, stop - start, tuple(pair))
        grad_gate, grad_up = pair

        grad_tokens, grad_logits = call(
            home_kernel,
            [((count, width), BF16), ((experts, count), F32)],
            [keep, got, select, base, coef],
            1 << 20,
            1 << 18,
        )
        return (
            grad_gate,
            grad_up,
            grad_down,
            grad_tokens,
            grad_logits.T,
            entropy.reshape(count),
            divergence.reshape(count),
        )

    return shards


def solution(mesh):
    in_specs = (
        P(("grp", "blk"), None),
        P(("grp", "blk"), None),
        P(None, "blk"),
        P(None, "blk"),
        P("blk", None),
        P(("grp", "blk"), None),
        P(("grp", "blk"), None),
        P(("grp", "blk"), None),
    )
    out_specs = (
        P("grp", "blk"),
        P("grp", "blk"),
        P(("grp", "blk"), None),
        P(("grp", "blk"), None),
        P(("grp", "blk"), None),
        P(("grp", "blk")),
        P(("grp", "blk")),
    )
    return jax.shard_map(
        make_shards(mesh.shape["blk"]),
        mesh=mesh,
        in_specs=in_specs,
        out_specs=out_specs,
        check_vma=False,
    )
```

```python
import functools

import jax
import jax.numpy as jnp
from jax import lax
from jax.experimental import pallas as pl
from jax.experimental.pallas import tpu as pltpu
from jax.sharding import PartitionSpec as P

F32 = jnp.float32
BF16 = jnp.bfloat16
LANES = 128
MIB = 1 << 20


def dot(left, right, dims):
    return lax.dot_general(left, right, (dims, ((), ())), preferred_element_type=F32)


def whole(count):
    return [pl.BlockSpec(memory_space=pltpu.VMEM)] * count


def call(kernel, outs, args, flops, moved, limit=8):
    return pl.pallas_call(
        kernel,
        out_shape=[jax.ShapeDtypeStruct(s, t) for s, t in outs],
        in_specs=whole(len(args)),
        out_specs=whole(len(outs)),
        compiler_params=pltpu.CompilerParams(vmem_limit_bytes=limit * MIB),
        cost_estimate=pl.CostEstimate(flops=flops, bytes_accessed=moved, transcendentals=0),
    )(*args)


def in_hbm(array):
    return pltpu.with_memory_space_constraint(array, pltpu.HBM)


def in_vmem(array):
    return pltpu.with_memory_space_constraint(array, pltpu.VMEM)


def lane_pair(rows, first, second):
    lane = lax.broadcasted_iota(jnp.int32, (rows, LANES), 1)
    return jnp.where(lane == 0, first, jnp.where(lane == 1, second, 0.0))


def split_pair(value):
    high = value.astype(BF16).astype(F32)
    return lane_pair(value.shape[0], high, value - high)


def start_all(sources, targets, sems):
    copies = [
        pltpu.make_async_copy(s, t, sems.at[i]) for i, (s, t) in enumerate(zip(sources, targets))
    ]
    for copy in copies:
        copy.start()
    return copies


def gates(logits, routes):
    first, second = routes[0:1, :], routes[1:2, :]
    routed = jnp.where((first == 0) | (second == 0), 1.0, 0.0)
    expert = lax.broadcasted_iota(jnp.int32, logits.shape, 0)
    partner_hot = jnp.where(expert == first + second, 1.0, 0.0)
    partner_logit = jnp.sum(logits * partner_hot, axis=0, keepdims=True)
    gate = jnp.where(routed > 0.0, jax.nn.sigmoid(logits[0:1, :] - partner_logit), 0.0)
    window_hot = jnp.where(expert == 0, 1.0, 0.0)
    return routed, gate, (window_hot - partner_hot) * (gate * (1.0 - gate))


def select_kernel(
    logits_in, routes_in, tokens_in, y_in, send, select_out, logits, routes, tokens, y, sems
):
    copies = start_all(
        (logits_in, routes_in, tokens_in, y_in), (logits, routes, tokens, y), sems
    )
    slots, width = send.shape[0], tokens.shape[1]
    count = logits.shape[1]
    for copy in copies[:2]:
        copy.wait()
    routed, gate, _ = gates(logits[...], routes[...])
    token = lax.broadcasted_iota(jnp.int32, (1, count), 1)
    position = jnp.full((1, count), -1.0, F32)
    for t in range(count):
        position += jnp.where(token >= t, routed[:, t : t + 1], 0.0)
    slot = lax.broadcasted_iota(jnp.int32, (count, count), 0)
    hit = (slot == position.astype(jnp.int32)) & (routed > 0.0) & (slot < slots)
    select = jnp.where(hit, 1.0, 0.0)
    select_out[...] = select
    gate_low = gate.astype(BF16).astype(F32)
    g_slots = jnp.sum(select * gate_low, axis=1, keepdims=True)
    wide = width + LANES
    send[:, width:wide] = jnp.broadcast_to(g_slots[:slots], (slots, LANES)).astype(BF16)
    for copy in copies[2:]:
        copy.wait()
    x_slots = dot(select.astype(BF16), tokens[...], ((1,), (0,)))
    send[:, :width] = x_slots[:slots].astype(BF16)
    send[:, wide:] = y[...]


def router_kernel(
    logits_in,
    ref_in,
    routes_in,
    after,
    entropy,
    divergence,
    base,
    coef,
    logits,
    ref_logits,
    routes,
    sems,
):
    copies = start_all((logits_in, ref_in, routes_in), (logits, ref_logits, routes), sems)
    for copy in copies:
        copy.wait()
    x, r = logits[...], ref_logits[...]
    shifted = x - jnp.max(x, axis=0, keepdims=True)
    policy_log = shifted - jnp.log(jnp.sum(jnp.exp(shifted), axis=0, keepdims=True))
    shifted = r - jnp.max(r, axis=0, keepdims=True)
    frozen_log = shifted - jnp.log(jnp.sum(jnp.exp(shifted), axis=0, keepdims=True))
    probs = jnp.exp(policy_log)
    ratio = policy_log - frozen_log
    div = jnp.sum(probs * ratio, axis=0, keepdims=True)
    entropy[...] = -jnp.sum(probs * policy_log, axis=0, keepdims=True)
    divergence[...] = div
    base[...] = probs * (ratio - div)
    coef[...] = gates(x, routes[...])[2]


def fetch_copies(sources, targets, sems):
    parts = sems.shape[1]
    copies = []
    for k, ((source, row), target) in enumerate(zip(sources, targets)):
        step = target.shape[0] // parts
        for i in range(parts):
            copies.append(
                pltpu.make_async_copy(
                    source.at[pl.ds(row + i * step, step)],
                    target.at[pl.ds(i * step, step)],
                    sems.at[k, i],
                )
            )
    return copies


def fetch_kernel(count, *refs):
    sources, targets, sems = refs[:count], refs[count + 1 : -1], refs[-1]
    copies = fetch_copies([(source, 0) for source in sources], targets, sems)
    for copy in copies:
        copy.start()
    for copy in copies:
        copy.wait()


def fetch(weights, rows, after):
    anywhere = pl.BlockSpec(memory_space=pl.ANY)
    count = len(weights)
    out = pl.pallas_call(
        functools.partial(fetch_kernel, count),
        out_shape=[pltpu.VMEM((r, w.shape[1]), w.dtype) for w, r in zip(weights, rows)],
        in_specs=[anywhere] * (count + 1),
        out_specs=whole(count),
        scratch_shapes=[pltpu.SemaphoreType.DMA((count, 4))],
        compiler_params=pltpu.CompilerParams(vmem_limit_bytes=8 * MIB),
        cost_estimate=pl.CostEstimate(
            flops=0, bytes_accessed=2 * sum(w.size for w in weights), transcendentals=0
        ),
    )(*[in_hbm(w) for w in weights], after)
    return [in_vmem(w) for w in out]


def relay_kernel(block, *refs):
    refs[-1][...] = block[...]


def relay(block, *after):
    return pl.pallas_call(
        relay_kernel,
        out_shape=jax.ShapeDtypeStruct(block.shape, block.dtype),
        in_specs=whole(1) + [pl.BlockSpec(memory_space=pl.ANY)] * len(after),
        out_specs=whole(1)[0],
        compiler_params=pltpu.CompilerParams(vmem_limit_bytes=8 * MIB),
        cost_estimate=pl.CostEstimate(
            flops=0, bytes_accessed=4 * MIB, transcendentals=0
        ),
    )(block, *after)


def expert_kernel(*refs):
    pieces, (down_in, gate_w, up_w), refs = refs[:4], refs[4:7], refs[7:]
    send, keep, weighted_t, d_both, x_t, y, x, down_w, sems = refs
    rows, width, hidden_dim = x.shape[0], gate_w.shape[0], gate_w.shape[1]
    wide = width + LANES
    half = rows // 2
    copies = fetch_copies([(down_in, 0)], [down_w], sems)
    for copy in copies:
        copy.start()
    for c in range(0, wide, LANES):
        at = pl.ds(c, LANES)
        block = jnp.concatenate([ref[:, at].astype(F32) for ref in pieces])
        x[:, at] = block.astype(BF16)
        if c < width:
            x_t[at, :] = block.T.astype(BF16)
    quarter = rows // 4
    for i, ref in enumerate(pieces):
        y[i * quarter : (i + 1) * quarter, :] = ref[:, wide:]
    pre_gate = dot(x[:, :width], gate_w[...], ((1,), (0,)))
    pre_up = dot(x[:, :width], up_w[...], ((1,), (0,)))
    for copy in copies:
        copy.wait()
    back = dot(y[...], down_w[...], ((1,), (1,)))
    g = x[:, width:][:, 0:1].astype(F32)
    sig = jax.nn.sigmoid(pre_gate)
    act = pre_gate * sig
    hidden = act * pre_up
    weighted_t[...] = (g * hidden).T.astype(BF16)
    products = jnp.sum(hidden * back, axis=1, keepdims=True)
    scaled = g * back
    d_both[:, :hidden_dim] = (
        scaled * pre_up * sig * (1.0 + pre_gate * (1.0 - sig))
    ).astype(BF16)
    d_both[:, hidden_dim:] = (scaled * act).astype(BF16)
    keep[:, width:] = lane_pair(half, products[:half], 0.0)
    send[:, width:] = split_pair(products[half:]).astype(BF16)
    wide = 1024
    for i in range(width // wide):
        at = pl.ds(i * wide, wide)
        part = dot(d_both[:, :hidden_dim], gate_w[at, :], ((1,), (1,)))
        part += dot(d_both[:, hidden_dim:], up_w[at, :], ((1,), (1,)))
        keep[:, at] = part[:half]
        send[:, at] = part[half:].astype(BF16)


def fold_kernel(have, got, keep, send):
    half = keep.shape[0]
    width = keep.shape[1] - LANES
    total = have[:, :width] + got[:, :width].astype(F32)
    keep[:, :width] = total[:half]
    send[:, :width] = total[half:].astype(BF16)
    tail = have[:, width:] + got[:, width:].astype(F32)
    value = tail[:, 0:1] + tail[:, 1:2]
    keep[:, width:] = lane_pair(half, value[:half], 0.0)
    send[:, width:] = split_pair(value[half:]).astype(BF16)


def home_kernel(have, got, select, base, coef, grad_tokens, grad_logits):
    slots = have.shape[0]
    width = have.shape[1] - LANES
    count = select.shape[0]
    total = (have[:, :width] + got[:, :width].astype(F32)).astype(BF16)
    padded = jnp.concatenate([total, jnp.zeros((count - slots, width), BF16)], axis=0)
    grad_tokens[...] = dot(select[...].astype(BF16), padded, ((0,), (0,))).astype(BF16)
    tail = have[:, width:] + got[:, width:].astype(F32)
    value = tail[:, 0:1] + tail[:, 1:2]
    token_products = jnp.sum(select[0:slots, :] * value, axis=0, keepdims=True)
    grad_logits[...] = base[...] + coef[...] * token_products


def tiles(out, left, right):
    tall = 128
    for c in range(0, right.shape[1], 256):
        for r in range(0, left.shape[0], tall):
            part = dot(left[r : r + tall], right[:, c : c + 256], ((1,), (0,)))
            out[r : r + tall, c : c + 256] = part.astype(BF16)


def loop(count, body):
    for i in range(count):
        body(i)


def late_copies(row, sources, targets, sems):
    step = sources[0].shape[0]
    return [
        pltpu.make_async_copy(source, target.at[pl.ds(row, step)], sems.at[k])
        for k, (source, target) in enumerate(zip(sources, targets))
    ]


def grads_kernel(first_row, last, x_t, d_both, *refs):
    left = refs[:2] if first_row else ()
    gate_buf, up_buf, sems = refs[-3:]
    outs = refs[-5:-3] if last else refs[-7:-5]
    kept = () if last else refs[-5:-3]
    chunks, step, cols = gate_buf.shape
    copies = late_copies(first_row - step, left, outs, sems.at[chunks]) if left else []
    for copy in copies:
        copy.start()
    for i in range(chunks if last else chunks + 1):
        at = pl.ds(first_row + i * step, step)
        for k, target in enumerate(outs):
            tile = (gate_buf, up_buf)[k].at[i] if i < chunks else kept[k]
            tiles(tile, x_t.at[at], d_both.at[:, pl.ds(k * cols, cols)])
            if i < chunks:
                copy = pltpu.make_async_copy(tile, target.at[at], sems.at[i, k])
                copy.start()
                copies.append(copy)
    for copy in copies:
        copy.wait()


def first_kernel(weighted_t, y, x_t, d_both, down_out, *refs):
    down_buf, down_sems = refs[4:6]
    chunks, _, step = down_buf.shape
    copies = []
    for i in range(chunks):
        at = pl.ds(i * step, step)
        tiles(down_buf.at[i], weighted_t, y.at[:, at])
        copies.append(pltpu.make_async_copy(down_buf.at[i], down_out.at[:, at], down_sems.at[i]))
        copies[i].start()
    grads_kernel(0, False, x_t, d_both, *refs[:4], *refs[6:])
    for copy in copies:
        copy.wait()


def grads_of(x_t, d_both, first_row, rows, before, down=()):
    width, slots = x_t.shape
    cols = d_both.shape[1] // 2
    step = 256
    last = first_row + rows == width
    chunks = rows // step - (0 if last else 1)
    anywhere = pl.BlockSpec(memory_space=pl.ANY)
    outs = [jax.ShapeDtypeStruct((width, cols), BF16)] * 2
    outs += [] if last else [jax.ShapeDtypeStruct((step, cols), BF16)] * 2
    out_specs = [anywhere] * 2 + whole(len(outs) - 2)
    scratch = [
        pltpu.VMEM((chunks, step, cols), BF16),
        pltpu.VMEM((chunks, step, cols), BF16),
        pltpu.SemaphoreType.DMA((chunks + 1, 2)),
    ]
    kernel = functools.partial(grads_kernel, first_row, last)
    if down:
        kernel = first_kernel
        wide = 1024
        outs = [jax.ShapeDtypeStruct((cols, width), BF16)] + outs
        out_specs = [anywhere] + out_specs
        scratch = [
            pltpu.VMEM((width // wide, cols, wide), BF16),
            pltpu.SemaphoreType.DMA((width // wide,)),
        ] + scratch
    elements = 2 * rows * cols + (width * cols if down else 0)
    return pl.pallas_call(
        kernel,
        out_shape=outs,
        in_specs=whole(2 + len(down)) + (whole(2) + [anywhere] * 2 if before else []),
        out_specs=out_specs,
        scratch_shapes=scratch,
        input_output_aliases={4: 0, 5: 1} if before else {},
        compiler_params=pltpu.CompilerParams(vmem_limit_bytes=20 * MIB),
        cost_estimate=pl.CostEstimate(
            flops=8 * slots * elements, bytes_accessed=2 * elements, transcendentals=0
        ),
    )(*down, x_t, d_both, *before[2:], *before[:2])


def make_shards(n):
    levels = []
    bit = n // 2
    while bit > 4:
        levels.append((bit, bit))
        bit //= 2
    levels += [(4, 2), (2, 4)]

    def swap(block, bits):
        return lax.ppermute(block, "blk", [(i, i ^ bits[i % 2]) for i in range(n)])

    def shards(
        tokens, cotangent, gate_weight, up_weight, down_weight, logits, ref_logits, routes
    ):
        count, width = tokens.shape
        slots = cotangent.shape[0]
        experts = logits.shape[1]
        hidden = down_weight.shape[0]
        rows = n * slots
        wide = width + LANES
        anywhere = pl.BlockSpec(memory_space=pl.ANY)

        small = [in_hbm(a) for a in (logits.T, ref_logits.T, routes.T)]
        send, select = pl.pallas_call(
            select_kernel,
            out_shape=[
                jax.ShapeDtypeStruct((slots, wide + width), BF16),
                jax.ShapeDtypeStruct((count, count), F32),
            ],
            in_specs=[anywhere] * 4,
            out_specs=whole(2),
            scratch_shapes=[
                pltpu.VMEM((experts, count), F32),
                pltpu.VMEM((2, count), jnp.int32),
                pltpu.VMEM((count, width), BF16),
                pltpu.VMEM((slots, width), BF16),
                pltpu.SemaphoreType.DMA((4,)),
            ],
            compiler_params=pltpu.CompilerParams(vmem_limit_bytes=8 * MIB),
            cost_estimate=pl.CostEstimate(
                flops=1 << 20, bytes_accessed=1 << 22, transcendentals=0
            ),
        )(small[0], small[2], in_hbm(tokens), in_hbm(cotangent))

        own = send
        for bits in levels[:-3]:
            own = jnp.concatenate([own, swap(own, bits)])
        first, second, third = levels[-3:]
        block_1 = relay(relay(swap(own, first)))
        block_2 = swap(own, second)
        block_3 = swap(own, third)
        gate_w, up_w = fetch([gate_weight, up_weight], [width, width], own)
        block_1 = relay(block_1, gate_w, block_2, block_3)
        block_12 = swap(block_1, second)
        block_13 = swap(relay(block_1), third)
        block_23 = swap(block_3, second)
        block_123 = swap(relay(block_12), third)
        low_half = jnp.concatenate([own, block_1, block_2, block_12])
        high_half = jnp.concatenate([block_3, block_13, block_23, block_123])
        pieces = [low_half, high_half]
        pieces += [swap(piece, (1, 1)) for piece in pieces]

        entropy, divergence, base, coef = pl.pallas_call(
            router_kernel,
            out_shape=[
                jax.ShapeDtypeStruct((1, count), F32),
                jax.ShapeDtypeStruct((1, count), F32),
                jax.ShapeDtypeStruct((experts, count), F32),
                jax.ShapeDtypeStruct((experts, count), F32),
            ],
            in_specs=[anywhere] * 4,
            out_specs=whole(4),
            scratch_shapes=[
                pltpu.VMEM((experts, count), F32),
                pltpu.VMEM((experts, count), F32),
                pltpu.VMEM((2, count), jnp.int32),
                pltpu.SemaphoreType.DMA((3,)),
            ],
            compiler_params=pltpu.CompilerParams(vmem_limit_bytes=8 * MIB),
            cost_estimate=pl.CostEstimate(
                flops=1 << 20, bytes_accessed=1 << 22, transcendentals=0
            ),
        )(*small, high_half)

        work = 2 * rows * width * hidden
        half = rows // 2
        low, keep, weighted_t, d_both, x_t, y_all = pl.pallas_call(
            expert_kernel,
            out_shape=[
                jax.ShapeDtypeStruct((half, wide), BF16),
                jax.ShapeDtypeStruct((half, wide), F32),
                jax.ShapeDtypeStruct((hidden, rows), BF16),
                jax.ShapeDtypeStruct((rows, 2 * hidden), BF16),
                jax.ShapeDtypeStruct((width, rows), BF16),
                jax.ShapeDtypeStruct((rows, width), BF16),
            ],
            in_specs=whole(4) + [anywhere] + whole(2),
            out_specs=whole(6),
            scratch_shapes=[
                pltpu.VMEM((rows, wide), BF16),
                pltpu.VMEM((hidden, width), BF16),
                pltpu.SemaphoreType.DMA((1, 4)),
            ],
            compiler_params=pltpu.CompilerParams(vmem_limit_bytes=24 * MIB),
            cost_estimate=pl.CostEstimate(
                flops=16 * work, bytes_accessed=4 * width * hidden, transcendentals=0
            ),
        )(*pieces, in_hbm(down_weight), gate_w, up_w)

        for bits in [(1, 1)] + levels[::-1]:
            got = swap(low, bits)
            if bits == levels[0]:
                break
            half //= 2
            keep, low = call(
                fold_kernel,
                [((half, wide), F32), ((half, wide), BF16)],
                [keep, got],
                4 * half * wide,
                16 * half * wide,
            )

        cuts = [0, width // 3, 2 * width // 3, width]
        grad_down, *pair = grads_of(x_t, d_both, 0, cuts[1], (), (weighted_t, y_all))
        for start, stop in zip(cuts[1:], cuts[2:]):
            pair = grads_of(x_t, d_both, start, stop - start, tuple(pair))
        grad_gate, grad_up = pair

        grad_tokens, grad_logits = call(
            home_kernel,
            [((count, width), BF16), ((experts, count), F32)],
            [keep, got, select, base, coef],
            1 << 20,
            1 << 18,
        )
        return (
            grad_gate,
            grad_up,
            grad_down,
            grad_tokens,
            grad_logits.T,
            entropy.reshape(count),
            divergence.reshape(count),
        )

    return shards


def solution(mesh):
    in_specs = (
        P(("grp", "blk"), None),
        P(("grp", "blk"), None),
        P(None, "blk"),
        P(None, "blk"),
        P("blk", None),
        P(("grp", "blk"), None),
        P(("grp", "blk"), None),
        P(("grp", "blk"), None),
    )
    out_specs = (
        P("grp", "blk"),
        P("grp", "blk"),
        P(("grp", "blk"), None),
        P(("grp", "blk"), None),
        P(("grp", "blk"), None),
        P(("grp", "blk")),
        P(("grp", "blk")),
    )
    return jax.shard_map(
        make_shards(mesh.shape["blk"]),
        mesh=mesh,
        in_specs=in_specs,
        out_specs=out_specs,
        check_vma=False,
    )
```

```python
import functools

import jax
import jax.numpy as jnp
from jax import lax
from jax.experimental import pallas as pl
from jax.experimental.pallas import tpu as pltpu
from jax.sharding import PartitionSpec as P

F32 = jnp.float32
BF16 = jnp.bfloat16
LANES = 128
MIB = 1 << 20


def dot(left, right, dims):
    return lax.dot_general(left, right, (dims, ((), ())), preferred_element_type=F32)


def whole(count):
    return [pl.BlockSpec(memory_space=pltpu.VMEM)] * count


def call(kernel, outs, args, flops, moved, limit=8):
    return pl.pallas_call(
        kernel,
        out_shape=[jax.ShapeDtypeStruct(s, t) for s, t in outs],
        in_specs=whole(len(args)),
        out_specs=whole(len(outs)),
        compiler_params=pltpu.CompilerParams(vmem_limit_bytes=limit * MIB),
        cost_estimate=pl.CostEstimate(flops=flops, bytes_accessed=moved, transcendentals=0),
    )(*args)


def in_hbm(array):
    return pltpu.with_memory_space_constraint(array, pltpu.HBM)


def in_vmem(array):
    return pltpu.with_memory_space_constraint(array, pltpu.VMEM)


def lane_pair(rows, first, second):
    lane = lax.broadcasted_iota(jnp.int32, (rows, LANES), 1)
    return jnp.where(lane == 0, first, jnp.where(lane == 1, second, 0.0))


def split_pair(value):
    high = value.astype(BF16).astype(F32)
    return lane_pair(value.shape[0], high, value - high)


def start_all(sources, targets, sems):
    copies = [
        pltpu.make_async_copy(s, t, sems.at[i]) for i, (s, t) in enumerate(zip(sources, targets))
    ]
    for copy in copies:
        copy.start()
    return copies


def gates(logits, routes):
    first, second = routes[0:1, :], routes[1:2, :]
    routed = jnp.where((first == 0) | (second == 0), 1.0, 0.0)
    expert = lax.broadcasted_iota(jnp.int32, logits.shape, 0)
    partner_hot = jnp.where(expert == first + second, 1.0, 0.0)
    partner_logit = jnp.sum(logits * partner_hot, axis=0, keepdims=True)
    gate = jnp.where(routed > 0.0, jax.nn.sigmoid(logits[0:1, :] - partner_logit), 0.0)
    window_hot = jnp.where(expert == 0, 1.0, 0.0)
    return routed, gate, (window_hot - partner_hot) * (gate * (1.0 - gate))


def select_kernel(
    logits_in, routes_in, tokens_in, y_in, send, select_out, logits, routes, tokens, y, sems
):
    copies = start_all(
        (logits_in, routes_in, tokens_in, y_in), (logits, routes, tokens, y), sems
    )
    slots, width = send.shape[0], tokens.shape[1]
    count = logits.shape[1]
    for copy in copies[:2]:
        copy.wait()
    routed, gate, _ = gates(logits[...], routes[...])
    token = lax.broadcasted_iota(jnp.int32, (1, count), 1)
    position = jnp.full((1, count), -1.0, F32)
    for t in range(count):
        position += jnp.where(token >= t, routed[:, t : t + 1], 0.0)
    slot = lax.broadcasted_iota(jnp.int32, (count, count), 0)
    hit = (slot == position.astype(jnp.int32)) & (routed > 0.0) & (slot < slots)
    select = jnp.where(hit, 1.0, 0.0)
    select_out[...] = select
    gate_low = gate.astype(BF16).astype(F32)
    g_slots = jnp.sum(select * gate_low, axis=1, keepdims=True)
    wide = width + LANES
    send[:, width:wide] = jnp.broadcast_to(g_slots[:slots], (slots, LANES)).astype(BF16)
    for copy in copies[2:]:
        copy.wait()
    x_slots = dot(select.astype(BF16), tokens[...], ((1,), (0,)))
    send[:, :width] = x_slots[:slots].astype(BF16)
    send[:, wide:] = y[...]


def router_kernel(
    logits_in,
    ref_in,
    routes_in,
    after,
    entropy,
    divergence,
    base,
    coef,
    logits,
    ref_logits,
    routes,
    sems,
):
    copies = start_all((logits_in, ref_in, routes_in), (logits, ref_logits, routes), sems)
    for copy in copies:
        copy.wait()
    x, r = logits[...], ref_logits[...]
    shifted = x - jnp.max(x, axis=0, keepdims=True)
    policy_log = shifted - jnp.log(jnp.sum(jnp.exp(shifted), axis=0, keepdims=True))
    shifted = r - jnp.max(r, axis=0, keepdims=True)
    frozen_log = shifted - jnp.log(jnp.sum(jnp.exp(shifted), axis=0, keepdims=True))
    probs = jnp.exp(policy_log)
    ratio = policy_log - frozen_log
    div = jnp.sum(probs * ratio, axis=0, keepdims=True)
    entropy[...] = -jnp.sum(probs * policy_log, axis=0, keepdims=True)
    divergence[...] = div
    base[...] = probs * (ratio - div)
    coef[...] = gates(x, routes[...])[2]


def fetch_copies(sources, targets, sems):
    parts = sems.shape[1]
    copies = []
    for k, ((source, row), target) in enumerate(zip(sources, targets)):
        step = target.shape[0] // parts
        for i in range(parts):
            copies.append(
                pltpu.make_async_copy(
                    source.at[pl.ds(row + i * step, step)],
                    target.at[pl.ds(i * step, step)],
                    sems.at[k, i],
                )
            )
    return copies


def fetch_kernel(count, *refs):
    sources, targets, sems = refs[:count], refs[count + 1 : -1], refs[-1]
    copies = fetch_copies([(source, 0) for source in sources], targets, sems)
    for copy in copies:
        copy.start()
    for copy in copies:
        copy.wait()


def fetch(weights, rows, after):
    anywhere = pl.BlockSpec(memory_space=pl.ANY)
    count = len(weights)
    out = pl.pallas_call(
        functools.partial(fetch_kernel, count),
        out_shape=[pltpu.VMEM((r, w.shape[1]), w.dtype) for w, r in zip(weights, rows)],
        in_specs=[anywhere] * (count + 1),
        out_specs=whole(count),
        scratch_shapes=[pltpu.SemaphoreType.DMA((count, 4))],
        compiler_params=pltpu.CompilerParams(vmem_limit_bytes=8 * MIB),
        cost_estimate=pl.CostEstimate(
            flops=0, bytes_accessed=2 * sum(w.size for w in weights), transcendentals=0
        ),
    )(*[in_hbm(w) for w in weights], after)
    return [in_vmem(w) for w in out]


def relay_kernel(block, *refs):
    refs[-1][...] = block[...]


def relay(block, *after):
    return pl.pallas_call(
        relay_kernel,
        out_shape=jax.ShapeDtypeStruct(block.shape, block.dtype),
        in_specs=whole(1) + [pl.BlockSpec(memory_space=pl.ANY)] * len(after),
        out_specs=whole(1)[0],
        compiler_params=pltpu.CompilerParams(vmem_limit_bytes=8 * MIB),
        cost_estimate=pl.CostEstimate(
            flops=0, bytes_accessed=4 * MIB, transcendentals=0
        ),
    )(block, *after)


def expert_kernel(*refs):
    pieces, (down_in, gate_w, up_w), refs = refs[:4], refs[4:7], refs[7:]
    send, keep, weighted_t, d_both, x_t, y, x, down_w, sems = refs
    rows, width, hidden_dim = x.shape[0], gate_w.shape[0], gate_w.shape[1]
    wide = width + LANES
    half = rows // 2
    copies = fetch_copies([(down_in, 0)], [down_w], sems)
    for copy in copies:
        copy.start()
    quarter = rows // 4
    for i, ref in enumerate(pieces):
        x[i * quarter : (i + 1) * quarter, :] = ref[:, :wide]
    pre_gate = dot(x[:, :width], gate_w[...], ((1,), (0,)))
    pre_up = dot(x[:, :width], up_w[...], ((1,), (0,)))
    for copy in copies:
        copy.wait()
    for i, ref in enumerate(pieces):
        y[i * quarter : (i + 1) * quarter, :] = ref[:, wide:]
    back = dot(y[...], down_w[...], ((1,), (1,)))
    g = x[:, width:][:, 0:1].astype(F32)
    sig = jax.nn.sigmoid(pre_gate)
    act = pre_gate * sig
    hidden = act * pre_up
    weighted_t[...] = (g * hidden).T.astype(BF16)
    products = jnp.sum(hidden * back, axis=1, keepdims=True)
    scaled = g * back
    d_both[:, :hidden_dim] = (
        scaled * pre_up * sig * (1.0 + pre_gate * (1.0 - sig))
    ).astype(BF16)
    d_both[:, hidden_dim:] = (scaled * act).astype(BF16)
    keep[:, width:] = lane_pair(half, products[:half], 0.0)
    send[:, width:] = split_pair(products[half:]).astype(BF16)
    wide = 1024
    for i in range(width // wide):
        at = pl.ds(i * wide, wide)
        part = dot(d_both[:, :hidden_dim], gate_w[at, :], ((1,), (1,)))
        part += dot(d_both[:, hidden_dim:], up_w[at, :], ((1,), (1,)))
        keep[:, at] = part[:half]
        send[:, at] = part[half:].astype(BF16)
        for c in range(i * wide, (i + 1) * wide, LANES):
            x_t[c : c + LANES, :] = x[:, c : c + LANES].astype(F32).T.astype(BF16)


def fold_kernel(have, got, keep, send):
    half = keep.shape[0]
    width = keep.shape[1] - LANES
    total = have[:, :width] + got[:, :width].astype(F32)
    keep[:, :width] = total[:half]
    send[:, :width] = total[half:].astype(BF16)
    tail = have[:, width:] + got[:, width:].astype(F32)
    value = tail[:, 0:1] + tail[:, 1:2]
    keep[:, width:] = lane_pair(half, value[:half], 0.0)
    send[:, width:] = split_pair(value[half:]).astype(BF16)


def home_kernel(have, got, select, base, coef, grad_tokens, grad_logits):
    slots = have.shape[0]
    width = have.shape[1] - LANES
    count = select.shape[0]
    total = (have[:, :width] + got[:, :width].astype(F32)).astype(BF16)
    padded = jnp.concatenate([total, jnp.zeros((count - slots, width), BF16)], axis=0)
    grad_tokens[...] = dot(select[...].astype(BF16), padded, ((0,), (0,))).astype(BF16)
    tail = have[:, width:] + got[:, width:].astype(F32)
    value = tail[:, 0:1] + tail[:, 1:2]
    token_products = jnp.sum(select[0:slots, :] * value, axis=0, keepdims=True)
    grad_logits[...] = base[...] + coef[...] * token_products


def tiles(out, left, right):
    tall = 128
    for c in range(0, right.shape[1], 256):
        for r in range(0, left.shape[0], tall):
            part = dot(left[r : r + tall], right[:, c : c + 256], ((1,), (0,)))
            out[r : r + tall, c : c + 256] = part.astype(BF16)


def loop(count, body):
    for i in range(count):
        body(i)


def late_copies(row, sources, targets, sems):
    step = sources[0].shape[0]
    return [
        pltpu.make_async_copy(source, target.at[pl.ds(row, step)], sems.at[k])
        for k, (source, target) in enumerate(zip(sources, targets))
    ]


def grads_kernel(first_row, last, x_t, d_both, *refs):
    left = refs[:2] if first_row else ()
    gate_buf, up_buf, sems = refs[-3:]
    outs = refs[-5:-3] if last else refs[-7:-5]
    kept = () if last else refs[-5:-3]
    chunks, step, cols = gate_buf.shape
    copies = late_copies(first_row - step, left, outs, sems.at[chunks]) if left else []
    for copy in copies:
        copy.start()
    for i in range(chunks if last else chunks + 1):
        at = pl.ds(first_row + i * step, step)
        for k, target in enumerate(outs):
            tile = (gate_buf, up_buf)[k].at[i] if i < chunks else kept[k]
            tiles(tile, x_t.at[at], d_both.at[:, pl.ds(k * cols, cols)])
            if i < chunks:
                copy = pltpu.make_async_copy(tile, target.at[at], sems.at[i, k])
                copy.start()
                copies.append(copy)
    for copy in copies:
        copy.wait()


def first_kernel(weighted_t, y, x_t, d_both, down_out, *refs):
    down_buf, down_sems = refs[4:6]
    chunks, _, step = down_buf.shape
    copies = []
    for i in range(chunks):
        at = pl.ds(i * step, step)
        tiles(down_buf.at[i], weighted_t, y.at[:, at])
        copies.append(pltpu.make_async_copy(down_buf.at[i], down_out.at[:, at], down_sems.at[i]))
        copies[i].start()
    grads_kernel(0, False, x_t, d_both, *refs[:4], *refs[6:])
    for copy in copies:
        copy.wait()


def grads_of(x_t, d_both, first_row, rows, before, down=()):
    width, slots = x_t.shape
    cols = d_both.shape[1] // 2
    step = 256
    last = first_row + rows == width
    chunks = rows // step - (0 if last else 1)
    anywhere = pl.BlockSpec(memory_space=pl.ANY)
    outs = [jax.ShapeDtypeStruct((width, cols), BF16)] * 2
    outs += [] if last else [jax.ShapeDtypeStruct((step, cols), BF16)] * 2
    out_specs = [anywhere] * 2 + whole(len(outs) - 2)
    scratch = [
        pltpu.VMEM((chunks, step, cols), BF16),
        pltpu.VMEM((chunks, step, cols), BF16),
        pltpu.SemaphoreType.DMA((chunks + 1, 2)),
    ]
    kernel = functools.partial(grads_kernel, first_row, last)
    if down:
        kernel = first_kernel
        wide = 1024
        outs = [jax.ShapeDtypeStruct((cols, width), BF16)] + outs
        out_specs = [anywhere] + out_specs
        scratch = [
            pltpu.VMEM((width // wide, cols, wide), BF16),
            pltpu.SemaphoreType.DMA((width // wide,)),
        ] + scratch
    elements = 2 * rows * cols + (width * cols if down else 0)
    return pl.pallas_call(
        kernel,
        out_shape=outs,
        in_specs=whole(2 + len(down)) + (whole(2) + [anywhere] * 2 if before else []),
        out_specs=out_specs,
        scratch_shapes=scratch,
        input_output_aliases={4: 0, 5: 1} if before else {},
        compiler_params=pltpu.CompilerParams(vmem_limit_bytes=20 * MIB),
        cost_estimate=pl.CostEstimate(
            flops=8 * slots * elements, bytes_accessed=2 * elements, transcendentals=0
        ),
    )(*down, x_t, d_both, *before[2:], *before[:2])


def make_shards(n):
    levels = []
    bit = n // 2
    while bit > 4:
        levels.append((bit, bit))
        bit //= 2
    levels += [(4, 2), (2, 4)]

    def swap(block, bits):
        return lax.ppermute(block, "blk", [(i, i ^ bits[i % 2]) for i in range(n)])

    def shards(
        tokens, cotangent, gate_weight, up_weight, down_weight, logits, ref_logits, routes
    ):
        count, width = tokens.shape
        slots = cotangent.shape[0]
        experts = logits.shape[1]
        hidden = down_weight.shape[0]
        rows = n * slots
        wide = width + LANES
        anywhere = pl.BlockSpec(memory_space=pl.ANY)

        small = [in_hbm(a) for a in (logits.T, ref_logits.T, routes.T)]
        send, select = pl.pallas_call(
            select_kernel,
            out_shape=[
                jax.ShapeDtypeStruct((slots, wide + width), BF16),
                jax.ShapeDtypeStruct((count, count), F32),
            ],
            in_specs=[anywhere] * 4,
            out_specs=whole(2),
            scratch_shapes=[
                pltpu.VMEM((experts, count), F32),
                pltpu.VMEM((2, count), jnp.int32),
                pltpu.VMEM((count, width), BF16),
                pltpu.VMEM((slots, width), BF16),
                pltpu.SemaphoreType.DMA((4,)),
            ],
            compiler_params=pltpu.CompilerParams(vmem_limit_bytes=8 * MIB),
            cost_estimate=pl.CostEstimate(
                flops=1 << 20, bytes_accessed=1 << 22, transcendentals=0
            ),
        )(small[0], small[2], in_hbm(tokens), in_hbm(cotangent))

        own = send
        for bits in levels[:-3]:
            own = jnp.concatenate([own, swap(own, bits)])
        first, second, third = levels[-3:]
        block_1 = relay(relay(swap(own, first)))
        block_2 = swap(own, second)
        block_3 = swap(own, third)
        gate_w, up_w = fetch([gate_weight, up_weight], [width, width], own)
        block_1 = relay(block_1, gate_w, block_2, block_3)
        block_12 = swap(block_1, second)
        block_13 = swap(relay(block_1), third)
        block_23 = swap(block_3, second)
        block_123 = swap(relay(block_12), third)
        low_half = jnp.concatenate([own, block_1, block_2, block_12])
        high_half = jnp.concatenate([block_3, block_13, block_23, block_123])
        pieces = [low_half, high_half]
        pieces += [swap(piece, (1, 1)) for piece in pieces]

        entropy, divergence, base, coef = pl.pallas_call(
            router_kernel,
            out_shape=[
                jax.ShapeDtypeStruct((1, count), F32),
                jax.ShapeDtypeStruct((1, count), F32),
                jax.ShapeDtypeStruct((experts, count), F32),
                jax.ShapeDtypeStruct((experts, count), F32),
            ],
            in_specs=[anywhere] * 4,
            out_specs=whole(4),
            scratch_shapes=[
                pltpu.VMEM((experts, count), F32),
                pltpu.VMEM((experts, count), F32),
                pltpu.VMEM((2, count), jnp.int32),
                pltpu.SemaphoreType.DMA((3,)),
            ],
            compiler_params=pltpu.CompilerParams(vmem_limit_bytes=8 * MIB),
            cost_estimate=pl.CostEstimate(
                flops=1 << 20, bytes_accessed=1 << 22, transcendentals=0
            ),
        )(*small, high_half)

        work = 2 * rows * width * hidden
        half = rows // 2
        low, keep, weighted_t, d_both, x_t, y_all = pl.pallas_call(
            expert_kernel,
            out_shape=[
                jax.ShapeDtypeStruct((half, wide), BF16),
                jax.ShapeDtypeStruct((half, wide), F32),
                jax.ShapeDtypeStruct((hidden, rows), BF16),
                jax.ShapeDtypeStruct((rows, 2 * hidden), BF16),
                jax.ShapeDtypeStruct((width, rows), BF16),
                jax.ShapeDtypeStruct((rows, width), BF16),
            ],
            in_specs=whole(4) + [anywhere] + whole(2),
            out_specs=whole(6),
            scratch_shapes=[
                pltpu.VMEM((rows, wide), BF16),
                pltpu.VMEM((hidden, width), BF16),
                pltpu.SemaphoreType.DMA((1, 4)),
            ],
            compiler_params=pltpu.CompilerParams(vmem_limit_bytes=24 * MIB),
            cost_estimate=pl.CostEstimate(
                flops=16 * work, bytes_accessed=4 * width * hidden, transcendentals=0
            ),
        )(*pieces, in_hbm(down_weight), gate_w, up_w)

        for bits in [(1, 1)] + levels[::-1]:
            got = swap(low, bits)
            if bits == levels[0]:
                break
            half //= 2
            keep, low = call(
                fold_kernel,
                [((half, wide), F32), ((half, wide), BF16)],
                [keep, got],
                4 * half * wide,
                16 * half * wide,
            )

        cuts = [0, width // 3, 2 * width // 3, width]
        grad_down, *pair = grads_of(x_t, d_both, 0, cuts[1], (), (weighted_t, y_all))
        for start, stop in zip(cuts[1:], cuts[2:]):
            pair = grads_of(x_t, d_both, start, stop - start, tuple(pair))
        grad_gate, grad_up = pair

        grad_tokens, grad_logits = call(
            home_kernel,
            [((count, width), BF16), ((experts, count), F32)],
            [keep, got, select, base, coef],
            1 << 20,
            1 << 18,
        )
        return (
            grad_gate,
            grad_up,
            grad_down,
            grad_tokens,
            grad_logits.T,
            entropy.reshape(count),
            divergence.reshape(count),
        )

    return shards


def solution(mesh):
    in_specs = (
        P(("grp", "blk"), None),
        P(("grp", "blk"), None),
        P(None, "blk"),
        P(None, "blk"),
        P("blk", None),
        P(("grp", "blk"), None),
        P(("grp", "blk"), None),
        P(("grp", "blk"), None),
    )
    out_specs = (
        P("grp", "blk"),
        P("grp", "blk"),
        P(("grp", "blk"), None),
        P(("grp", "blk"), None),
        P(("grp", "blk"), None),
        P(("grp", "blk")),
        P(("grp", "blk")),
    )
    return jax.shard_map(
        make_shards(mesh.shape["blk"]),
        mesh=mesh,
        in_specs=in_specs,
        out_specs=out_specs,
        check_vma=False,
    )
```

```python
import functools

import jax
import jax.numpy as jnp
from jax import lax
from jax.experimental import pallas as pl
from jax.experimental.pallas import tpu as pltpu
from jax.sharding import PartitionSpec as P

F32 = jnp.float32
BF16 = jnp.bfloat16
LANES = 128
MIB = 1 << 20


def dot(left, right, dims):
    return lax.dot_general(left, right, (dims, ((), ())), preferred_element_type=F32)


def whole(count):
    return [pl.BlockSpec(memory_space=pltpu.VMEM)] * count


def call(kernel, outs, args, flops, moved, limit=8):
    return pl.pallas_call(
        kernel,
        out_shape=[jax.ShapeDtypeStruct(s, t) for s, t in outs],
        in_specs=whole(len(args)),
        out_specs=whole(len(outs)),
        compiler_params=pltpu.CompilerParams(vmem_limit_bytes=limit * MIB),
        cost_estimate=pl.CostEstimate(flops=flops, bytes_accessed=moved, transcendentals=0),
    )(*args)


def in_hbm(array):
    return pltpu.with_memory_space_constraint(array, pltpu.HBM)


def in_vmem(array):
    return pltpu.with_memory_space_constraint(array, pltpu.VMEM)


def lane_pair(rows, first, second):
    lane = lax.broadcasted_iota(jnp.int32, (rows, LANES), 1)
    return jnp.where(lane == 0, first, jnp.where(lane == 1, second, 0.0))


def split_pair(value):
    high = value.astype(BF16).astype(F32)
    return lane_pair(value.shape[0], high, value - high)


def start_all(sources, targets, sems):
    copies = [
        pltpu.make_async_copy(s, t, sems.at[i]) for i, (s, t) in enumerate(zip(sources, targets))
    ]
    for copy in copies:
        copy.start()
    return copies


def gates(logits, routes):
    first, second = routes[0:1, :], routes[1:2, :]
    routed = jnp.where((first == 0) | (second == 0), 1.0, 0.0)
    expert = lax.broadcasted_iota(jnp.int32, logits.shape, 0)
    partner_hot = jnp.where(expert == first + second, 1.0, 0.0)
    partner_logit = jnp.sum(logits * partner_hot, axis=0, keepdims=True)
    gate = jnp.where(routed > 0.0, jax.nn.sigmoid(logits[0:1, :] - partner_logit), 0.0)
    window_hot = jnp.where(expert == 0, 1.0, 0.0)
    return routed, gate, (window_hot - partner_hot) * (gate * (1.0 - gate))


def select_kernel(
    logits_in, routes_in, tokens_in, y_in, send, select_out, logits, routes, tokens, y, sems
):
    copies = start_all(
        (logits_in, routes_in, tokens_in, y_in), (logits, routes, tokens, y), sems
    )
    slots, width = send.shape[0], tokens.shape[1]
    count = logits.shape[1]
    for copy in copies[:2]:
        copy.wait()
    routed, gate, _ = gates(logits[...], routes[...])
    token = lax.broadcasted_iota(jnp.int32, (1, count), 1)
    position = jnp.full((1, count), -1.0, F32)
    for t in range(count):
        position += jnp.where(token >= t, routed[:, t : t + 1], 0.0)
    slot = lax.broadcasted_iota(jnp.int32, (count, count), 0)
    hit = (slot == position.astype(jnp.int32)) & (routed > 0.0) & (slot < slots)
    select = jnp.where(hit, 1.0, 0.0)
    select_out[...] = select
    gate_low = gate.astype(BF16).astype(F32)
    g_slots = jnp.sum(select * gate_low, axis=1, keepdims=True)
    wide = width + LANES
    send[:, width:wide] = jnp.broadcast_to(g_slots[:slots], (slots, LANES)).astype(BF16)
    for copy in copies[2:]:
        copy.wait()
    x_slots = dot(select.astype(BF16), tokens[...], ((1,), (0,)))
    send[:, :width] = x_slots[:slots].astype(BF16)
    send[:, wide:] = y[...]


def router_kernel(
    logits_in,
    ref_in,
    routes_in,
    after,
    entropy,
    divergence,
    base,
    coef,
    logits,
    ref_logits,
    routes,
    sems,
):
    copies = start_all((logits_in, ref_in, routes_in), (logits, ref_logits, routes), sems)
    for copy in copies:
        copy.wait()
    x, r = logits[...], ref_logits[...]
    shifted = x - jnp.max(x, axis=0, keepdims=True)
    policy_log = shifted - jnp.log(jnp.sum(jnp.exp(shifted), axis=0, keepdims=True))
    shifted = r - jnp.max(r, axis=0, keepdims=True)
    frozen_log = shifted - jnp.log(jnp.sum(jnp.exp(shifted), axis=0, keepdims=True))
    probs = jnp.exp(policy_log)
    ratio = policy_log - frozen_log
    div = jnp.sum(probs * ratio, axis=0, keepdims=True)
    entropy[...] = -jnp.sum(probs * policy_log, axis=0, keepdims=True)
    divergence[...] = div
    base[...] = probs * (ratio - div)
    coef[...] = gates(x, routes[...])[2]


def fetch_copies(sources, targets, sems):
    parts = sems.shape[1]
    copies = []
    for k, ((source, row), target) in enumerate(zip(sources, targets)):
        step = target.shape[0] // parts
        for i in range(parts):
            copies.append(
                pltpu.make_async_copy(
                    source.at[pl.ds(row + i * step, step)],
                    target.at[pl.ds(i * step, step)],
                    sems.at[k, i],
                )
            )
    return copies


def fetch_kernel(count, *refs):
    sources, targets, sems = refs[:count], refs[count + 1 : -1], refs[-1]
    copies = fetch_copies([(source, 0) for source in sources], targets, sems)
    for copy in copies:
        copy.start()
    for copy in copies:
        copy.wait()


def fetch(weights, rows, after):
    anywhere = pl.BlockSpec(memory_space=pl.ANY)
    count = len(weights)
    out = pl.pallas_call(
        functools.partial(fetch_kernel, count),
        out_shape=[pltpu.VMEM((r, w.shape[1]), w.dtype) for w, r in zip(weights, rows)],
        in_specs=[anywhere] * (count + 1),
        out_specs=whole(count),
        scratch_shapes=[pltpu.SemaphoreType.DMA((count, 4))],
        compiler_params=pltpu.CompilerParams(vmem_limit_bytes=8 * MIB),
        cost_estimate=pl.CostEstimate(
            flops=0, bytes_accessed=2 * sum(w.shape[1] * r for w, r in zip(weights, rows)), transcendentals=0
        ),
    )(*[in_hbm(w) for w in weights], after)
    return [in_vmem(w) for w in out]


def relay_kernel(block, *refs):
    refs[-1][...] = block[...]


def relay(block, *after):
    return pl.pallas_call(
        relay_kernel,
        out_shape=jax.ShapeDtypeStruct(block.shape, block.dtype),
        in_specs=whole(1) + [pl.BlockSpec(memory_space=pl.ANY)] * len(after),
        out_specs=whole(1)[0],
        compiler_params=pltpu.CompilerParams(vmem_limit_bytes=8 * MIB),
        cost_estimate=pl.CostEstimate(
            flops=0, bytes_accessed=4 * MIB, transcendentals=0
        ),
    )(block, *after)


def expert_kernel(*refs):
    pieces, (down_in, gate_w, up_w, down_head), refs = refs[:4], refs[4:8], refs[8:]
    send, keep, weighted_t, d_both, x_t, y, x, down_tail, sems = refs
    rows, width, hidden_dim = x.shape[0], gate_w.shape[0], gate_w.shape[1]
    wide = width + LANES
    half = rows // 2
    copies = fetch_copies([(down_in, down_head.shape[0])], [down_tail], sems)
    for copy in copies:
        copy.start()
    quarter = rows // 4
    for i, ref in enumerate(pieces):
        x[i * quarter : (i + 1) * quarter, :] = ref[:, :wide]
    pre_gate = dot(x[:, :width], gate_w[...], ((1,), (0,)))
    pre_up = dot(x[:, :width], up_w[...], ((1,), (0,)))
    for i, ref in enumerate(pieces):
        y[i * quarter : (i + 1) * quarter, :] = ref[:, wide:]
    back_head = dot(y[...], down_head[...], ((1,), (1,)))
    for copy in copies:
        copy.wait()
    back_tail = dot(y[...], down_tail[...], ((1,), (1,)))
    back = jnp.concatenate([back_head, back_tail], axis=1)
    g = x[:, width:][:, 0:1].astype(F32)
    sig = jax.nn.sigmoid(pre_gate)
    act = pre_gate * sig
    hidden = act * pre_up
    weighted_t[...] = (g * hidden).T.astype(BF16)
    products = jnp.sum(hidden * back, axis=1, keepdims=True)
    scaled = g * back
    d_both[:, :hidden_dim] = (
        scaled * pre_up * sig * (1.0 + pre_gate * (1.0 - sig))
    ).astype(BF16)
    d_both[:, hidden_dim:] = (scaled * act).astype(BF16)
    keep[:, width:] = lane_pair(half, products[:half], 0.0)
    send[:, width:] = split_pair(products[half:]).astype(BF16)
    wide = 1024
    for i in range(width // wide):
        at = pl.ds(i * wide, wide)
        part = dot(d_both[:, :hidden_dim], gate_w[at, :], ((1,), (1,)))
        part += dot(d_both[:, hidden_dim:], up_w[at, :], ((1,), (1,)))
        keep[:, at] = part[:half]
        send[:, at] = part[half:].astype(BF16)
        for c in range(i * wide, (i + 1) * wide, LANES):
            x_t[c : c + LANES, :] = x[:, c : c + LANES].astype(F32).T.astype(BF16)


def fold_kernel(have, got, keep, send):
    half = keep.shape[0]
    width = keep.shape[1] - LANES
    total = have[:, :width] + got[:, :width].astype(F32)
    keep[:, :width] = total[:half]
    send[:, :width] = total[half:].astype(BF16)
    tail = have[:, width:] + got[:, width:].astype(F32)
    value = tail[:, 0:1] + tail[:, 1:2]
    keep[:, width:] = lane_pair(half, value[:half], 0.0)
    send[:, width:] = split_pair(value[half:]).astype(BF16)


def home_kernel(have, got, select, base, coef, grad_tokens, grad_logits):
    slots = have.shape[0]
    width = have.shape[1] - LANES
    count = select.shape[0]
    total = (have[:, :width] + got[:, :width].astype(F32)).astype(BF16)
    padded = jnp.concatenate([total, jnp.zeros((count - slots, width), BF16)], axis=0)
    grad_tokens[...] = dot(select[...].astype(BF16), padded, ((0,), (0,))).astype(BF16)
    tail = have[:, width:] + got[:, width:].astype(F32)
    value = tail[:, 0:1] + tail[:, 1:2]
    token_products = jnp.sum(select[0:slots, :] * value, axis=0, keepdims=True)
    grad_logits[...] = base[...] + coef[...] * token_products


def tiles(out, left, right):
    tall = 128
    for c in range(0, right.shape[1], 256):
        for r in range(0, left.shape[0], tall):
            part = dot(left[r : r + tall], right[:, c : c + 256], ((1,), (0,)))
            out[r : r + tall, c : c + 256] = part.astype(BF16)


def loop(count, body):
    for i in range(count):
        body(i)


def late_copies(row, sources, targets, sems):
    step = sources[0].shape[0]
    return [
        pltpu.make_async_copy(source, target.at[pl.ds(row, step)], sems.at[k])
        for k, (source, target) in enumerate(zip(sources, targets))
    ]


def grads_kernel(first_row, last, x_t, d_both, *refs):
    left = refs[:2] if first_row else ()
    gate_buf, up_buf, sems = refs[-3:]
    outs = refs[-5:-3] if last else refs[-7:-5]
    kept = () if last else refs[-5:-3]
    chunks, step, cols = gate_buf.shape
    copies = late_copies(first_row - step, left, outs, sems.at[chunks]) if left else []
    for copy in copies:
        copy.start()
    for i in range(chunks if last else chunks + 1):
        at = pl.ds(first_row + i * step, step)
        for k, target in enumerate(outs):
            tile = (gate_buf, up_buf)[k].at[i] if i < chunks else kept[k]
            tiles(tile, x_t.at[at], d_both.at[:, pl.ds(k * cols, cols)])
            if i < chunks:
                copy = pltpu.make_async_copy(tile, target.at[at], sems.at[i, k])
                copy.start()
                copies.append(copy)
    for copy in copies:
        copy.wait()


def first_kernel(weighted_t, y, x_t, d_both, down_out, *refs):
    down_buf, down_sems = refs[4:6]
    chunks, _, step = down_buf.shape
    copies = []
    for i in range(chunks):
        at = pl.ds(i * step, step)
        tiles(down_buf.at[i], weighted_t, y.at[:, at])
        copies.append(pltpu.make_async_copy(down_buf.at[i], down_out.at[:, at], down_sems.at[i]))
        copies[i].start()
    grads_kernel(0, False, x_t, d_both, *refs[:4], *refs[6:])
    for copy in copies:
        copy.wait()


def grads_of(x_t, d_both, first_row, rows, before, down=()):
    width, slots = x_t.shape
    cols = d_both.shape[1] // 2
    step = 256
    last = first_row + rows == width
    chunks = rows // step - (0 if last else 1)
    anywhere = pl.BlockSpec(memory_space=pl.ANY)
    outs = [jax.ShapeDtypeStruct((width, cols), BF16)] * 2
    outs += [] if last else [jax.ShapeDtypeStruct((step, cols), BF16)] * 2
    out_specs = [anywhere] * 2 + whole(len(outs) - 2)
    scratch = [
        pltpu.VMEM((chunks, step, cols), BF16),
        pltpu.VMEM((chunks, step, cols), BF16),
        pltpu.SemaphoreType.DMA((chunks + 1, 2)),
    ]
    kernel = functools.partial(grads_kernel, first_row, last)
    if down:
        kernel = first_kernel
        wide = 1024
        outs = [jax.ShapeDtypeStruct((cols, width), BF16)] + outs
        out_specs = [anywhere] + out_specs
        scratch = [
            pltpu.VMEM((width // wide, cols, wide), BF16),
            pltpu.SemaphoreType.DMA((width // wide,)),
        ] + scratch
    elements = 2 * rows * cols + (width * cols if down else 0)
    return pl.pallas_call(
        kernel,
        out_shape=outs,
        in_specs=whole(2 + len(down)) + (whole(2) + [anywhere] * 2 if before else []),
        out_specs=out_specs,
        scratch_shapes=scratch,
        input_output_aliases={4: 0, 5: 1} if before else {},
        compiler_params=pltpu.CompilerParams(vmem_limit_bytes=20 * MIB),
        cost_estimate=pl.CostEstimate(
            flops=8 * slots * elements, bytes_accessed=2 * elements, transcendentals=0
        ),
    )(*down, x_t, d_both, *before[2:], *before[:2])


def make_shards(n):
    levels = []
    bit = n // 2
    while bit > 4:
        levels.append((bit, bit))
        bit //= 2
    levels += [(2, 4), (4, 2)]

    def swap(block, bits):
        return lax.ppermute(block, "blk", [(i, i ^ bits[i % 2]) for i in range(n)])

    def shards(
        tokens, cotangent, gate_weight, up_weight, down_weight, logits, ref_logits, routes
    ):
        count, width = tokens.shape
        slots = cotangent.shape[0]
        experts = logits.shape[1]
        hidden = down_weight.shape[0]
        rows = n * slots
        wide = width + LANES
        anywhere = pl.BlockSpec(memory_space=pl.ANY)

        small = [in_hbm(a) for a in (logits.T, ref_logits.T, routes.T)]
        send, select = pl.pallas_call(
            select_kernel,
            out_shape=[
                jax.ShapeDtypeStruct((slots, wide + width), BF16),
                jax.ShapeDtypeStruct((count, count), F32),
            ],
            in_specs=[anywhere] * 4,
            out_specs=whole(2),
            scratch_shapes=[
                pltpu.VMEM((experts, count), F32),
                pltpu.VMEM((2, count), jnp.int32),
                pltpu.VMEM((count, width), BF16),
                pltpu.VMEM((slots, width), BF16),
                pltpu.SemaphoreType.DMA((4,)),
            ],
            compiler_params=pltpu.CompilerParams(vmem_limit_bytes=8 * MIB),
            cost_estimate=pl.CostEstimate(
                flops=1 << 20, bytes_accessed=1 << 22, transcendentals=0
            ),
        )(small[0], small[2], in_hbm(tokens), in_hbm(cotangent))

        own = send
        for bits in levels[:-3]:
            own = jnp.concatenate([own, swap(own, bits)])
        first, second, third = levels[-3:]
        block_1 = relay(relay(swap(own, first)))
        block_2 = swap(own, second)
        block_3 = swap(own, third)
        gate_w, up_w = fetch([gate_weight, up_weight], [width, width], own)
        block_1 = relay(block_1, gate_w, block_2, block_3)
        block_12 = swap(block_1, second)
        block_13_source = relay(block_1)
        block_13 = swap(block_13_source, third)
        block_23 = swap(block_3, second)
        (down_head,) = fetch([down_weight], [hidden // 2], relay(block_13_source))
        block_123 = swap(relay(block_12, down_head), third)
        low_half = jnp.concatenate([own, block_1, block_2, block_12])
        high_half = jnp.concatenate([block_3, block_13, block_23, block_123])
        pieces = [low_half, high_half]
        pieces += [swap(piece, (1, 1)) for piece in pieces]

        entropy, divergence, base, coef = pl.pallas_call(
            router_kernel,
            out_shape=[
                jax.ShapeDtypeStruct((1, count), F32),
                jax.ShapeDtypeStruct((1, count), F32),
                jax.ShapeDtypeStruct((experts, count), F32),
                jax.ShapeDtypeStruct((experts, count), F32),
            ],
            in_specs=[anywhere] * 4,
            out_specs=whole(4),
            scratch_shapes=[
                pltpu.VMEM((experts, count), F32),
                pltpu.VMEM((experts, count), F32),
                pltpu.VMEM((2, count), jnp.int32),
                pltpu.SemaphoreType.DMA((3,)),
            ],
            compiler_params=pltpu.CompilerParams(vmem_limit_bytes=8 * MIB),
            cost_estimate=pl.CostEstimate(
                flops=1 << 20, bytes_accessed=1 << 22, transcendentals=0
            ),
        )(*small, high_half)

        work = 2 * rows * width * hidden
        half = rows // 2
        low, keep, weighted_t, d_both, x_t, y_all = pl.pallas_call(
            expert_kernel,
            out_shape=[
                jax.ShapeDtypeStruct((half, wide), BF16),
                jax.ShapeDtypeStruct((half, wide), F32),
                jax.ShapeDtypeStruct((hidden, rows), BF16),
                jax.ShapeDtypeStruct((rows, 2 * hidden), BF16),
                jax.ShapeDtypeStruct((width, rows), BF16),
                jax.ShapeDtypeStruct((rows, width), BF16),
            ],
            in_specs=whole(4) + [anywhere] + whole(3),
            out_specs=whole(6),
            scratch_shapes=[
                pltpu.VMEM((rows, wide), BF16),
                pltpu.VMEM((hidden // 2, width), BF16),
                pltpu.SemaphoreType.DMA((1, 4)),
            ],
            compiler_params=pltpu.CompilerParams(vmem_limit_bytes=24 * MIB),
            cost_estimate=pl.CostEstimate(
                flops=16 * work, bytes_accessed=4 * width * hidden, transcendentals=0
            ),
        )(*pieces, in_hbm(down_weight), gate_w, up_w, down_head)

        for bits in [(1, 1)] + levels[::-1]:
            got = swap(low, bits)
            if bits == levels[0]:
                break
            half //= 2
            keep, low = call(
                fold_kernel,
                [((half, wide), F32), ((half, wide), BF16)],
                [keep, got],
                4 * half * wide,
                16 * half * wide,
            )

        cuts = [0, width // 3, 2 * width // 3, width]
        grad_down, *pair = grads_of(x_t, d_both, 0, cuts[1], (), (weighted_t, y_all))
        for start, stop in zip(cuts[1:], cuts[2:]):
            pair = grads_of(x_t, d_both, start, stop - start, tuple(pair))
        grad_gate, grad_up = pair

        grad_tokens, grad_logits = call(
            home_kernel,
            [((count, width), BF16), ((experts, count), F32)],
            [keep, got, select, base, coef],
            1 << 20,
            1 << 18,
        )
        return (
            grad_gate,
            grad_up,
            grad_down,
            grad_tokens,
            grad_logits.T,
            entropy.reshape(count),
            divergence.reshape(count),
        )

    return shards


def solution(mesh):
    in_specs = (
        P(("grp", "blk"), None),
        P(("grp", "blk"), None),
        P(None, "blk"),
        P(None, "blk"),
        P("blk", None),
        P(("grp", "blk"), None),
        P(("grp", "blk"), None),
        P(("grp", "blk"), None),
    )
    out_specs = (
        P("grp", "blk"),
        P("grp", "blk"),
        P(("grp", "blk"), None),
        P(("grp", "blk"), None),
        P(("grp", "blk"), None),
        P(("grp", "blk")),
        P(("grp", "blk")),
    )
    return jax.shard_map(
        make_shards(mesh.shape["blk"]),
        mesh=mesh,
        in_specs=in_specs,
        out_specs=out_specs,
        check_vma=False,
    )
```

```python
import functools

import jax
import jax.numpy as jnp
from jax import lax
from jax.experimental import pallas as pl
from jax.experimental.pallas import tpu as pltpu
from jax.sharding import PartitionSpec as P

F32 = jnp.float32
BF16 = jnp.bfloat16
LANES = 128
MIB = 1 << 20


def dot(left, right, dims):
    return lax.dot_general(left, right, (dims, ((), ())), preferred_element_type=F32)


def whole(count):
    return [pl.BlockSpec(memory_space=pltpu.VMEM)] * count


def call(kernel, outs, args, flops, moved, limit=8):
    return pl.pallas_call(
        kernel,
        out_shape=[jax.ShapeDtypeStruct(s, t) for s, t in outs],
        in_specs=whole(len(args)),
        out_specs=whole(len(outs)),
        compiler_params=pltpu.CompilerParams(vmem_limit_bytes=limit * MIB),
        cost_estimate=pl.CostEstimate(flops=flops, bytes_accessed=moved, transcendentals=0),
    )(*args)


def in_hbm(array):
    return pltpu.with_memory_space_constraint(array, pltpu.HBM)


def in_vmem(array):
    return pltpu.with_memory_space_constraint(array, pltpu.VMEM)


def lane_pair(rows, first, second):
    lane = lax.broadcasted_iota(jnp.int32, (rows, LANES), 1)
    return jnp.where(lane == 0, first, jnp.where(lane == 1, second, 0.0))


def split_pair(value):
    high = value.astype(BF16).astype(F32)
    return lane_pair(value.shape[0], high, value - high)


def start_all(sources, targets, sems):
    copies = [
        pltpu.make_async_copy(s, t, sems.at[i]) for i, (s, t) in enumerate(zip(sources, targets))
    ]
    for copy in copies:
        copy.start()
    return copies


def gates(logits, routes):
    first, second = routes[0:1, :], routes[1:2, :]
    routed = jnp.where((first == 0) | (second == 0), 1.0, 0.0)
    expert = lax.broadcasted_iota(jnp.int32, logits.shape, 0)
    partner_hot = jnp.where(expert == first + second, 1.0, 0.0)
    partner_logit = jnp.sum(logits * partner_hot, axis=0, keepdims=True)
    gate = jnp.where(routed > 0.0, jax.nn.sigmoid(logits[0:1, :] - partner_logit), 0.0)
    window_hot = jnp.where(expert == 0, 1.0, 0.0)
    return routed, gate, (window_hot - partner_hot) * (gate * (1.0 - gate))


def select_kernel(
    logits_in, routes_in, tokens_in, y_in, send, select_out, logits, routes, tokens, y, sems
):
    copies = start_all(
        (logits_in, routes_in, tokens_in, y_in), (logits, routes, tokens, y), sems
    )
    slots, width = send.shape[0], tokens.shape[1]
    count = logits.shape[1]
    for copy in copies[:2]:
        copy.wait()
    routed, gate, _ = gates(logits[...], routes[...])
    token = lax.broadcasted_iota(jnp.int32, (1, count), 1)
    position = jnp.full((1, count), -1.0, F32)
    for t in range(count):
        position += jnp.where(token >= t, routed[:, t : t + 1], 0.0)
    slot = lax.broadcasted_iota(jnp.int32, (count, count), 0)
    hit = (slot == position.astype(jnp.int32)) & (routed > 0.0) & (slot < slots)
    select = jnp.where(hit, 1.0, 0.0)
    select_out[...] = select
    gate_low = gate.astype(BF16).astype(F32)
    g_slots = jnp.sum(select * gate_low, axis=1, keepdims=True)
    wide = width + LANES
    send[:, width:wide] = jnp.broadcast_to(g_slots[:slots], (slots, LANES)).astype(BF16)
    for copy in copies[2:]:
        copy.wait()
    x_slots = dot(select.astype(BF16), tokens[...], ((1,), (0,)))
    send[:, :width] = x_slots[:slots].astype(BF16)
    send[:, wide:] = y[...]


def router_kernel(
    logits_in,
    ref_in,
    routes_in,
    after,
    entropy,
    divergence,
    base,
    coef,
    logits,
    ref_logits,
    routes,
    sems,
):
    copies = start_all((logits_in, ref_in, routes_in), (logits, ref_logits, routes), sems)
    for copy in copies:
        copy.wait()
    x, r = logits[...], ref_logits[...]
    shifted = x - jnp.max(x, axis=0, keepdims=True)
    policy_log = shifted - jnp.log(jnp.sum(jnp.exp(shifted), axis=0, keepdims=True))
    shifted = r - jnp.max(r, axis=0, keepdims=True)
    frozen_log = shifted - jnp.log(jnp.sum(jnp.exp(shifted), axis=0, keepdims=True))
    probs = jnp.exp(policy_log)
    ratio = policy_log - frozen_log
    div = jnp.sum(probs * ratio, axis=0, keepdims=True)
    entropy[...] = -jnp.sum(probs * policy_log, axis=0, keepdims=True)
    divergence[...] = div
    base[...] = probs * (ratio - div)
    coef[...] = gates(x, routes[...])[2]


def fetch_copies(sources, targets, sems):
    parts = sems.shape[1]
    copies = []
    for k, ((source, row), target) in enumerate(zip(sources, targets)):
        step = target.shape[0] // parts
        for i in range(parts):
            copies.append(
                pltpu.make_async_copy(
                    source.at[pl.ds(row + i * step, step)],
                    target.at[pl.ds(i * step, step)],
                    sems.at[k, i],
                )
            )
    return copies


def fetch_kernel(count, *refs):
    sources, targets, sems = refs[:count], refs[count + 1 : -1], refs[-1]
    copies = fetch_copies([(source, 0) for source in sources], targets, sems)
    for copy in copies:
        copy.start()
    for copy in copies:
        copy.wait()


def fetch(weights, rows, after):
    anywhere = pl.BlockSpec(memory_space=pl.ANY)
    count = len(weights)
    out = pl.pallas_call(
        functools.partial(fetch_kernel, count),
        out_shape=[pltpu.VMEM((r, w.shape[1]), w.dtype) for w, r in zip(weights, rows)],
        in_specs=[anywhere] * (count + 1),
        out_specs=whole(count),
        scratch_shapes=[pltpu.SemaphoreType.DMA((count, 4))],
        compiler_params=pltpu.CompilerParams(vmem_limit_bytes=8 * MIB),
        cost_estimate=pl.CostEstimate(
            flops=0, bytes_accessed=2 * sum(w.size for w in weights), transcendentals=0
        ),
    )(*[in_hbm(w) for w in weights], after)
    return [in_vmem(w) for w in out]


def relay_kernel(block, *refs):
    refs[-1][...] = block[...]


def relay(block, *after):
    return pl.pallas_call(
        relay_kernel,
        out_shape=jax.ShapeDtypeStruct(block.shape, block.dtype),
        in_specs=whole(1) + [pl.BlockSpec(memory_space=pl.ANY)] * len(after),
        out_specs=whole(1)[0],
        compiler_params=pltpu.CompilerParams(vmem_limit_bytes=8 * MIB),
        cost_estimate=pl.CostEstimate(
            flops=0, bytes_accessed=4 * MIB, transcendentals=0
        ),
    )(block, *after)


def expert_kernel(*refs):
    pieces, (down_in, gate_w, up_w), refs = refs[:4], refs[4:7], refs[7:]
    send, keep, weighted_t, d_both, x_t, y, x, down_w, sems = refs
    rows, width, hidden_dim = x.shape[0], gate_w.shape[0], gate_w.shape[1]
    wide = width + LANES
    half = rows // 2
    copies = fetch_copies([(down_in, 0)], [down_w], sems)
    for copy in copies:
        copy.start()
    quarter = rows // 4
    for i, ref in enumerate(pieces):
        x[i * quarter : (i + 1) * quarter, :] = ref[:, :wide]
    pre_gate = dot(x[:, :width], gate_w[...], ((1,), (0,)))
    pre_up = dot(x[:, :width], up_w[...], ((1,), (0,)))
    for copy in copies:
        copy.wait()
    for i, ref in enumerate(pieces):
        y[i * quarter : (i + 1) * quarter, :] = ref[:, wide:]
    back = dot(y[...], down_w[...], ((1,), (1,)))
    g = x[:, width:][:, 0:1].astype(F32)
    sig = jax.nn.sigmoid(pre_gate)
    act = pre_gate * sig
    hidden = act * pre_up
    weighted_t[...] = (g * hidden).T.astype(BF16)
    products = jnp.sum(hidden * back, axis=1, keepdims=True)
    scaled = g * back
    d_both[:, :hidden_dim] = (
        scaled * pre_up * sig * (1.0 + pre_gate * (1.0 - sig))
    ).astype(BF16)
    d_both[:, hidden_dim:] = (scaled * act).astype(BF16)
    keep[:, width:] = lane_pair(half, products[:half], 0.0)
    send[:, width:] = split_pair(products[half:]).astype(BF16)
    wide = 1024
    for i in range(width // wide):
        at = pl.ds(i * wide, wide)
        part = dot(d_both[:, :hidden_dim], gate_w[at, :], ((1,), (1,)))
        part += dot(d_both[:, hidden_dim:], up_w[at, :], ((1,), (1,)))
        keep[:, at] = part[:half]
        send[:, at] = part[half:].astype(BF16)
        for c in range(i * wide, (i + 1) * wide, LANES):
            x_t[c : c + LANES, :] = x[:, c : c + LANES].astype(F32).T.astype(BF16)


def folded(have, gots):
    width = have.shape[1] - LANES
    total, tail = have[:, :width], have[:, width:]
    for got in gots:
        total += got[:, :width].astype(F32)
        tail += got[:, width:].astype(F32)
    return total, tail[:, 0:1] + tail[:, 1:2]


def put_keep(out, total, value):
    width = total.shape[1]
    out[:, :width] = total
    out[:, width:] = lane_pair(total.shape[0], value, 0.0)


def put_send(out, total, value):
    width = total.shape[1]
    out[:, :width] = total.astype(BF16)
    out[:, width:] = split_pair(value).astype(BF16)


def fold_kernel(have, *refs):
    keep = next(i for i, ref in enumerate(refs) if ref.dtype == F32)
    gots, keep, sends = refs[:keep], refs[keep], refs[keep + 1 :]
    rows = keep.shape[0]
    total, value = folded(have, gots)
    put_keep(keep, total[:rows], value[:rows])
    for i, send in enumerate(sends):
        part = slice((i + 1) * rows, (i + 2) * rows)
        put_send(send, total[part], value[part])


def home_kernel(have, *refs):
    gots, (select, base, coef, grad_tokens, grad_logits) = refs[:-5], refs[-5:]
    slots = have.shape[0]
    count = select.shape[0]
    total, value = folded(have, gots)
    total = total.astype(BF16)
    padded = jnp.concatenate([total, jnp.zeros((count - slots, total.shape[1]), BF16)], axis=0)
    grad_tokens[...] = dot(select[...].astype(BF16), padded, ((0,), (0,))).astype(BF16)
    token_products = jnp.sum(select[0:slots, :] * value, axis=0, keepdims=True)
    grad_logits[...] = base[...] + coef[...] * token_products


def tiles(out, left, right):
    tall = 128
    for c in range(0, right.shape[1], 256):
        for r in range(0, left.shape[0], tall):
            part = dot(left[r : r + tall], right[:, c : c + 256], ((1,), (0,)))
            out[r : r + tall, c : c + 256] = part.astype(BF16)


def loop(count, body):
    for i in range(count):
        body(i)


def late_copies(row, sources, targets, sems):
    step = sources[0].shape[0]
    return [
        pltpu.make_async_copy(source, target.at[pl.ds(row, step)], sems.at[k])
        for k, (source, target) in enumerate(zip(sources, targets))
    ]


def grads_kernel(first_row, last, x_t, d_both, *refs):
    left = refs[:2] if first_row else ()
    gate_buf, up_buf, sems = refs[-3:]
    outs = refs[-5:-3] if last else refs[-7:-5]
    kept = () if last else refs[-5:-3]
    chunks, step, cols = gate_buf.shape
    copies = late_copies(first_row - step, left, outs, sems.at[chunks]) if left else []
    for copy in copies:
        copy.start()
    for i in range(chunks if last else chunks + 1):
        at = pl.ds(first_row + i * step, step)
        for k, target in enumerate(outs):
            tile = (gate_buf, up_buf)[k].at[i] if i < chunks else kept[k]
            tiles(tile, x_t.at[at], d_both.at[:, pl.ds(k * cols, cols)])
            if i < chunks:
                copy = pltpu.make_async_copy(tile, target.at[at], sems.at[i, k])
                copy.start()
                copies.append(copy)
    for copy in copies:
        copy.wait()


def first_kernel(weighted_t, y, x_t, d_both, down_out, *refs):
    down_buf, down_sems = refs[4:6]
    chunks, _, step = down_buf.shape
    copies = []
    for i in range(chunks):
        at = pl.ds(i * step, step)
        tiles(down_buf.at[i], weighted_t, y.at[:, at])
        copies.append(pltpu.make_async_copy(down_buf.at[i], down_out.at[:, at], down_sems.at[i]))
        copies[i].start()
    grads_kernel(0, False, x_t, d_both, *refs[:4], *refs[6:])
    for copy in copies:
        copy.wait()


def grads_of(x_t, d_both, first_row, rows, before, down=()):
    width, slots = x_t.shape
    cols = d_both.shape[1] // 2
    step = 256
    last = first_row + rows == width
    chunks = rows // step - (0 if last else 1)
    anywhere = pl.BlockSpec(memory_space=pl.ANY)
    outs = [jax.ShapeDtypeStruct((width, cols), BF16)] * 2
    outs += [] if last else [jax.ShapeDtypeStruct((step, cols), BF16)] * 2
    out_specs = [anywhere] * 2 + whole(len(outs) - 2)
    scratch = [
        pltpu.VMEM((chunks, step, cols), BF16),
        pltpu.VMEM((chunks, step, cols), BF16),
        pltpu.SemaphoreType.DMA((chunks + 1, 2)),
    ]
    kernel = functools.partial(grads_kernel, first_row, last)
    if down:
        kernel = first_kernel
        wide = 1024
        outs = [jax.ShapeDtypeStruct((cols, width), BF16)] + outs
        out_specs = [anywhere] + out_specs
        scratch = [
            pltpu.VMEM((width // wide, cols, wide), BF16),
            pltpu.SemaphoreType.DMA((width // wide,)),
        ] + scratch
    elements = 2 * rows * cols + (width * cols if down else 0)
    return pl.pallas_call(
        kernel,
        out_shape=outs,
        in_specs=whole(2 + len(down)) + (whole(2) + [anywhere] * 2 if before else []),
        out_specs=out_specs,
        scratch_shapes=scratch,
        input_output_aliases={4: 0, 5: 1} if before else {},
        compiler_params=pltpu.CompilerParams(vmem_limit_bytes=20 * MIB),
        cost_estimate=pl.CostEstimate(
            flops=8 * slots * elements, bytes_accessed=2 * elements, transcendentals=0
        ),
    )(*down, x_t, d_both, *before[2:], *before[:2])


def make_shards(n):
    levels = []
    bit = n // 2
    while bit > 4:
        levels.append((bit, bit))
        bit //= 2
    levels += [(4, 2), (2, 4)]

    def swap(block, bits):
        return lax.ppermute(block, "blk", [(i, i ^ bits[i % 2]) for i in range(n)])

    def shards(
        tokens, cotangent, gate_weight, up_weight, down_weight, logits, ref_logits, routes
    ):
        count, width = tokens.shape
        slots = cotangent.shape[0]
        experts = logits.shape[1]
        hidden = down_weight.shape[0]
        rows = n * slots
        wide = width + LANES
        anywhere = pl.BlockSpec(memory_space=pl.ANY)

        small = [in_hbm(a) for a in (logits.T, ref_logits.T, routes.T)]
        send, select = pl.pallas_call(
            select_kernel,
            out_shape=[
                jax.ShapeDtypeStruct((slots, wide + width), BF16),
                jax.ShapeDtypeStruct((count, count), F32),
            ],
            in_specs=[anywhere] * 4,
            out_specs=whole(2),
            scratch_shapes=[
                pltpu.VMEM((experts, count), F32),
                pltpu.VMEM((2, count), jnp.int32),
                pltpu.VMEM((count, width), BF16),
                pltpu.VMEM((slots, width), BF16),
                pltpu.SemaphoreType.DMA((4,)),
            ],
            compiler_params=pltpu.CompilerParams(vmem_limit_bytes=8 * MIB),
            cost_estimate=pl.CostEstimate(
                flops=1 << 20, bytes_accessed=1 << 22, transcendentals=0
            ),
        )(small[0], small[2], in_hbm(tokens), in_hbm(cotangent))

        own = send
        for bits in levels[:-3]:
            own = jnp.concatenate([own, swap(own, bits)])
        first, second, third = levels[-3:]
        block_1 = relay(relay(swap(own, first)))
        block_2 = swap(own, second)
        block_3 = swap(own, third)
        gate_w, up_w = fetch([gate_weight, up_weight], [width, width], own)
        block_1 = relay(block_1, gate_w, block_2, block_3)
        block_12 = swap(block_1, second)
        block_13 = swap(relay(block_1), third)
        block_23 = swap(block_3, second)
        block_123 = swap(relay(block_12), third)
        low_half = jnp.concatenate([own, block_1, block_2, block_12])
        high_half = jnp.concatenate([block_3, block_13, block_23, block_123])
        pieces = [low_half, high_half]
        pieces += [swap(piece, (1, 1)) for piece in pieces]

        entropy, divergence, base, coef = pl.pallas_call(
            router_kernel,
            out_shape=[
                jax.ShapeDtypeStruct((1, count), F32),
                jax.ShapeDtypeStruct((1, count), F32),
                jax.ShapeDtypeStruct((experts, count), F32),
                jax.ShapeDtypeStruct((experts, count), F32),
            ],
            in_specs=[anywhere] * 4,
            out_specs=whole(4),
            scratch_shapes=[
                pltpu.VMEM((experts, count), F32),
                pltpu.VMEM((experts, count), F32),
                pltpu.VMEM((2, count), jnp.int32),
                pltpu.SemaphoreType.DMA((3,)),
            ],
            compiler_params=pltpu.CompilerParams(vmem_limit_bytes=8 * MIB),
            cost_estimate=pl.CostEstimate(
                flops=1 << 20, bytes_accessed=1 << 22, transcendentals=0
            ),
        )(*small, high_half)

        work = 2 * rows * width * hidden
        half = rows // 2
        low, keep, weighted_t, d_both, x_t, y_all = pl.pallas_call(
            expert_kernel,
            out_shape=[
                jax.ShapeDtypeStruct((half, wide), BF16),
                jax.ShapeDtypeStruct((half, wide), F32),
                jax.ShapeDtypeStruct((hidden, rows), BF16),
                jax.ShapeDtypeStruct((rows, 2 * hidden), BF16),
                jax.ShapeDtypeStruct((width, rows), BF16),
                jax.ShapeDtypeStruct((rows, width), BF16),
            ],
            in_specs=whole(4) + [anywhere] + whole(2),
            out_specs=whole(6),
            scratch_shapes=[
                pltpu.VMEM((rows, wide), BF16),
                pltpu.VMEM((hidden, width), BF16),
                pltpu.SemaphoreType.DMA((1, 4)),
            ],
            compiler_params=pltpu.CompilerParams(vmem_limit_bytes=24 * MIB),
            cost_estimate=pl.CostEstimate(
                flops=16 * work, bytes_accessed=4 * width * hidden, transcendentals=0
            ),
        )(*pieces, in_hbm(down_weight), gate_w, up_w)

        both = tuple(f ^ s for f, s in zip(first, second))
        paths = [((1, 1),), (third,), (first, second, both)] + [(b,) for b in levels[:-3][::-1]]
        sent = [low]
        for path, following in zip(paths, paths[1:] + [()]):
            gots = [swap(block, bits) for block, bits in zip(sent, path)]
            if not following:
                break
            rows_kept = keep.shape[0] // (len(following) + 1)
            keep, *sent = call(
                fold_kernel,
                [((rows_kept, wide), F32)] + [((rows_kept, wide), BF16)] * len(following),
                [keep, *gots],
                4 * keep.shape[0] * wide,
                16 * keep.shape[0] * wide,
            )

        cuts = [0, width // 3, width]
        grad_down, *pair = grads_of(x_t, d_both, 0, cuts[1], (), (weighted_t, y_all))
        for start, stop in zip(cuts[1:], cuts[2:]):
            pair = grads_of(x_t, d_both, start, stop - start, tuple(pair))
        grad_gate, grad_up = pair

        grad_tokens, grad_logits = call(
            home_kernel,
            [((count, width), BF16), ((experts, count), F32)],
            [keep, *gots, select, base, coef],
            1 << 20,
            1 << 18,
        )
        return (
            grad_gate,
            grad_up,
            grad_down,
            grad_tokens,
            grad_logits.T,
            entropy.reshape(count),
            divergence.reshape(count),
        )

    return shards


def solution(mesh):
    in_specs = (
        P(("grp", "blk"), None),
        P(("grp", "blk"), None),
        P(None, "blk"),
        P(None, "blk"),
        P("blk", None),
        P(("grp", "blk"), None),
        P(("grp", "blk"), None),
        P(("grp", "blk"), None),
    )
    out_specs = (
        P("grp", "blk"),
        P("grp", "blk"),
        P(("grp", "blk"), None),
        P(("grp", "blk"), None),
        P(("grp", "blk"), None),
        P(("grp", "blk")),
        P(("grp", "blk")),
    )
    return jax.shard_map(
        make_shards(mesh.shape["blk"]),
        mesh=mesh,
        in_specs=in_specs,
        out_specs=out_specs,
        check_vma=False,
    )
```

```python
import functools

import jax
import jax.numpy as jnp
from jax import lax
from jax.experimental import pallas as pl
from jax.experimental.pallas import tpu as pltpu
from jax.sharding import PartitionSpec as P

F32 = jnp.float32
BF16 = jnp.bfloat16
LANES = 128
MIB = 1 << 20


def dot(left, right, dims):
    return lax.dot_general(left, right, (dims, ((), ())), preferred_element_type=F32)


def whole(count):
    return [pl.BlockSpec(memory_space=pltpu.VMEM)] * count


def call(kernel, outs, args, flops, moved, limit=8):
    return pl.pallas_call(
        kernel,
        out_shape=[jax.ShapeDtypeStruct(s, t) for s, t in outs],
        in_specs=whole(len(args)),
        out_specs=whole(len(outs)),
        compiler_params=pltpu.CompilerParams(vmem_limit_bytes=limit * MIB),
        cost_estimate=pl.CostEstimate(flops=flops, bytes_accessed=moved, transcendentals=0),
    )(*args)


def in_hbm(array):
    return pltpu.with_memory_space_constraint(array, pltpu.HBM)


def in_vmem(array):
    return pltpu.with_memory_space_constraint(array, pltpu.VMEM)


def lane_pair(rows, first, second):
    lane = lax.broadcasted_iota(jnp.int32, (rows, LANES), 1)
    return jnp.where(lane == 0, first, jnp.where(lane == 1, second, 0.0))


def split_pair(value):
    high = value.astype(BF16).astype(F32)
    return lane_pair(value.shape[0], high, value - high)


def start_all(sources, targets, sems):
    copies = [
        pltpu.make_async_copy(s, t, sems.at[i]) for i, (s, t) in enumerate(zip(sources, targets))
    ]
    for copy in copies:
        copy.start()
    return copies


def gates(logits, routes):
    first, second = routes[0:1, :], routes[1:2, :]
    routed = jnp.where((first == 0) | (second == 0), 1.0, 0.0)
    expert = lax.broadcasted_iota(jnp.int32, logits.shape, 0)
    partner_hot = jnp.where(expert == first + second, 1.0, 0.0)
    partner_logit = jnp.sum(logits * partner_hot, axis=0, keepdims=True)
    gate = jnp.where(routed > 0.0, jax.nn.sigmoid(logits[0:1, :] - partner_logit), 0.0)
    window_hot = jnp.where(expert == 0, 1.0, 0.0)
    return routed, gate, (window_hot - partner_hot) * (gate * (1.0 - gate))


def select_kernel(
    logits_in, routes_in, tokens_in, y_in, send, select_out, logits, routes, tokens, y, sems
):
    copies = start_all(
        (logits_in, routes_in, tokens_in, y_in), (logits, routes, tokens, y), sems
    )
    slots, width = send.shape[0], tokens.shape[1]
    count = logits.shape[1]
    for copy in copies[:2]:
        copy.wait()
    routed, gate, _ = gates(logits[...], routes[...])
    token = lax.broadcasted_iota(jnp.int32, (1, count), 1)
    position = jnp.full((1, count), -1.0, F32)
    for t in range(count):
        position += jnp.where(token >= t, routed[:, t : t + 1], 0.0)
    slot = lax.broadcasted_iota(jnp.int32, (count, count), 0)
    hit = (slot == position.astype(jnp.int32)) & (routed > 0.0) & (slot < slots)
    select = jnp.where(hit, 1.0, 0.0)
    select_out[...] = select
    gate_low = gate.astype(BF16).astype(F32)
    g_slots = jnp.sum(select * gate_low, axis=1, keepdims=True)
    wide = width + LANES
    send[:, width:wide] = jnp.broadcast_to(g_slots[:slots], (slots, LANES)).astype(BF16)
    for copy in copies[2:]:
        copy.wait()
    x_slots = dot(select.astype(BF16), tokens[...], ((1,), (0,)))
    send[:, :width] = x_slots[:slots].astype(BF16)
    send[:, wide:] = y[...]


def router_kernel(
    logits_in,
    ref_in,
    routes_in,
    after,
    entropy,
    divergence,
    base,
    coef,
    logits,
    ref_logits,
    routes,
    sems,
):
    copies = start_all((logits_in, ref_in, routes_in), (logits, ref_logits, routes), sems)
    for copy in copies:
        copy.wait()
    x, r = logits[...], ref_logits[...]
    shifted = x - jnp.max(x, axis=0, keepdims=True)
    policy_log = shifted - jnp.log(jnp.sum(jnp.exp(shifted), axis=0, keepdims=True))
    shifted = r - jnp.max(r, axis=0, keepdims=True)
    frozen_log = shifted - jnp.log(jnp.sum(jnp.exp(shifted), axis=0, keepdims=True))
    probs = jnp.exp(policy_log)
    ratio = policy_log - frozen_log
    div = jnp.sum(probs * ratio, axis=0, keepdims=True)
    entropy[...] = -jnp.sum(probs * policy_log, axis=0, keepdims=True)
    divergence[...] = div
    base[...] = probs * (ratio - div)
    coef[...] = gates(x, routes[...])[2]


def fetch_copies(sources, targets, sems):
    parts = sems.shape[1]
    copies = []
    for k, ((source, row), target) in enumerate(zip(sources, targets)):
        step = target.shape[0] // parts
        for i in range(parts):
            copies.append(
                pltpu.make_async_copy(
                    source.at[pl.ds(row + i * step, step)],
                    target.at[pl.ds(i * step, step)],
                    sems.at[k, i],
                )
            )
    return copies


def fetch_kernel(count, *refs):
    sources, targets, sems = refs[:count], refs[count + 1 : -1], refs[-1]
    copies = fetch_copies([(source, 0) for source in sources], targets, sems)
    for copy in copies:
        copy.start()
    for copy in copies:
        copy.wait()


def fetch(weights, rows, after):
    anywhere = pl.BlockSpec(memory_space=pl.ANY)
    count = len(weights)
    out = pl.pallas_call(
        functools.partial(fetch_kernel, count),
        out_shape=[pltpu.VMEM((r, w.shape[1]), w.dtype) for w, r in zip(weights, rows)],
        in_specs=[anywhere] * (count + 1),
        out_specs=whole(count),
        scratch_shapes=[pltpu.SemaphoreType.DMA((count, 4))],
        compiler_params=pltpu.CompilerParams(vmem_limit_bytes=8 * MIB),
        cost_estimate=pl.CostEstimate(
            flops=0, bytes_accessed=2 * sum(w.size for w in weights), transcendentals=0
        ),
    )(*[in_hbm(w) for w in weights], after)
    return [in_vmem(w) for w in out]


def relay_kernel(block, *refs):
    refs[-1][...] = block[...]


def relay(block, *after):
    return pl.pallas_call(
        relay_kernel,
        out_shape=jax.ShapeDtypeStruct(block.shape, block.dtype),
        in_specs=whole(1) + [pl.BlockSpec(memory_space=pl.ANY)] * len(after),
        out_specs=whole(1)[0],
        compiler_params=pltpu.CompilerParams(vmem_limit_bytes=8 * MIB),
        cost_estimate=pl.CostEstimate(
            flops=0, bytes_accessed=4 * MIB, transcendentals=0
        ),
    )(block, *after)


def expert_kernel(*refs):
    pieces, (down_in, gate_w, up_w), refs = refs[:4], refs[4:7], refs[7:]
    send, keep, weighted_t, d_both, x_t, y, x, down_w, sems = refs
    rows, width, hidden_dim = x.shape[0], gate_w.shape[0], gate_w.shape[1]
    wide = width + LANES
    half = rows // 2
    copies = fetch_copies([(down_in, 0)], [down_w], sems)
    for copy in copies:
        copy.start()
    quarter = rows // 4
    for i, ref in enumerate(pieces):
        x[i * quarter : (i + 1) * quarter, :] = ref[:, :wide]
    pre_gate = dot(x[:, :width], gate_w[...], ((1,), (0,)))
    pre_up = dot(x[:, :width], up_w[...], ((1,), (0,)))
    for copy in copies:
        copy.wait()
    for i, ref in enumerate(pieces):
        y[i * quarter : (i + 1) * quarter, :] = ref[:, wide:]
    back = dot(y[...], down_w[...], ((1,), (1,)))
    g = x[:, width:][:, 0:1].astype(F32)
    sig = jax.nn.sigmoid(pre_gate)
    act = pre_gate * sig
    hidden = act * pre_up
    weighted_t[...] = (g * hidden).T.astype(BF16)
    products = jnp.sum(hidden * back, axis=1, keepdims=True)
    scaled = g * back
    d_both[:, :hidden_dim] = (
        scaled * pre_up * sig * (1.0 + pre_gate * (1.0 - sig))
    ).astype(BF16)
    d_both[:, hidden_dim:] = (scaled * act).astype(BF16)
    keep[:, width:] = lane_pair(half, products[:half], 0.0)
    send[:, width:] = split_pair(products[half:]).astype(BF16)
    wide = 1024
    for i in range(width // wide):
        at = pl.ds(i * wide, wide)
        part = dot(d_both[:, :hidden_dim], gate_w[at, :], ((1,), (1,)))
        part += dot(d_both[:, hidden_dim:], up_w[at, :], ((1,), (1,)))
        keep[:, at] = part[:half]
        send[:, at] = part[half:].astype(BF16)
        for c in range(i * wide, (i + 1) * wide, LANES):
            x_t[c : c + LANES, :] = x[:, c : c + LANES].astype(F32).T.astype(BF16)


def folded(have, gots):
    width = have.shape[1] - LANES
    total, tail = have[:, :width], have[:, width:]
    for got in gots:
        total += got[:, :width].astype(F32)
        tail += got[:, width:].astype(F32)
    return total, tail[:, 0:1] + tail[:, 1:2]


def put_keep(out, total, value):
    width = total.shape[1]
    out[:, :width] = total
    out[:, width:] = lane_pair(total.shape[0], value, 0.0)


def put_send(out, total, value):
    width = total.shape[1]
    out[:, :width] = total.astype(BF16)
    out[:, width:] = split_pair(value).astype(BF16)


def fold_kernel(have, *refs):
    keep = next(i for i, ref in enumerate(refs) if ref.dtype == F32)
    gots, keep, sends = refs[:keep], refs[keep], refs[keep + 1 :]
    rows = keep.shape[0]
    total, value = folded(have, gots)
    put_keep(keep, total[:rows], value[:rows])
    for i, send in enumerate(sends):
        part = slice((i + 1) * rows, (i + 2) * rows)
        put_send(send, total[part], value[part])


def home_kernel(have, *refs):
    gots, (select, base, coef, grad_tokens, grad_logits) = refs[:-5], refs[-5:]
    slots = have.shape[0]
    count = select.shape[0]
    total, value = folded(have, gots)
    total = total.astype(BF16)
    padded = jnp.concatenate([total, jnp.zeros((count - slots, total.shape[1]), BF16)], axis=0)
    grad_tokens[...] = dot(select[...].astype(BF16), padded, ((0,), (0,))).astype(BF16)
    token_products = jnp.sum(select[0:slots, :] * value, axis=0, keepdims=True)
    grad_logits[...] = base[...] + coef[...] * token_products


def tiles(out, left, right):
    tall = 128
    for c in range(0, right.shape[1], 256):
        for r in range(0, left.shape[0], tall):
            part = dot(left[r : r + tall], right[:, c : c + 256], ((1,), (0,)))
            out[r : r + tall, c : c + 256] = part.astype(BF16)


def loop(count, body):
    for i in range(count):
        body(i)


def late_copies(row, sources, targets, sems):
    step = sources[0].shape[0]
    return [
        pltpu.make_async_copy(source, target.at[pl.ds(row, step)], sems.at[k])
        for k, (source, target) in enumerate(zip(sources, targets))
    ]


def grads_kernel(first_row, last, x_t, d_both, *refs):
    left = refs[:2] if first_row else ()
    gate_buf, up_buf, sems = refs[-3:]
    outs = refs[-5:-3] if last else refs[-7:-5]
    kept = () if last else refs[-5:-3]
    chunks, step, cols = gate_buf.shape
    copies = late_copies(first_row - step, left, outs, sems.at[chunks]) if left else []
    for copy in copies:
        copy.start()
    for i in range(chunks if last else chunks + 1):
        at = pl.ds(first_row + i * step, step)
        for k, target in enumerate(outs):
            tile = (gate_buf, up_buf)[k].at[i] if i < chunks else kept[k]
            tiles(tile, x_t.at[at], d_both.at[:, pl.ds(k * cols, cols)])
            if i < chunks:
                copy = pltpu.make_async_copy(tile, target.at[at], sems.at[i, k])
                copy.start()
                copies.append(copy)
    for copy in copies:
        copy.wait()


def first_kernel(weighted_t, y, x_t, d_both, down_out, *refs):
    down_buf, down_sems = refs[4:6]
    chunks, _, step = down_buf.shape
    copies = []
    for i in range(chunks):
        at = pl.ds(i * step, step)
        tiles(down_buf.at[i], weighted_t, y.at[:, at])
        copies.append(pltpu.make_async_copy(down_buf.at[i], down_out.at[:, at], down_sems.at[i]))
        copies[i].start()
    grads_kernel(0, False, x_t, d_both, *refs[:4], *refs[6:])
    for copy in copies:
        copy.wait()


def grads_of(x_t, d_both, first_row, rows, before, down=()):
    width, slots = x_t.shape
    cols = d_both.shape[1] // 2
    step = 256
    last = first_row + rows == width
    chunks = rows // step - (0 if last else 1)
    anywhere = pl.BlockSpec(memory_space=pl.ANY)
    outs = [jax.ShapeDtypeStruct((width, cols), BF16)] * 2
    outs += [] if last else [jax.ShapeDtypeStruct((step, cols), BF16)] * 2
    out_specs = [anywhere] * 2 + whole(len(outs) - 2)
    scratch = [
        pltpu.VMEM((chunks, step, cols), BF16),
        pltpu.VMEM((chunks, step, cols), BF16),
        pltpu.SemaphoreType.DMA((chunks + 1, 2)),
    ]
    kernel = functools.partial(grads_kernel, first_row, last)
    if down:
        kernel = first_kernel
        wide = 1024
        outs = [jax.ShapeDtypeStruct((cols, width), BF16)] + outs
        out_specs = [anywhere] + out_specs
        scratch = [
            pltpu.VMEM((width // wide, cols, wide), BF16),
            pltpu.SemaphoreType.DMA((width // wide,)),
        ] + scratch
    elements = 2 * rows * cols + (width * cols if down else 0)
    return pl.pallas_call(
        kernel,
        out_shape=outs,
        in_specs=whole(2 + len(down)) + (whole(2) + [anywhere] * 2 if before else []),
        out_specs=out_specs,
        scratch_shapes=scratch,
        input_output_aliases={4: 0, 5: 1} if before else {},
        compiler_params=pltpu.CompilerParams(vmem_limit_bytes=20 * MIB),
        cost_estimate=pl.CostEstimate(
            flops=8 * slots * elements, bytes_accessed=2 * elements, transcendentals=0
        ),
    )(*down, x_t, d_both, *before[2:], *before[:2])


def make_shards(n):
    levels = []
    bit = n // 2
    while bit > 4:
        levels.append((bit, bit))
        bit //= 2
    levels += [(4, 2), (2, 4)]

    def swap(block, bits):
        return lax.ppermute(block, "blk", [(i, i ^ bits[i % 2]) for i in range(n)])

    def shards(
        tokens, cotangent, gate_weight, up_weight, down_weight, logits, ref_logits, routes
    ):
        count, width = tokens.shape
        slots = cotangent.shape[0]
        experts = logits.shape[1]
        hidden = down_weight.shape[0]
        rows = n * slots
        wide = width + LANES
        anywhere = pl.BlockSpec(memory_space=pl.ANY)

        small = [in_hbm(a) for a in (logits.T, ref_logits.T, routes.T)]
        send, select = pl.pallas_call(
            select_kernel,
            out_shape=[
                jax.ShapeDtypeStruct((slots, wide + width), BF16),
                jax.ShapeDtypeStruct((count, count), F32),
            ],
            in_specs=[anywhere] * 4,
            out_specs=whole(2),
            scratch_shapes=[
                pltpu.VMEM((experts, count), F32),
                pltpu.VMEM((2, count), jnp.int32),
                pltpu.VMEM((count, width), BF16),
                pltpu.VMEM((slots, width), BF16),
                pltpu.SemaphoreType.DMA((4,)),
            ],
            compiler_params=pltpu.CompilerParams(vmem_limit_bytes=8 * MIB),
            cost_estimate=pl.CostEstimate(
                flops=1 << 20, bytes_accessed=1 << 22, transcendentals=0
            ),
        )(small[0], small[2], in_hbm(tokens), in_hbm(cotangent))

        own = send
        for bits in levels[:-3]:
            own = jnp.concatenate([own, swap(own, bits)])
        first, second, third = levels[-3:]
        across = tuple(s ^ t for s, t in zip(second, third))
        block_1 = relay(relay(swap(own, first)))
        block_2 = swap(own, second)
        block_3 = swap(own, third)
        gate_w, up_w = fetch([gate_weight, up_weight], [width, width], own)
        block_1 = relay(block_1, gate_w, block_2, block_3)
        block_123 = relay(relay(swap(block_1, across)))
        block_12 = relay(swap(block_1, second))
        block_13 = swap(block_1, third)
        block_23 = swap(block_3, second)
        low_half = jnp.concatenate([own, block_1, block_2, block_12])
        high_half = jnp.concatenate([block_3, block_13, block_23, block_123])
        pieces = [low_half, high_half]
        pieces += [swap(piece, (1, 1)) for piece in pieces]

        entropy, divergence, base, coef = pl.pallas_call(
            router_kernel,
            out_shape=[
                jax.ShapeDtypeStruct((1, count), F32),
                jax.ShapeDtypeStruct((1, count), F32),
                jax.ShapeDtypeStruct((experts, count), F32),
                jax.ShapeDtypeStruct((experts, count), F32),
            ],
            in_specs=[anywhere] * 4,
            out_specs=whole(4),
            scratch_shapes=[
                pltpu.VMEM((experts, count), F32),
                pltpu.VMEM((experts, count), F32),
                pltpu.VMEM((2, count), jnp.int32),
                pltpu.SemaphoreType.DMA((3,)),
            ],
            compiler_params=pltpu.CompilerParams(vmem_limit_bytes=8 * MIB),
            cost_estimate=pl.CostEstimate(
                flops=1 << 20, bytes_accessed=1 << 22, transcendentals=0
            ),
        )(*small, high_half)

        work = 2 * rows * width * hidden
        half = rows // 2
        low, keep, weighted_t, d_both, x_t, y_all = pl.pallas_call(
            expert_kernel,
            out_shape=[
                jax.ShapeDtypeStruct((half, wide), BF16),
                jax.ShapeDtypeStruct((half, wide), F32),
                jax.ShapeDtypeStruct((hidden, rows), BF16),
                jax.ShapeDtypeStruct((rows, 2 * hidden), BF16),
                jax.ShapeDtypeStruct((width, rows), BF16),
                jax.ShapeDtypeStruct((rows, width), BF16),
            ],
            in_specs=whole(4) + [anywhere] + whole(2),
            out_specs=whole(6),
            scratch_shapes=[
                pltpu.VMEM((rows, wide), BF16),
                pltpu.VMEM((hidden, width), BF16),
                pltpu.SemaphoreType.DMA((1, 4)),
            ],
            compiler_params=pltpu.CompilerParams(vmem_limit_bytes=24 * MIB),
            cost_estimate=pl.CostEstimate(
                flops=16 * work, bytes_accessed=4 * width * hidden, transcendentals=0
            ),
        )(*pieces, in_hbm(down_weight), gate_w, up_w)

        both = tuple(f ^ s for f, s in zip(first, second))
        paths = [((1, 1),), (third,), (first, second, both)] + [(b,) for b in levels[:-3][::-1]]
        sent = [low]
        for path, following in zip(paths, paths[1:] + [()]):
            gots = [swap(block, bits) for block, bits in zip(sent, path)]
            if not following:
                break
            rows_kept = keep.shape[0] // (len(following) + 1)
            keep, *sent = call(
                fold_kernel,
                [((rows_kept, wide), F32)] + [((rows_kept, wide), BF16)] * len(following),
                [keep, *gots],
                4 * keep.shape[0] * wide,
                16 * keep.shape[0] * wide,
            )

        cuts = [0, width // 24 * 10, width]
        grad_down, *pair = grads_of(x_t, d_both, 0, cuts[1], (), (weighted_t, y_all))
        for start, stop in zip(cuts[1:], cuts[2:]):
            pair = grads_of(x_t, d_both, start, stop - start, tuple(pair))
        grad_gate, grad_up = pair

        grad_tokens, grad_logits = call(
            home_kernel,
            [((count, width), BF16), ((experts, count), F32)],
            [keep, *gots, select, base, coef],
            1 << 20,
            1 << 18,
        )
        return (
            grad_gate,
            grad_up,
            grad_down,
            grad_tokens,
            grad_logits.T,
            entropy.reshape(count),
            divergence.reshape(count),
        )

    return shards


def solution(mesh):
    in_specs = (
        P(("grp", "blk"), None),
        P(("grp", "blk"), None),
        P(None, "blk"),
        P(None, "blk"),
        P("blk", None),
        P(("grp", "blk"), None),
        P(("grp", "blk"), None),
        P(("grp", "blk"), None),
    )
    out_specs = (
        P("grp", "blk"),
        P("grp", "blk"),
        P(("grp", "blk"), None),
        P(("grp", "blk"), None),
        P(("grp", "blk"), None),
        P(("grp", "blk")),
        P(("grp", "blk")),
    )
    return jax.shard_map(
        make_shards(mesh.shape["blk"]),
        mesh=mesh,
        in_specs=in_specs,
        out_specs=out_specs,
        check_vma=False,
    )
```

```python
import functools

import jax
import jax.numpy as jnp
from jax import lax
from jax.experimental import pallas as pl
from jax.experimental.pallas import tpu as pltpu
from jax.sharding import PartitionSpec as P

F32 = jnp.float32
BF16 = jnp.bfloat16
LANES = 128
MIB = 1 << 20


def dot(left, right, dims):
    return lax.dot_general(left, right, (dims, ((), ())), preferred_element_type=F32)


def whole(count):
    return [pl.BlockSpec(memory_space=pltpu.VMEM)] * count


def call(kernel, outs, args, flops, moved, limit=8, after=()):
    def body(*refs):
        kernel(*refs[: len(args)], *refs[len(args) + len(after) :])

    return pl.pallas_call(
        body,
        out_shape=[jax.ShapeDtypeStruct(s, t) for s, t in outs],
        in_specs=whole(len(args)) + [pl.BlockSpec(memory_space=pl.ANY)] * len(after),
        out_specs=whole(len(outs)),
        compiler_params=pltpu.CompilerParams(vmem_limit_bytes=limit * MIB),
        cost_estimate=pl.CostEstimate(flops=flops, bytes_accessed=moved, transcendentals=0),
    )(*args, *after)


def in_hbm(array):
    return pltpu.with_memory_space_constraint(array, pltpu.HBM)


def in_vmem(array):
    return pltpu.with_memory_space_constraint(array, pltpu.VMEM)


def lane_pair(rows, first, second):
    lane = lax.broadcasted_iota(jnp.int32, (rows, LANES), 1)
    return jnp.where(lane == 0, first, jnp.where(lane == 1, second, 0.0))


def split_pair(value):
    high = value.astype(BF16).astype(F32)
    return lane_pair(value.shape[0], high, value - high)


def start_all(sources, targets, sems):
    copies = [
        pltpu.make_async_copy(s, t, sems.at[i]) for i, (s, t) in enumerate(zip(sources, targets))
    ]
    for copy in copies:
        copy.start()
    return copies


def gates(logits, routes):
    first, second = routes[0:1, :], routes[1:2, :]
    routed = jnp.where((first == 0) | (second == 0), 1.0, 0.0)
    expert = lax.broadcasted_iota(jnp.int32, logits.shape, 0)
    partner_hot = jnp.where(expert == first + second, 1.0, 0.0)
    partner_logit = jnp.sum(logits * partner_hot, axis=0, keepdims=True)
    gate = jnp.where(routed > 0.0, jax.nn.sigmoid(logits[0:1, :] - partner_logit), 0.0)
    window_hot = jnp.where(expert == 0, 1.0, 0.0)
    return routed, gate, (window_hot - partner_hot) * (gate * (1.0 - gate))


def select_kernel(
    logits_in, routes_in, tokens_in, y_in, send, select_out, logits, routes, tokens, y, sems
):
    copies = start_all(
        (logits_in, routes_in, tokens_in, y_in), (logits, routes, tokens, y), sems
    )
    slots, width = send.shape[0], tokens.shape[1]
    count = logits.shape[1]
    for copy in copies[:2]:
        copy.wait()
    routed, gate, _ = gates(logits[...], routes[...])
    token = lax.broadcasted_iota(jnp.int32, (1, count), 1)
    position = jnp.full((1, count), -1.0, F32)
    for t in range(count):
        position += jnp.where(token >= t, routed[:, t : t + 1], 0.0)
    slot = lax.broadcasted_iota(jnp.int32, (count, count), 0)
    hit = (slot == position.astype(jnp.int32)) & (routed > 0.0) & (slot < slots)
    select = jnp.where(hit, 1.0, 0.0)
    select_out[...] = select
    gate_low = gate.astype(BF16).astype(F32)
    g_slots = jnp.sum(select * gate_low, axis=1, keepdims=True)
    wide = width + LANES
    send[:, width:wide] = jnp.broadcast_to(g_slots[:slots], (slots, LANES)).astype(BF16)
    for copy in copies[2:]:
        copy.wait()
    x_slots = dot(select.astype(BF16), tokens[...], ((1,), (0,)))
    send[:, :width] = x_slots[:slots].astype(BF16)
    send[:, wide:] = y[...]


def router_kernel(
    logits_in,
    ref_in,
    routes_in,
    after,
    entropy,
    divergence,
    base,
    coef,
    logits,
    ref_logits,
    routes,
    sems,
):
    copies = start_all((logits_in, ref_in, routes_in), (logits, ref_logits, routes), sems)
    for copy in copies:
        copy.wait()
    x, r = logits[...], ref_logits[...]
    shifted = x - jnp.max(x, axis=0, keepdims=True)
    policy_log = shifted - jnp.log(jnp.sum(jnp.exp(shifted), axis=0, keepdims=True))
    shifted = r - jnp.max(r, axis=0, keepdims=True)
    frozen_log = shifted - jnp.log(jnp.sum(jnp.exp(shifted), axis=0, keepdims=True))
    probs = jnp.exp(policy_log)
    ratio = policy_log - frozen_log
    div = jnp.sum(probs * ratio, axis=0, keepdims=True)
    entropy[...] = -jnp.sum(probs * policy_log, axis=0, keepdims=True)
    divergence[...] = div
    base[...] = probs * (ratio - div)
    coef[...] = gates(x, routes[...])[2]


def fetch_copies(sources, targets, sems):
    parts = sems.shape[1]
    copies = []
    for k, ((source, row), target) in enumerate(zip(sources, targets)):
        step = target.shape[0] // parts
        for i in range(parts):
            copies.append(
                pltpu.make_async_copy(
                    source.at[pl.ds(row + i * step, step)],
                    target.at[pl.ds(i * step, step)],
                    sems.at[k, i],
                )
            )
    return copies


def fetch_kernel(count, *refs):
    sources, targets, sems = refs[:count], refs[count + 1 : -1], refs[-1]
    copies = fetch_copies([(source, 0) for source in sources], targets, sems)
    for copy in copies:
        copy.start()
    for copy in copies:
        copy.wait()


def fetch(weights, rows, after):
    anywhere = pl.BlockSpec(memory_space=pl.ANY)
    count = len(weights)
    out = pl.pallas_call(
        functools.partial(fetch_kernel, count),
        out_shape=[pltpu.VMEM((r, w.shape[1]), w.dtype) for w, r in zip(weights, rows)],
        in_specs=[anywhere] * (count + 1),
        out_specs=whole(count),
        scratch_shapes=[pltpu.SemaphoreType.DMA((count, 4))],
        compiler_params=pltpu.CompilerParams(vmem_limit_bytes=8 * MIB),
        cost_estimate=pl.CostEstimate(
            flops=0, bytes_accessed=2 * sum(w.size for w in weights), transcendentals=0
        ),
    )(*[in_hbm(w) for w in weights], after)
    return [in_vmem(w) for w in out]


def relay_kernel(block, *refs):
    refs[-1][...] = block[...]


def relay(block, *after):
    return pl.pallas_call(
        relay_kernel,
        out_shape=jax.ShapeDtypeStruct(block.shape, block.dtype),
        in_specs=whole(1) + [pl.BlockSpec(memory_space=pl.ANY)] * len(after),
        out_specs=whole(1)[0],
        compiler_params=pltpu.CompilerParams(vmem_limit_bytes=8 * MIB),
        cost_estimate=pl.CostEstimate(
            flops=0, bytes_accessed=4 * MIB, transcendentals=0
        ),
    )(block, *after)


def expert_kernel(*refs):
    pieces, (down_in, gate_w, up_w), refs = refs[:4], refs[4:7], refs[8:]
    send, keep, weighted_t, d_both, x_t, y, x, down_w, sems = refs
    rows, width, hidden_dim = x.shape[0], gate_w.shape[0], gate_w.shape[1]
    wide = width + LANES
    half = rows // 2
    copies = fetch_copies([(down_in, 0)], [down_w], sems)
    for copy in copies:
        copy.start()
    quarter = rows // 4
    for i, ref in enumerate(pieces):
        x[i * quarter : (i + 1) * quarter, :] = ref[:, :wide]
    pre_gate = dot(x[:, :width], gate_w[...], ((1,), (0,)))
    pre_up = dot(x[:, :width], up_w[...], ((1,), (0,)))
    for copy in copies:
        copy.wait()
    for i, ref in enumerate(pieces):
        y[i * quarter : (i + 1) * quarter, :] = ref[:, wide:]
    back = dot(y[...], down_w[...], ((1,), (1,)))
    g = x[:, width:][:, 0:1].astype(F32)
    sig = jax.nn.sigmoid(pre_gate)
    act = pre_gate * sig
    hidden = act * pre_up
    weighted_t[...] = (g * hidden).T.astype(BF16)
    products = jnp.sum(hidden * back, axis=1, keepdims=True)
    scaled = g * back
    d_both[:, :hidden_dim] = (
        scaled * pre_up * sig * (1.0 + pre_gate * (1.0 - sig))
    ).astype(BF16)
    d_both[:, hidden_dim:] = (scaled * act).astype(BF16)
    keep[:, width:] = lane_pair(half, products[:half], 0.0)
    send[:, width:] = split_pair(products[half:]).astype(BF16)
    wide = 1024
    for i in range(width // wide):
        at = pl.ds(i * wide, wide)
        part = dot(d_both[:, :hidden_dim], gate_w[at, :], ((1,), (1,)))
        part += dot(d_both[:, hidden_dim:], up_w[at, :], ((1,), (1,)))
        keep[:, at] = part[:half]
        send[:, at] = part[half:].astype(BF16)
        for c in range(i * wide, (i + 1) * wide, LANES):
            x_t[c : c + LANES, :] = x[:, c : c + LANES].astype(F32).T.astype(BF16)


def folded(have, gots):
    width = have.shape[1] - LANES
    total, tail = have[:, :width], have[:, width:]
    for got in gots:
        total += got[:, :width].astype(F32)
        tail += got[:, width:].astype(F32)
    return total, tail[:, 0:1] + tail[:, 1:2]


def put_keep(out, total, value):
    width = total.shape[1]
    out[:, :width] = total
    out[:, width:] = lane_pair(total.shape[0], value, 0.0)


def put_send(out, total, value):
    width = total.shape[1]
    out[:, :width] = total.astype(BF16)
    out[:, width:] = split_pair(value).astype(BF16)


def fold_kernel(have, *refs):
    keep = next(i for i, ref in enumerate(refs) if ref.dtype == F32)
    gots, keep, sends = refs[:keep], refs[keep], refs[keep + 1 :]
    rows = keep.shape[0]
    total, value = folded(have, gots)
    put_keep(keep, total[:rows], value[:rows])
    for i, send in enumerate(sends):
        part = slice((i + 1) * rows, (i + 2) * rows)
        put_send(send, total[part], value[part])


def home_kernel(have, *refs):
    gots, (select, base, coef, grad_tokens, grad_logits) = refs[:-5], refs[-5:]
    slots = have.shape[0]
    count = select.shape[0]
    total, value = folded(have, gots)
    total = total.astype(BF16)
    padded = jnp.concatenate([total, jnp.zeros((count - slots, total.shape[1]), BF16)], axis=0)
    grad_tokens[...] = dot(select[...].astype(BF16), padded, ((0,), (0,))).astype(BF16)
    token_products = jnp.sum(select[0:slots, :] * value, axis=0, keepdims=True)
    grad_logits[...] = base[...] + coef[...] * token_products


def tiles(out, left, right):
    tall = 128
    for c in range(0, right.shape[1], 256):
        for r in range(0, left.shape[0], tall):
            part = dot(left[r : r + tall], right[:, c : c + 256], ((1,), (0,)))
            out[r : r + tall, c : c + 256] = part.astype(BF16)


def loop(count, body):
    for i in range(count):
        body(i)


def late_copies(row, sources, targets, sems):
    step = sources[0].shape[0]
    return [
        pltpu.make_async_copy(source, target.at[pl.ds(row, step)], sems.at[k])
        for k, (source, target) in enumerate(zip(sources, targets))
    ]


def grads_kernel(first_row, last, x_t, d_both, *refs):
    left = refs[:2] if first_row else ()
    gate_buf, up_buf, sems = refs[-3:]
    outs = refs[-5:-3] if last else refs[-7:-5]
    kept = () if last else refs[-5:-3]
    chunks, step, cols = gate_buf.shape
    copies = late_copies(first_row - step, left, outs, sems.at[chunks]) if left else []
    for copy in copies:
        copy.start()
    for i in range(chunks if last else chunks + 1):
        at = pl.ds(first_row + i * step, step)
        for k, target in enumerate(outs):
            tile = (gate_buf, up_buf)[k].at[i] if i < chunks else kept[k]
            tiles(tile, x_t.at[at], d_both.at[:, pl.ds(k * cols, cols)])
            if i < chunks:
                copy = pltpu.make_async_copy(tile, target.at[at], sems.at[i, k])
                copy.start()
                copies.append(copy)
    for copy in copies:
        copy.wait()


def first_kernel(first_row, weighted_t, y, x_t, d_both, *refs):
    left, down_out, refs = refs[:4], refs[4], refs[5:]
    down_buf, down_sems = refs[4:6]
    chunks, _, step = down_buf.shape
    copies = []
    for i in range(chunks):
        at = pl.ds(i * step, step)
        tiles(down_buf.at[i], weighted_t, y.at[:, at])
        copies.append(pltpu.make_async_copy(down_buf.at[i], down_out.at[:, at], down_sems.at[i]))
        copies[i].start()
    grads_kernel(first_row, False, x_t, d_both, *left, *refs[:4], *refs[6:])
    for copy in copies:
        copy.wait()


def grads_of(x_t, d_both, first_row, rows, before, down=()):
    width, slots = x_t.shape
    cols = d_both.shape[1] // 2
    step = 256
    last = first_row + rows == width
    chunks = rows // step - (0 if last else 1)
    anywhere = pl.BlockSpec(memory_space=pl.ANY)
    outs = [jax.ShapeDtypeStruct((width, cols), BF16)] * 2
    outs += [] if last else [jax.ShapeDtypeStruct((step, cols), BF16)] * 2
    out_specs = [anywhere] * 2 + whole(len(outs) - 2)
    scratch = [
        pltpu.VMEM((chunks, step, cols), BF16),
        pltpu.VMEM((chunks, step, cols), BF16),
        pltpu.SemaphoreType.DMA((chunks + 1, 2)),
    ]
    kernel = functools.partial(grads_kernel, first_row, last)
    if down:
        kernel = functools.partial(first_kernel, first_row)
        wide = 1024
        outs = [jax.ShapeDtypeStruct((cols, width), BF16)] + outs
        out_specs = [anywhere] + out_specs
        scratch = [
            pltpu.VMEM((width // wide, cols, wide), BF16),
            pltpu.SemaphoreType.DMA((width // wide,)),
        ] + scratch
    elements = 2 * rows * cols + (width * cols if down else 0)
    return pl.pallas_call(
        kernel,
        out_shape=outs,
        in_specs=whole(2 + len(down)) + (whole(2) + [anywhere] * 2 if before else []),
        out_specs=out_specs,
        scratch_shapes=scratch,
        input_output_aliases=({6: 1, 7: 2} if down else {4: 0, 5: 1}) if before else {},
        compiler_params=pltpu.CompilerParams(vmem_limit_bytes=20 * MIB),
        cost_estimate=pl.CostEstimate(
            flops=8 * slots * elements, bytes_accessed=2 * elements, transcendentals=0
        ),
    )(*down, x_t, d_both, *before[2:], *before[:2])


def make_shards(n):
    levels = []
    bit = n // 2
    while bit > 4:
        levels.append((bit, bit))
        bit //= 2
    levels += [(4, 2), (2, 4)]

    def swap(block, bits):
        return lax.ppermute(block, "blk", [(i, i ^ bits[i % 2]) for i in range(n)])

    def shards(
        tokens, cotangent, gate_weight, up_weight, down_weight, logits, ref_logits, routes
    ):
        count, width = tokens.shape
        slots = cotangent.shape[0]
        experts = logits.shape[1]
        hidden = down_weight.shape[0]
        rows = n * slots
        wide = width + LANES
        anywhere = pl.BlockSpec(memory_space=pl.ANY)

        small = [in_hbm(a) for a in (logits.T, ref_logits.T, routes.T)]
        send, select = pl.pallas_call(
            select_kernel,
            out_shape=[
                jax.ShapeDtypeStruct((slots, wide + width), BF16),
                jax.ShapeDtypeStruct((count, count), F32),
            ],
            in_specs=[anywhere] * 4,
            out_specs=whole(2),
            scratch_shapes=[
                pltpu.VMEM((experts, count), F32),
                pltpu.VMEM((2, count), jnp.int32),
                pltpu.VMEM((count, width), BF16),
                pltpu.VMEM((slots, width), BF16),
                pltpu.SemaphoreType.DMA((4,)),
            ],
            compiler_params=pltpu.CompilerParams(vmem_limit_bytes=8 * MIB),
            cost_estimate=pl.CostEstimate(
                flops=1 << 20, bytes_accessed=1 << 22, transcendentals=0
            ),
        )(small[0], small[2], in_hbm(tokens), in_hbm(cotangent))

        own = send
        for bits in levels[:-3]:
            own = jnp.concatenate([own, swap(own, bits)])
        first, second, third = levels[-3:]
        across = tuple(s ^ t for s, t in zip(second, third))
        block_1 = relay(relay(swap(own, first)))
        block_2 = swap(own, second)
        block_3 = swap(own, third)
        gate_w, up_w = fetch([gate_weight, up_weight], [width, width], own)
        block_1 = relay(block_1, gate_w, block_2, block_3)
        block_123 = relay(relay(swap(block_1, across)))
        block_12 = relay(swap(block_1, second))
        block_13 = swap(block_1, third)
        block_23 = swap(block_3, second)
        low_half = jnp.concatenate([own, block_1, block_2, block_12])
        high_half = jnp.concatenate([block_3, block_13, block_23, block_123])
        pieces = [low_half, high_half]
        pieces += [swap(piece, (1, 1)) for piece in pieces]

        entropy, divergence, base, coef = pl.pallas_call(
            router_kernel,
            out_shape=[
                jax.ShapeDtypeStruct((1, count), F32),
                jax.ShapeDtypeStruct((1, count), F32),
                jax.ShapeDtypeStruct((experts, count), F32),
                jax.ShapeDtypeStruct((experts, count), F32),
            ],
            in_specs=[anywhere] * 4,
            out_specs=whole(4),
            scratch_shapes=[
                pltpu.VMEM((experts, count), F32),
                pltpu.VMEM((experts, count), F32),
                pltpu.VMEM((2, count), jnp.int32),
                pltpu.SemaphoreType.DMA((3,)),
            ],
            compiler_params=pltpu.CompilerParams(vmem_limit_bytes=8 * MIB),
            cost_estimate=pl.CostEstimate(
                flops=1 << 20, bytes_accessed=1 << 22, transcendentals=0
            ),
        )(*small, high_half)

        work = 2 * rows * width * hidden
        half = rows // 2
        low, keep, weighted_t, d_both, x_t, y_all = pl.pallas_call(
            expert_kernel,
            out_shape=[
                jax.ShapeDtypeStruct((half, wide), BF16),
                jax.ShapeDtypeStruct((half, wide), F32),
                jax.ShapeDtypeStruct((hidden, rows), BF16),
                jax.ShapeDtypeStruct((rows, 2 * hidden), BF16),
                jax.ShapeDtypeStruct((width, rows), BF16),
                jax.ShapeDtypeStruct((rows, width), BF16),
            ],
            in_specs=whole(4) + [anywhere] + whole(2) + [anywhere],
            out_specs=whole(6),
            scratch_shapes=[
                pltpu.VMEM((rows, wide), BF16),
                pltpu.VMEM((hidden, width), BF16),
                pltpu.SemaphoreType.DMA((1, 4)),
            ],
            compiler_params=pltpu.CompilerParams(vmem_limit_bytes=24 * MIB),
            cost_estimate=pl.CostEstimate(
                flops=16 * work, bytes_accessed=4 * width * hidden, transcendentals=0
            ),
        )(*pieces, in_hbm(down_weight), gate_w, up_w, base)

        unit = width // 24
        cuts = [0, 3 * unit, 12 * unit, width]
        pair = first_pair = grads_of(x_t, d_both, 0, cuts[1], ())
        grad_down, *pair = grads_of(
            x_t, d_both, cuts[1], cuts[2] - cuts[1], tuple(pair), (weighted_t, y_all)
        )
        grad_gate, grad_up = grads_of(x_t, d_both, cuts[2], cuts[3] - cuts[2], tuple(pair))

        both = tuple(f ^ s for f, s in zip(first, second))
        paths = [((1, 1),), (third,), (first, second, both)] + [(b,) for b in levels[:-3][::-1]]
        sent = [low]
        for path, following in zip(paths, paths[1:] + [()]):
            gots = [swap(block, bits) for block, bits in zip(sent, path)]
            if not following:
                break
            rows_kept = keep.shape[0] // (len(following) + 1)
            keep, *sent = call(
                fold_kernel,
                [((rows_kept, wide), F32)] + [((rows_kept, wide), BF16)] * len(following),
                [keep, *gots],
                4 * keep.shape[0] * wide,
                16 * keep.shape[0] * wide,
                after=[first_pair[2]] if path == paths[0] else [],
            )


        grad_tokens, grad_logits = call(
            home_kernel,
            [((count, width), BF16), ((experts, count), F32)],
            [keep, *gots, select, base, coef],
            1 << 20,
            1 << 18,
        )
        return (
            grad_gate,
            grad_up,
            grad_down,
            grad_tokens,
            grad_logits.T,
            entropy.reshape(count),
            divergence.reshape(count),
        )

    return shards


def solution(mesh):
    in_specs = (
        P(("grp", "blk"), None),
        P(("grp", "blk"), None),
        P(None, "blk"),
        P(None, "blk"),
        P("blk", None),
        P(("grp", "blk"), None),
        P(("grp", "blk"), None),
        P(("grp", "blk"), None),
    )
    out_specs = (
        P("grp", "blk"),
        P("grp", "blk"),
        P(("grp", "blk"), None),
        P(("grp", "blk"), None),
        P(("grp", "blk"), None),
        P(("grp", "blk")),
        P(("grp", "blk")),
    )
    return jax.shard_map(
        make_shards(mesh.shape["blk"]),
        mesh=mesh,
        in_specs=in_specs,
        out_specs=out_specs,
        check_vma=False,
    )
```

```python
import functools

import jax
import jax.numpy as jnp
from jax import lax
from jax.experimental import pallas as pl
from jax.experimental.pallas import tpu as pltpu
from jax.sharding import PartitionSpec as P

F32 = jnp.float32
BF16 = jnp.bfloat16
LANES = 128
MIB = 1 << 20


def dot(left, right, dims):
    return lax.dot_general(left, right, (dims, ((), ())), preferred_element_type=F32)


def whole(count):
    return [pl.BlockSpec(memory_space=pltpu.VMEM)] * count


def call(kernel, outs, args, flops, moved, limit=8, after=()):
    def body(*refs):
        kernel(*refs[: len(args)], *refs[len(args) + len(after) :])

    return pl.pallas_call(
        body,
        out_shape=[jax.ShapeDtypeStruct(s, t) for s, t in outs],
        in_specs=whole(len(args)) + [pl.BlockSpec(memory_space=pl.ANY)] * len(after),
        out_specs=whole(len(outs)),
        compiler_params=pltpu.CompilerParams(vmem_limit_bytes=limit * MIB),
        cost_estimate=pl.CostEstimate(flops=flops, bytes_accessed=moved, transcendentals=0),
    )(*args, *after)


def in_hbm(array):
    return pltpu.with_memory_space_constraint(array, pltpu.HBM)


def in_vmem(array):
    return pltpu.with_memory_space_constraint(array, pltpu.VMEM)


def lane_pair(rows, first, second):
    lane = lax.broadcasted_iota(jnp.int32, (rows, LANES), 1)
    return jnp.where(lane == 0, first, jnp.where(lane == 1, second, 0.0))


def split_pair(value):
    high = value.astype(BF16).astype(F32)
    return lane_pair(value.shape[0], high, value - high)


def start_all(sources, targets, sems):
    copies = [
        pltpu.make_async_copy(s, t, sems.at[i]) for i, (s, t) in enumerate(zip(sources, targets))
    ]
    for copy in copies:
        copy.start()
    return copies


def gates(logits, routes):
    first, second = routes[0:1, :], routes[1:2, :]
    routed = jnp.where((first == 0) | (second == 0), 1.0, 0.0)
    expert = lax.broadcasted_iota(jnp.int32, logits.shape, 0)
    partner_hot = jnp.where(expert == first + second, 1.0, 0.0)
    partner_logit = jnp.sum(logits * partner_hot, axis=0, keepdims=True)
    gate = jnp.where(routed > 0.0, jax.nn.sigmoid(logits[0:1, :] - partner_logit), 0.0)
    window_hot = jnp.where(expert == 0, 1.0, 0.0)
    return routed, gate, (window_hot - partner_hot) * (gate * (1.0 - gate))


def select_kernel(
    logits_in, routes_in, tokens_in, y_in, send, select_out, logits, routes, tokens, y, sems
):
    copies = start_all(
        (logits_in, routes_in, tokens_in, y_in), (logits, routes, tokens, y), sems
    )
    slots, width = send.shape[0], tokens.shape[1]
    count = logits.shape[1]
    for copy in copies[:2]:
        copy.wait()
    routed, gate, _ = gates(logits[...], routes[...])
    token = lax.broadcasted_iota(jnp.int32, (1, count), 1)
    position = jnp.full((1, count), -1.0, F32)
    for t in range(count):
        position += jnp.where(token >= t, routed[:, t : t + 1], 0.0)
    slot = lax.broadcasted_iota(jnp.int32, (count, count), 0)
    hit = (slot == position.astype(jnp.int32)) & (routed > 0.0) & (slot < slots)
    select = jnp.where(hit, 1.0, 0.0)
    select_out[...] = select
    gate_low = gate.astype(BF16).astype(F32)
    g_slots = jnp.sum(select * gate_low, axis=1, keepdims=True)
    wide = width + LANES
    send[:, width:wide] = jnp.broadcast_to(g_slots[:slots], (slots, LANES)).astype(BF16)
    for copy in copies[2:]:
        copy.wait()
    x_slots = dot(select.astype(BF16), tokens[...], ((1,), (0,)))
    send[:, :width] = x_slots[:slots].astype(BF16)
    send[:, wide:] = y[...]


def router_kernel(
    logits_in,
    ref_in,
    routes_in,
    after,
    entropy,
    divergence,
    base,
    coef,
    logits,
    ref_logits,
    routes,
    sems,
):
    copies = start_all((logits_in, ref_in, routes_in), (logits, ref_logits, routes), sems)
    for copy in copies:
        copy.wait()
    x, r = logits[...], ref_logits[...]
    shifted = x - jnp.max(x, axis=0, keepdims=True)
    policy_log = shifted - jnp.log(jnp.sum(jnp.exp(shifted), axis=0, keepdims=True))
    shifted = r - jnp.max(r, axis=0, keepdims=True)
    frozen_log = shifted - jnp.log(jnp.sum(jnp.exp(shifted), axis=0, keepdims=True))
    probs = jnp.exp(policy_log)
    ratio = policy_log - frozen_log
    div = jnp.sum(probs * ratio, axis=0, keepdims=True)
    entropy[...] = -jnp.sum(probs * policy_log, axis=0, keepdims=True)
    divergence[...] = div
    base[...] = probs * (ratio - div)
    coef[...] = gates(x, routes[...])[2]


def fetch_copies(sources, targets, sems):
    parts = sems.shape[1]
    copies = []
    for k, ((source, row), target) in enumerate(zip(sources, targets)):
        step = target.shape[0] // parts
        for i in range(parts):
            copies.append(
                pltpu.make_async_copy(
                    source.at[pl.ds(row + i * step, step)],
                    target.at[pl.ds(i * step, step)],
                    sems.at[k, i],
                )
            )
    return copies


def fetch_kernel(count, *refs):
    sources, targets, sems = refs[:count], refs[count + 1 : -1], refs[-1]
    copies = fetch_copies([(source, 0) for source in sources], targets, sems)
    for copy in copies:
        copy.start()
    for copy in copies:
        copy.wait()


def fetch(weights, rows, after):
    anywhere = pl.BlockSpec(memory_space=pl.ANY)
    count = len(weights)
    out = pl.pallas_call(
        functools.partial(fetch_kernel, count),
        out_shape=[pltpu.VMEM((r, w.shape[1]), w.dtype) for w, r in zip(weights, rows)],
        in_specs=[anywhere] * (count + 1),
        out_specs=whole(count),
        scratch_shapes=[pltpu.SemaphoreType.DMA((count, 4))],
        compiler_params=pltpu.CompilerParams(vmem_limit_bytes=8 * MIB),
        cost_estimate=pl.CostEstimate(
            flops=0, bytes_accessed=2 * sum(w.size for w in weights), transcendentals=0
        ),
    )(*[in_hbm(w) for w in weights], after)
    return [in_vmem(w) for w in out]


def relay_kernel(block, *refs):
    refs[-1][...] = block[...]


def relay(block, *after):
    return pl.pallas_call(
        relay_kernel,
        out_shape=jax.ShapeDtypeStruct(block.shape, block.dtype),
        in_specs=whole(1) + [pl.BlockSpec(memory_space=pl.ANY)] * len(after),
        out_specs=whole(1)[0],
        compiler_params=pltpu.CompilerParams(vmem_limit_bytes=8 * MIB),
        cost_estimate=pl.CostEstimate(
            flops=0, bytes_accessed=4 * MIB, transcendentals=0
        ),
    )(block, *after)


def expert_kernel(*refs):
    pieces, (down_in, gate_w, up_w), refs = refs[:4], refs[4:7], refs[8:]
    send, keep, weighted_t, d_both, x_t, y, x, down_w, sems = refs
    rows, width, hidden_dim = x.shape[0], gate_w.shape[0], gate_w.shape[1]
    wide = width + LANES
    half = rows // 2
    copies = fetch_copies([(down_in, 0)], [down_w], sems)
    for copy in copies:
        copy.start()
    quarter = rows // 4
    for i, ref in enumerate(pieces):
        x[i * quarter : (i + 1) * quarter, :] = ref[:, :wide]
    pre_gate = dot(x[:, :width], gate_w[...], ((1,), (0,)))
    pre_up = dot(x[:, :width], up_w[...], ((1,), (0,)))
    for copy in copies:
        copy.wait()
    for i, ref in enumerate(pieces):
        y[i * quarter : (i + 1) * quarter, :] = ref[:, wide:]
    back = dot(y[...], down_w[...], ((1,), (1,)))
    g = x[:, width:][:, 0:1].astype(F32)
    sig = jax.nn.sigmoid(pre_gate)
    act = pre_gate * sig
    hidden = act * pre_up
    weighted_t[...] = (g * hidden).T.astype(BF16)
    products = jnp.sum(hidden * back, axis=1, keepdims=True)
    scaled = g * back
    d_both[:, :hidden_dim] = (
        scaled * pre_up * sig * (1.0 + pre_gate * (1.0 - sig))
    ).astype(BF16)
    d_both[:, hidden_dim:] = (scaled * act).astype(BF16)
    keep[:, width:] = lane_pair(half, products[:half], 0.0)
    send[:, width:] = split_pair(products[half:]).astype(BF16)
    wide = 1024
    for i in range(width // wide):
        at = pl.ds(i * wide, wide)
        part = dot(d_both[:, :hidden_dim], gate_w[at, :], ((1,), (1,)))
        part += dot(d_both[:, hidden_dim:], up_w[at, :], ((1,), (1,)))
        keep[:, at] = part[:half]
        send[:, at] = part[half:].astype(BF16)
        for c in range(i * wide, (i + 1) * wide, LANES):
            x_t[c : c + LANES, :] = x[:, c : c + LANES].astype(F32).T.astype(BF16)


def folded(have, gots):
    width = have.shape[1] - LANES
    total, tail = have[:, :width], have[:, width:]
    for got in gots:
        total += got[:, :width].astype(F32)
        tail += got[:, width:].astype(F32)
    return total, tail[:, 0:1] + tail[:, 1:2]


def put_keep(out, total, value):
    width = total.shape[1]
    out[:, :width] = total
    out[:, width:] = lane_pair(total.shape[0], value, 0.0)


def put_send(out, total, value):
    width = total.shape[1]
    out[:, :width] = total.astype(BF16)
    out[:, width:] = split_pair(value).astype(BF16)


def fold_kernel(have, *refs):
    keep = next(i for i, ref in enumerate(refs) if ref.dtype == F32)
    gots, keep, sends = refs[:keep], refs[keep], refs[keep + 1 :]
    rows = keep.shape[0]
    total, value = folded(have, gots)
    put_keep(keep, total[:rows], value[:rows])
    for i, send in enumerate(sends):
        part = slice((i + 1) * rows, (i + 2) * rows)
        put_send(send, total[part], value[part])


def home_kernel(have, *refs):
    gots, (select, base, coef, grad_tokens, grad_logits) = refs[:-5], refs[-5:]
    slots = have.shape[0]
    count = select.shape[0]
    total, value = folded(have, gots)
    total = total.astype(BF16)
    padded = jnp.concatenate([total, jnp.zeros((count - slots, total.shape[1]), BF16)], axis=0)
    grad_tokens[...] = dot(select[...].astype(BF16), padded, ((0,), (0,))).astype(BF16)
    token_products = jnp.sum(select[0:slots, :] * value, axis=0, keepdims=True)
    grad_logits[...] = base[...] + coef[...] * token_products


def tiles(out, left, right):
    tall = 128
    for c in range(0, right.shape[1], 256):
        for r in range(0, left.shape[0], tall):
            part = dot(left[r : r + tall], right[:, c : c + 256], ((1,), (0,)))
            out[r : r + tall, c : c + 256] = part.astype(BF16)


def loop(count, body):
    for i in range(count):
        body(i)


def late_copies(row, sources, targets, sems):
    step = sources[0].shape[0]
    return [
        pltpu.make_async_copy(source, target.at[pl.ds(row, step)], sems.at[k])
        for k, (source, target) in enumerate(zip(sources, targets))
    ]


def grads_kernel(first_row, last, x_t, d_both, *refs):
    left = refs[:2] if first_row else ()
    gate_buf, up_buf, sems = refs[-3:]
    outs = refs[-5:-3] if last else refs[-7:-5]
    kept = () if last else refs[-5:-3]
    chunks, step, cols = gate_buf.shape
    copies = late_copies(first_row - step, left, outs, sems.at[chunks]) if left else []
    for copy in copies:
        copy.start()
    for i in range(chunks if last else chunks + 1):
        at = pl.ds(first_row + i * step, step)
        for k, target in enumerate(outs):
            tile = (gate_buf, up_buf)[k].at[i] if i < chunks else kept[k]
            tiles(tile, x_t.at[at], d_both.at[:, pl.ds(k * cols, cols)])
            if i < chunks:
                copy = pltpu.make_async_copy(tile, target.at[at], sems.at[i, k])
                copy.start()
                copies.append(copy)
    for copy in copies:
        copy.wait()


def first_kernel(first_row, weighted_t, y, x_t, d_both, *refs):
    left, down_out, refs = refs[:4], refs[4], refs[5:]
    down_buf, down_sems = refs[4:6]
    chunks, _, step = down_buf.shape
    copies = []
    for i in range(chunks):
        at = pl.ds(i * step, step)
        tiles(down_buf.at[i], weighted_t, y.at[:, at])
        copies.append(pltpu.make_async_copy(down_buf.at[i], down_out.at[:, at], down_sems.at[i]))
        copies[i].start()
    grads_kernel(first_row, False, x_t, d_both, *left, *refs[:4], *refs[6:])
    for copy in copies:
        copy.wait()


def grads_of(x_t, d_both, first_row, rows, before, down=()):
    width, slots = x_t.shape
    cols = d_both.shape[1] // 2
    step = 256
    last = first_row + rows == width
    chunks = rows // step - (0 if last else 1)
    anywhere = pl.BlockSpec(memory_space=pl.ANY)
    outs = [jax.ShapeDtypeStruct((width, cols), BF16)] * 2
    outs += [] if last else [jax.ShapeDtypeStruct((step, cols), BF16)] * 2
    out_specs = [anywhere] * 2 + whole(len(outs) - 2)
    scratch = [
        pltpu.VMEM((chunks, step, cols), BF16),
        pltpu.VMEM((chunks, step, cols), BF16),
        pltpu.SemaphoreType.DMA((chunks + 1, 2)),
    ]
    kernel = functools.partial(grads_kernel, first_row, last)
    if down:
        kernel = functools.partial(first_kernel, first_row)
        wide = 1024
        outs = [jax.ShapeDtypeStruct((cols, width), BF16)] + outs
        out_specs = [anywhere] + out_specs
        scratch = [
            pltpu.VMEM((width // wide, cols, wide), BF16),
            pltpu.SemaphoreType.DMA((width // wide,)),
        ] + scratch
    elements = 2 * rows * cols + (width * cols if down else 0)
    return pl.pallas_call(
        kernel,
        out_shape=outs,
        in_specs=whole(2 + len(down)) + (whole(2) + [anywhere] * 2 if before else []),
        out_specs=out_specs,
        scratch_shapes=scratch,
        input_output_aliases=({6: 1, 7: 2} if down else {4: 0, 5: 1}) if before else {},
        compiler_params=pltpu.CompilerParams(vmem_limit_bytes=20 * MIB),
        cost_estimate=pl.CostEstimate(
            flops=8 * slots * elements, bytes_accessed=2 * elements, transcendentals=0
        ),
    )(*down, x_t, d_both, *before[2:], *before[:2])


def make_shards(n):
    levels = []
    bit = n // 2
    while bit > 4:
        levels.append((bit, bit))
        bit //= 2
    levels += [(4, 2), (2, 4)]

    def swap(block, bits):
        return lax.ppermute(block, "blk", [(i, i ^ bits[i % 2]) for i in range(n)])

    def shards(
        tokens, cotangent, gate_weight, up_weight, down_weight, logits, ref_logits, routes
    ):
        count, width = tokens.shape
        slots = cotangent.shape[0]
        experts = logits.shape[1]
        hidden = down_weight.shape[0]
        rows = n * slots
        wide = width + LANES
        anywhere = pl.BlockSpec(memory_space=pl.ANY)

        small = [in_hbm(a) for a in (logits.T, ref_logits.T, routes.T)]
        send, select = pl.pallas_call(
            select_kernel,
            out_shape=[
                jax.ShapeDtypeStruct((slots, wide + width), BF16),
                jax.ShapeDtypeStruct((count, count), F32),
            ],
            in_specs=[anywhere] * 4,
            out_specs=whole(2),
            scratch_shapes=[
                pltpu.VMEM((experts, count), F32),
                pltpu.VMEM((2, count), jnp.int32),
                pltpu.VMEM((count, width), BF16),
                pltpu.VMEM((slots, width), BF16),
                pltpu.SemaphoreType.DMA((4,)),
            ],
            compiler_params=pltpu.CompilerParams(vmem_limit_bytes=8 * MIB),
            cost_estimate=pl.CostEstimate(
                flops=1 << 20, bytes_accessed=1 << 22, transcendentals=0
            ),
        )(small[0], small[2], in_hbm(tokens), in_hbm(cotangent))

        own = send
        for bits in levels[:-3]:
            own = jnp.concatenate([own, swap(own, bits)])
        first, second, third = levels[-3:]
        across = tuple(s ^ t for s, t in zip(second, third))
        block_1 = relay(relay(swap(own, first)))
        block_2 = swap(own, second)
        block_3 = swap(own, third)
        gate_w, up_w = fetch([gate_weight, up_weight], [width, width], own)
        block_1 = relay(block_1, gate_w, block_2, block_3)
        block_123 = relay(relay(swap(block_1, across)))
        block_12 = relay(swap(block_1, second))
        block_13 = swap(block_1, third)
        block_23 = swap(block_3, second)
        low_half = jnp.concatenate([own, block_1, block_2, block_12])
        high_half = jnp.concatenate([block_3, block_13, block_23, block_123])
        pieces = [low_half, high_half]
        pieces += [swap(piece, (1, 1)) for piece in pieces]

        entropy, divergence, base, coef = pl.pallas_call(
            router_kernel,
            out_shape=[
                jax.ShapeDtypeStruct((1, count), F32),
                jax.ShapeDtypeStruct((1, count), F32),
                jax.ShapeDtypeStruct((experts, count), F32),
                jax.ShapeDtypeStruct((experts, count), F32),
            ],
            in_specs=[anywhere] * 4,
            out_specs=whole(4),
            scratch_shapes=[
                pltpu.VMEM((experts, count), F32),
                pltpu.VMEM((experts, count), F32),
                pltpu.VMEM((2, count), jnp.int32),
                pltpu.SemaphoreType.DMA((3,)),
            ],
            compiler_params=pltpu.CompilerParams(vmem_limit_bytes=8 * MIB),
            cost_estimate=pl.CostEstimate(
                flops=1 << 20, bytes_accessed=1 << 22, transcendentals=0
            ),
        )(*small, high_half)

        work = 2 * rows * width * hidden
        half = rows // 2
        low, keep, weighted_t, d_both, x_t, y_all = pl.pallas_call(
            expert_kernel,
            out_shape=[
                jax.ShapeDtypeStruct((half, wide), BF16),
                jax.ShapeDtypeStruct((half, wide), F32),
                jax.ShapeDtypeStruct((hidden, rows), BF16),
                jax.ShapeDtypeStruct((rows, 2 * hidden), BF16),
                jax.ShapeDtypeStruct((width, rows), BF16),
                jax.ShapeDtypeStruct((rows, width), BF16),
            ],
            in_specs=whole(4) + [anywhere] + whole(2) + [anywhere],
            out_specs=whole(6),
            scratch_shapes=[
                pltpu.VMEM((rows, wide), BF16),
                pltpu.VMEM((hidden, width), BF16),
                pltpu.SemaphoreType.DMA((1, 4)),
            ],
            compiler_params=pltpu.CompilerParams(vmem_limit_bytes=24 * MIB),
            cost_estimate=pl.CostEstimate(
                flops=16 * work, bytes_accessed=4 * width * hidden, transcendentals=0
            ),
        )(*pieces, in_hbm(down_weight), gate_w, up_w, base)

        unit = width // 24
        cuts = [0, 3 * unit, 12 * unit, width]
        pair = first_pair = grads_of(x_t, d_both, 0, cuts[1], ())
        grad_down, *pair = grads_of(
            x_t, d_both, cuts[1], cuts[2] - cuts[1], tuple(pair), (weighted_t, y_all)
        )
        grad_gate, grad_up = grads_of(x_t, d_both, cuts[2], cuts[3] - cuts[2], tuple(pair))

        both = tuple(f ^ s for f, s in zip(first, second))
        paths = [((1, 1),), (third,), (both, first, second)] + [(b,) for b in levels[:-3][::-1]]
        sent = [low]
        for path, following in zip(paths, paths[1:] + [()]):
            gots = [swap(block, bits) for block, bits in zip(sent, path)]
            if not following:
                break
            rows_kept = keep.shape[0] // (len(following) + 1)
            keep, *sent = call(
                fold_kernel,
                [((rows_kept, wide), F32)] + [((rows_kept, wide), BF16)] * len(following),
                [keep, *gots],
                4 * keep.shape[0] * wide,
                16 * keep.shape[0] * wide,
                after=[first_pair[2]] if path == paths[0] else [],
            )
            if len(sent) == 3:
                sent = [sent[2], sent[0], sent[1]]


        grad_tokens, grad_logits = call(
            home_kernel,
            [((count, width), BF16), ((experts, count), F32)],
            [keep, *gots, select, base, coef],
            1 << 20,
            1 << 18,
        )
        return (
            grad_gate,
            grad_up,
            grad_down,
            grad_tokens,
            grad_logits.T,
            entropy.reshape(count),
            divergence.reshape(count),
        )

    return shards


def solution(mesh):
    in_specs = (
        P(("grp", "blk"), None),
        P(("grp", "blk"), None),
        P(None, "blk"),
        P(None, "blk"),
        P("blk", None),
        P(("grp", "blk"), None),
        P(("grp", "blk"), None),
        P(("grp", "blk"), None),
    )
    out_specs = (
        P("grp", "blk"),
        P("grp", "blk"),
        P(("grp", "blk"), None),
        P(("grp", "blk"), None),
        P(("grp", "blk"), None),
        P(("grp", "blk")),
        P(("grp", "blk")),
    )
    return jax.shard_map(
        make_shards(mesh.shape["blk"]),
        mesh=mesh,
        in_specs=in_specs,
        out_specs=out_specs,
        check_vma=False,
    )
```
